32 devices in a mesh: groups: 2 (over y), ctx: 4 (over z), head: 2 (over x), sub: 2 (over core).
Axes of the slice: x: 2, y: 2, z: 4, core: 2. Of those that a mesh axis runs over, the one named last changes fastest.
Arguments:
- key_cache: bfloat16 [8, 8192, 8, 128], P('groups', ('ctx', 'sub'), 'head'), parts along dimension 0, may hold values from -70 to 70
- value_cache: bfloat16 [8, 8192, 8, 128], P('groups', ('ctx', 'sub'), 'head'), parts along dimension 0, may hold values from -6 to 6
- lengths: int32 [8], P('groups'), parts along dimension 0, may hold values from 1 to 8192, 16384 in all
- owner_order: int32 [8], P('groups'), parts along dimension 0, may hold values from 0 to 3, each once
- first_tokens: bfloat16 [8, 8192], P(('groups', 'head', 'sub'), 'ctx'), parts along dimension 0, may hold values from -250 to 250
- second_tokens: bfloat16 [8, 8192], P(('groups', 'head', 'sub'), 'ctx'), parts along dimension 0, may hold values from -250 to 250
- norm_gain: bfloat16 [8192], P('ctx'), may hold values from 0.099609375 to 1.8984375
- w_query: bfloat16 [8192, 8192], P('ctx', ('head', 'sub')), may hold values from -1 to 1
- w_key: bfloat16 [8192, 1024], P('ctx', ('head', 'sub')), may hold values from -16 to 16
- w_value: bfloat16 [8192, 1024], P('ctx', ('head', 'sub')), may hold values from -0.0625 to 0.0625
- w_out: bfloat16 [8192, 8192], P(('head', 'sub'), 'ctx'), may hold values from -0.0625 to 0.0625
Outputs:
- key_cache_decode: bfloat16 [8, 8192, 8, 128], P(('groups', 'ctx'), None, ('head', 'sub')), parts along dimension 0
- value_cache_decode: bfloat16 [8, 8192, 8, 128], P(('groups', 'ctx'), None, ('head', 'sub')), parts along dimension 0
- first_out: bfloat16 [8, 8192], P(('groups', 'head', 'sub'), 'ctx'), parts along dimension 0
- second_out: bfloat16 [8, 8192], P(('groups', 'head', 'sub'), 'ctx'), parts along dimension 0
The draws below stay inside these ranges and needn't reach their ends.
There are 2 independent parts, one for each index of `groups`. The reference program is written for one: setup_inputs(seed, part) draws one part's arguments, and reference() takes and returns one part's arrays. A program takes and returns all parts, laid end to end along the dimension named above; an argument that names none is the same for every part. Nothing has to cross between parts.
Inputs may be any that keep to these rules, and one draw needn't show every extreme that they name: `lengths`: some request has a prompt of exactly 8192 positions. A permutation of the requests; with R = 4 / 4 requests an owner, decode owner c (the index along ctx) serves the requests owner_order[c * R] to owner_order[c * R + R - 1], in that order.
All inputs are finite; a program needn't handle non-finite values.
Results may differ from the reference program's by a relative error of at most 0.0039.
Values may be sent and summed in bfloat16 or wider, within the bound.
No kernel may reach another device: no remote copies, remote signals or barrier semaphores. Data moves between devices by JAX's collectives and lax.ppermute only.
A program may use at most 128 MiB of HBM per device.

```python
import math
import jax
import jax.numpy as jnp
import numpy as np
from jax import lax

D = 8192
HQ = 64
KVH = 8
HD = 128
SEQ = 8192
REQS = 4


def token_scales(scale_key, growth):
    column_key, row_key = jax.random.split(scale_key)
    positions = jnp.arange(D, dtype=jnp.float32) / D
    column_scale = jnp.exp(jax.random.uniform(column_key, (1, D), jnp.float32, math.log(0.3), math.log(3.0)))
    column_scale = column_scale * jnp.sqrt(1.0 + growth * positions)[None, :]
    row_scale = jnp.exp(jax.random.uniform(row_key, (REQS, 1), jnp.float32, 0.0, math.log(10.0)))
    return column_scale * row_scale


def draw_first_tokens(key, part):
    key = jax.random.fold_in(key, 11)
    scale_key, value_key = jax.random.split(key)
    random_part = jnp.clip(jax.random.normal(value_key, (REQS, D), jnp.float32), -4.0, 4.0)
    scales = token_scales(scale_key, 2.0)
    return (random_part * scales).astype(jnp.bfloat16)


def draw_second_tokens(key, part):
    key = jax.random.fold_in(key, 13)
    scale_key, value_key = jax.random.split(key)
    random_part = jnp.clip(jax.random.normal(value_key, (REQS, D), jnp.float32), -4.0, 4.0)
    scales = token_scales(scale_key, 2.0)
    return (random_part * scales).astype(jnp.bfloat16)


def draw_key_cache(key, part):
    key = jax.random.fold_in(key, 23)
    value_key, scale_key = jax.random.split(key, 2)
    shape_all = (REQS, SEQ, KVH, HD)
    scales = jnp.exp(jax.random.uniform(scale_key, (REQS, SEQ, KVH, 1), jnp.float32, math.log(0.3), math.log(3.0)))
    random_part = jnp.clip(jax.random.normal(value_key, shape_all, jnp.float32), -4.0, 4.0)
    return (random_part * scales).astype(jnp.bfloat16)


def query_base(base_key):
    return jnp.clip(jax.random.normal(base_key, (D, HQ * HD), jnp.float32), -4.0, 4.0)


def draw_w_query(key, part):
    base = query_base(key)
    return (base * D ** (-0.5)).astype(jnp.bfloat16)


def draw_w_key(key, part):
    base = query_base(key)
    key = jax.random.fold_in(key, 37)
    aligned = base.reshape(D, KVH, HQ // KVH, HD)[:, :, 0, :].reshape(D, KVH * HD)
    noise_part = jnp.clip(jax.random.normal(key, (D, KVH * HD), jnp.float32), -4.0, 4.0)
    spread_factor = 3.0
    return ((aligned + spread_factor * noise_part) * D ** (-0.5)).astype(jnp.bfloat16)


def block_levels(stream_key, extent, pieces, low, largest):
    def one(axis_at, shards_of):
        steps = jax.random.uniform(jax.random.fold_in(jax.random.fold_in(stream_key, 6), axis_at), (shards_of,), jnp.float32, low / len(pieces), largest / len(pieces))
        return jnp.repeat(jnp.exp(steps), extent[axis_at] // shards_of).reshape((-1,) + (1,) * (len(extent) - axis_at - 1))

    gain = one(*pieces[0])
    for cut in pieces[1:]:
        gain = gain * one(*cut)
    return gain


def profile(number_of, total, reach, lean):
    portions = [(1 << 20) // math.isqrt(standing ** lean) + 1 for standing in range(2, number_of + 1)]
    spare, given = total - reach - (number_of - 1), [1] * (number_of - 1)
    while spare > 0:
        movable = [i for i in range(number_of - 1) if given[i] < reach]
        mass, remaining = sum([portions[i] for i in movable]), spare
        for i in movable:
            more = min(reach - given[i], max(1, remaining * portions[i] // mass), spare)
            given[i] = given[i] + more
            spare = spare - more
    return np.array([reach] + given)


def ragged_sizes(own_key, number_of, total, bound, lean):
    if number_of == 2:
        one = jax.random.randint(own_key, (), max(1, total - bound), min(bound, total - 1) + 1)
        return jnp.stack([one, total - one])
    sizes = jnp.asarray(profile(number_of, total, bound, lean), jnp.int32)
    couples = (number_of - 1) // 2
    donor, sink = sizes[1:1 + 2 * couples:2], sizes[2:2 + 2 * couples:2]
    margin = jnp.minimum(donor - 1, bound - sink)
    shifted = jax.random.randint(jax.random.fold_in(own_key, 1), (couples,), 0, 1 << 20) % (margin + 1)
    sizes = sizes.at[1:1 + 2 * couples:2].set(donor - shifted).at[2:2 + 2 * couples:2].set(sink + shifted)
    return sizes[jax.random.permutation(jax.random.fold_in(own_key, 2), number_of)]


def bell_draw(own_key, extent, spread, reach, shards=(), kind=jnp.bfloat16):
    gain = block_levels(own_key, extent, shards, -0.22, 0.18) if shards else 1.0
    entries = jax.random.normal(own_key, extent, jnp.float32) * spread * gain
    return jnp.minimum(jnp.maximum(entries, -reach), reach).astype(kind)


def setup_inputs(seed: int = 0, part: int = 0) -> dict:
    key_list = jax.random.split(jax.random.key(seed), 12)
    part_keys = jax.random.split(jax.random.fold_in(key_list[11], part), 12)
    return {
        "key_cache": draw_key_cache(jax.random.fold_in(jax.random.fold_in(key_list[11], part), 71), part),
        "value_cache": bell_draw(part_keys[1], (REQS, SEQ, KVH, HD), 1.0, 6.0, ((1, 8), (2, 2))),
        "lengths": ragged_sizes(part_keys[2], REQS, REQS * SEQ // 2, SEQ, 2).astype(jnp.int32),
        "owner_order": jax.random.permutation(part_keys[3], REQS).astype(jnp.int32),
        "first_tokens": draw_first_tokens(jax.random.fold_in(jax.random.fold_in(key_list[11], part), 71), part),
        "second_tokens": draw_second_tokens(jax.random.fold_in(jax.random.fold_in(key_list[11], part), 71), part),
        "norm_gain": jnp.clip(1.0 + 0.18 * jax.random.normal(key_list[6], (D,), jnp.float32), 0.099609375, 1.8984375).astype(jnp.bfloat16),
        "w_query": draw_w_query(jax.random.fold_in(key_list[11], 71), part),
        "w_key": draw_w_key(jax.random.fold_in(key_list[11], 71), part),
        "w_value": bell_draw(key_list[9], (D, KVH * HD), D ** -0.5, 0.0625, ((0, 4), (1, 4))),
        "w_out": bell_draw(key_list[10], (HQ * HD, D), (HQ * HD) ** -0.5, 0.0625, ((0, 4), (1, 4))),
    }


theta_base = 500000.0
eps_norm = 1e-05
masked_score = -1e+30

def rotate(vectors, positions):
    half_dim = vectors.shape[-1] // 2
    exponents = jnp.arange(half_dim, dtype=jnp.float32) * (2.0 / vectors.shape[-1])
    frequency = theta_base ** (-exponents)
    angles = positions[:, None, None] * frequency[None, None, :]
    cosines = jnp.cos(angles)
    sines = jnp.sin(angles)
    lower_part = vectors[..., :half_dim]
    upper_part = vectors[..., half_dim:]
    return jnp.concatenate([lower_part * cosines - upper_part * sines, upper_part * cosines + lower_part * sines], axis=-1)

def project(tokens, positions, norm_gain, w_query, w_key, w_value):
    wide = tokens.astype(jnp.float32)
    row_squares = lax.optimization_barrier(jnp.sum(wide * wide, axis=1))
    normed = (wide * lax.rsqrt(row_squares / D + eps_norm)[:, None] * norm_gain.astype(jnp.float32)[None, :]).astype(jnp.bfloat16)
    queries = jnp.dot(normed, w_query, preferred_element_type=jnp.float32).reshape(-1, HQ, HD)
    new_keys = jnp.dot(normed, w_key, preferred_element_type=jnp.float32).reshape(-1, KVH, HD)
    new_values = jnp.dot(normed, w_value, preferred_element_type=jnp.float32).reshape(-1, KVH, HD).astype(jnp.bfloat16)
    return (rotate(queries, positions).astype(jnp.bfloat16), rotate(new_keys, positions).astype(jnp.bfloat16), new_values)

def attend_one(operands):
    queries, cached_keys, cached_values, fresh_keys, fresh_values, length = operands
    score_factor = HD ** (-0.5)
    grouped_heads = queries.astype(jnp.float32).reshape(KVH, HQ // KVH, HD)
    logit_scores = jnp.einsum('klz,ikz->kli', grouped_heads, cached_keys.astype(jnp.float32)) * score_factor
    live_mask = jnp.arange(SEQ, dtype=jnp.int32) < length
    logit_scores = jnp.where(live_mask[None, None, :], logit_scores, masked_score)
    fresh_scores = jnp.einsum('grd,ngd->grn', grouped_heads, fresh_keys.astype(jnp.float32)) * score_factor
    row_max = jnp.maximum(lax.optimization_barrier(jnp.max(logit_scores, axis=2)), lax.optimization_barrier(jnp.max(fresh_scores, axis=2)))[..., None]
    weights = jnp.exp(logit_scores - row_max)
    fresh_weights = jnp.exp(fresh_scores - row_max)
    denominator = lax.optimization_barrier(jnp.sum(weights, axis=2)) + lax.optimization_barrier(jnp.sum(fresh_weights, axis=2))
    rounded_scores = lax.optimization_barrier(weights.astype(jnp.bfloat16)).astype(jnp.float32)
    fresh_rounded = lax.optimization_barrier(fresh_weights.astype(jnp.bfloat16)).astype(jnp.float32)
    weighted_numerator = jnp.einsum('ocq,qou->ocu', rounded_scores, cached_values.astype(jnp.float32))
    weighted_numerator = weighted_numerator + jnp.einsum('grn,ngd->grd', fresh_rounded, fresh_values.astype(jnp.float32))
    return (weighted_numerator / denominator[..., None]).reshape(HQ * HD).astype(jnp.bfloat16)

def reference(key_cache, value_cache, lengths, owner_order, first_tokens, second_tokens, norm_gain, w_query, w_key, w_value, w_out):
    positions = lengths.astype(jnp.float32)
    first_queries, first_keys, first_values = project(first_tokens, positions, norm_gain, w_query, w_key, w_value)
    second_queries, second_keys, second_values = project(second_tokens, positions + 1.0, norm_gain, w_query, w_key, w_value)
    attended_first = lax.map(attend_one, (first_queries, key_cache, value_cache, first_keys[:, None], first_values[:, None], lengths))
    keys_both = jnp.stack([first_keys, second_keys], axis=1)
    values_both = jnp.stack([first_values, second_values], axis=1)
    attended_second = lax.map(attend_one, (second_queries, key_cache, value_cache, keys_both, values_both, lengths))
    first_rows = jnp.take(first_tokens, owner_order, axis=0).astype(jnp.float32)
    second_rows = jnp.take(second_tokens, owner_order, axis=0).astype(jnp.float32)
    first_out = (first_rows + jnp.dot(jnp.take(attended_first, owner_order, axis=0), w_out, preferred_element_type=jnp.float32)).astype(jnp.bfloat16)
    second_out = (second_rows + jnp.dot(jnp.take(attended_second, owner_order, axis=0), w_out, preferred_element_type=jnp.float32)).astype(jnp.bfloat16)
    key_cache_decode = jnp.take(key_cache, owner_order, axis=0)
    value_cache_decode = jnp.take(value_cache, owner_order, axis=0)
    return (key_cache_decode, value_cache_decode, first_out, second_out)
```

```python
import functools

import jax
import jax.numpy as jnp
from jax import lax
from jax.experimental import pallas as pl
from jax.experimental.pallas import tpu as pltpu
from jax.sharding import PartitionSpec as P

theta_base = 500000.0
eps_norm = 1e-05
masked_score = -1e30
LANES = 128
VMEM_BYTES = 48 * 1024 * 1024


def rotate(vectors, positions):
    half_dim = vectors.shape[-1] // 2
    exponents = jnp.arange(half_dim, dtype=jnp.float32) * (2.0 / vectors.shape[-1])
    frequency = theta_base ** (-exponents)
    angles = positions[..., None, None] * frequency
    cosines = jnp.cos(angles)
    sines = jnp.sin(angles)
    lower_part = vectors[..., :half_dim]
    upper_part = vectors[..., half_dim:]
    return jnp.concatenate(
        [lower_part * cosines - upper_part * sines, upper_part * cosines + lower_part * sines],
        axis=-1,
    )


def arrange(cache, owner_order, sub_count):
    requests, shard_length, heads, head_dim = cache.shape
    heads_decode = heads // sub_count
    split = cache.reshape(requests, shard_length, sub_count, heads_decode, head_dim)

    def kernel(order_ref, in_ref, out_ref, sems):
        copies = []
        for i in range(requests):
            for s in range(sub_count):
                copy = pltpu.make_async_copy(
                    in_ref.at[order_ref[i], :, s], out_ref.at[i, s], sems.at[i, s]
                )
                copy.start()
                copies.append(copy)
        for copy in copies:
            copy.wait()

    return pl.pallas_call(
        kernel,
        out_shape=jax.ShapeDtypeStruct(
            (requests, sub_count, shard_length, heads_decode, head_dim), cache.dtype
        ),
        in_specs=[
            pl.BlockSpec(memory_space=pltpu.SMEM),
            pl.BlockSpec(memory_space=pltpu.HBM),
        ],
        out_specs=pl.BlockSpec(memory_space=pltpu.HBM),
        scratch_shapes=[pltpu.SemaphoreType.DMA((requests, sub_count))],
        cost_estimate=pl.CostEstimate(
            flops=0, transcendentals=0, bytes_accessed=2 * cache.size * cache.dtype.itemsize
        ),
        name="arrange",
    )(owner_order, split)


def attend_shard(queries, keys, values, lengths, first_place, score_factor):
    requests, shard_length, heads, head_dim = keys.shape
    rows = queries.shape[1]
    per_head = rows // heads
    columns = shard_length * heads
    flat_keys = keys.reshape(requests, columns, head_dim)
    flat_values = values.reshape(requests, columns, head_dim)

    def kernel(lengths_ref, place_ref, q_ref, k_ref, v_ref, acc_ref, max_ref, sum_ref):
        request = pl.program_id(0)
        scores = (
            lax.dot_general(
                q_ref[0], k_ref[0], (((1,), (1,)), ((), ())), preferred_element_type=jnp.float32
            )
            * score_factor
        )
        row = lax.broadcasted_iota(jnp.int32, (rows, columns), 0)
        column = lax.broadcasted_iota(jnp.int32, (rows, columns), 1)
        live_columns = (lengths_ref[request] - place_ref[0]) * heads
        live = (lax.rem(column, heads) == lax.div(row, per_head)) & (column < live_columns)
        scores = jnp.where(live, scores, masked_score)
        row_max = jnp.max(scores, axis=1, keepdims=True)
        weights = jnp.where(live, jnp.exp(scores - row_max), 0.0)
        acc_ref[0] = jnp.dot(
            weights.astype(jnp.bfloat16), v_ref[0], preferred_element_type=jnp.float32
        )
        max_ref[0] = jnp.broadcast_to(row_max, (rows, head_dim))
        sum_ref[0] = jnp.broadcast_to(
            jnp.sum(weights, axis=1, keepdims=True), (rows, head_dim)
        )

    small = pl.BlockSpec((1, rows, head_dim), lambda r, *_: (r, 0, 0))
    large = pl.BlockSpec((1, columns, head_dim), lambda r, *_: (r, 0, 0))
    result = jax.ShapeDtypeStruct((requests, rows, head_dim), jnp.float32)
    return pl.pallas_call(
        kernel,
        out_shape=(result, result, result),
        grid_spec=pltpu.PrefetchScalarGridSpec(
            num_scalar_prefetch=2,
            grid=(requests,),
            in_specs=[small, large, large],
            out_specs=(small, small, small),
        ),
        compiler_params=pltpu.CompilerParams(vmem_limit_bytes=VMEM_BYTES),
        cost_estimate=pl.CostEstimate(
            flops=4 * requests * rows * columns * head_dim,
            transcendentals=requests * rows * columns,
            bytes_accessed=4 * keys.size,
        ),
        name="attend_shard",
    )(lengths, first_place, queries, flat_keys, flat_values)


def local(
    width,
    key_cache,
    value_cache,
    lengths,
    owner_order,
    first_tokens,
    second_tokens,
    norm_gain,
    w_query,
    w_key,
    w_value,
    w_out,
):
    ctx_count = lax.axis_size("ctx")
    sub_count = lax.axis_size("sub")
    requests, shard_length, heads, head_dim = key_cache.shape
    per_owner = requests // ctx_count
    heads_decode = heads // sub_count
    ctx_index = lax.axis_index("ctx")
    sub_index = lax.axis_index("sub")
    take = functools.partial(jnp.take, mode="clip")

    def hand_off(cache):
        blocks = arrange(cache, owner_order, sub_count)
        blocks = blocks.reshape(ctx_count, per_owner, sub_count, shard_length, heads_decode, head_dim)
        blocks = jnp.swapaxes(blocks, 1, 2)
        moved = lax.all_to_all(
            blocks.reshape(
                ctx_count * sub_count, per_owner, shard_length, heads_decode, head_dim
            ),
            ("ctx", "sub"),
            split_axis=0,
            concat_axis=2,
            tiled=True,
        )
        return moved.reshape(per_owner, -1, heads_decode, head_dim)

    moved_keys = hand_off(key_cache)
    moved_values = hand_off(value_cache)

    query_width = w_query.shape[1]
    key_width = w_key.shape[1]
    group_size = query_width // head_dim // heads_decode
    score_factor = head_dim ** (-0.5)
    rows_local = first_tokens.shape[0]
    tokens = lax.all_gather(
        jnp.stack([first_tokens, second_tokens]), ("head", "sub"), axis=1, tiled=True
    )
    wide = tokens.astype(jnp.float32).reshape(2 * requests, -1)
    gained = wide * norm_gain.astype(jnp.float32)
    upper = lax.reduce_precision(gained, 8, 7)
    lower = gained - upper
    halves = jnp.concatenate([upper, lower]).astype(jnp.bfloat16)
    products = jnp.concatenate(
        [
            jnp.dot(halves, weight, preferred_element_type=jnp.float32)
            for weight in (w_query, w_key, w_value)
        ],
        axis=1,
    )
    squares = jnp.sum(wide * wide, axis=1, keepdims=True)
    partial = jnp.concatenate(
        [
            products[: 2 * requests] + products[2 * requests :],
            jnp.broadcast_to(squares, (2 * requests, LANES)),
        ],
        axis=1,
    )
    summed = jnp.sum(lax.all_gather(partial, "ctx", axis=0), axis=0)
    raw = summed[:, :-LANES] * lax.rsqrt(summed[:, -LANES:][:, :1] / width + eps_norm)
    raw = raw.reshape(2, requests, -1, head_dim)
    positions = lengths.astype(jnp.float32)[None, :] + jnp.arange(2, dtype=jnp.float32)[:, None]
    query_heads = query_width // head_dim
    key_heads = key_width // head_dim
    rotated = rotate(raw[:, :, : query_heads + key_heads], positions).astype(jnp.bfloat16)
    queries = rotated[:, :, :query_heads].reshape(2, requests, heads_decode, group_size, head_dim)
    fresh_keys = rotated[:, :, query_heads:]
    fresh_values = raw[:, :, query_heads + key_heads :].astype(jnp.bfloat16)

    per_head = 2 * group_size
    own_queries = jnp.transpose(queries, (1, 2, 0, 3, 4)).reshape(
        requests, heads_decode * per_head, head_dim
    )
    all_queries = lax.all_gather(own_queries, "sub", axis=1, tiled=True)
    shard_index = ctx_index * sub_count + sub_index
    first_place = jnp.reshape(shard_index * shard_length, (1,)).astype(jnp.int32)
    sums, maxima, totals = attend_shard(
        all_queries, key_cache, value_cache, lengths, first_place, score_factor
    )

    own_rows = heads_decode * per_head

    def pack(core):
        part = lambda x: lax.dynamic_slice_in_dim(x, core * own_rows, own_rows, 1)
        return (part(sums), part(maxima)[:, :, 0], part(totals)[:, :, 0])

    def send_form(sums, maxima, totals):
        return jnp.concatenate(
            [x.reshape(-1, head_dim) for x in (sums, maxima, totals)], axis=0
        )

    count = requests * own_rows
    extra = count // head_dim

    def unpack(packed):
        lead = packed.shape[:-2]
        shape = lead + (requests, own_rows)
        return (
            packed[..., :count, :].reshape(shape + (head_dim,)),
            packed[..., count : count + extra, :].reshape(shape),
            packed[..., count + extra :, :].reshape(shape),
        )

    def merge(sums, maxima, totals):
        largest = jnp.max(maxima, axis=0)
        scale = jnp.exp(maxima - largest)
        return (
            jnp.sum(sums * scale[..., None], axis=0),
            largest,
            jnp.sum(totals * scale, axis=0),
        )

    kept = pack(sub_index)
    for shift in range(1, sub_count):
        pairs = [(i, (i + shift) % sub_count) for i in range(sub_count)]
        sent = send_form(*pack(lax.rem(sub_index + shift, sub_count)))
        received = unpack(lax.ppermute(sent, "sub", pairs))
        kept = merge(*(jnp.stack([a, b]) for a, b in zip(kept, received)))
    gathered = unpack(lax.all_gather(send_form(*kept), "ctx", axis=0))
    sums, maxima, totals = merge(*gathered)

    grouped = own_queries.reshape(requests, heads_decode, 2, group_size, head_dim).astype(
        jnp.float32
    )
    keys_wide = jnp.transpose(fresh_keys, (1, 2, 0, 3)).astype(jnp.float32)
    values_wide = jnp.transpose(fresh_values, (1, 2, 0, 3)).astype(jnp.float32)
    fresh_scores = (
        jnp.sum(grouped[:, :, :, :, None, :] * keys_wide[:, :, None, None, :, :], axis=-1)
        * score_factor
    )
    step = jnp.arange(2)
    seen = (step[None, :] <= step[:, None])[None, None, :, None, :]
    fresh_scores = jnp.where(seen, fresh_scores, masked_score)
    shape = (requests, heads_decode, 2, group_size)
    maxima = maxima.reshape(shape)
    largest = jnp.maximum(maxima, jnp.max(fresh_scores, axis=-1))
    old_scale = jnp.exp(maxima - largest)
    fresh_weights = jnp.where(seen, jnp.exp(fresh_scores - largest[..., None]), 0.0)
    denominator = totals.reshape(shape) * old_scale + jnp.sum(fresh_weights, axis=-1)
    numerator = sums.reshape(shape + (head_dim,)) * old_scale[..., None] + jnp.sum(
        lax.reduce_precision(fresh_weights, 8, 7)[..., None]
        * values_wide[:, :, None, None, :, :],
        axis=-2,
    )
    attended = (numerator / denominator[..., None]).astype(jnp.bfloat16)

    attended = take(attended, owner_order, axis=0)
    attended = jnp.transpose(attended, (2, 0, 1, 3, 4)).reshape(2 * requests, query_width)
    branch = jnp.dot(attended, w_out, preferred_element_type=jnp.float32)
    branch = branch.reshape(2, requests, -1)
    row_start = lax.axis_index(("head", "sub")) * rows_local
    parts = lax.all_gather(branch, ("head", "sub"), axis=0)
    parts = lax.dynamic_slice_in_dim(parts, row_start, rows_local, 2)
    own_ids = lax.dynamic_slice_in_dim(owner_order, row_start, rows_local)
    residual = take(tokens, own_ids, axis=1).astype(jnp.float32)
    result = (residual + jnp.sum(parts, axis=0)).astype(jnp.bfloat16)
    return (moved_keys, moved_values, result[0], result[1])


def solution(mesh):
    def whole(*arrays):
        return jax.shard_map(
            functools.partial(local, arrays[6].shape[0]),
            mesh=mesh,
            in_specs=(
                P("groups", ("ctx", "sub"), "head", None),
                P("groups", ("ctx", "sub"), "head", None),
                P("groups"),
                P("groups"),
                P(("groups", "head", "sub"), "ctx"),
                P(("groups", "head", "sub"), "ctx"),
                P("ctx"),
                P("ctx", ("head", "sub")),
                P("ctx", ("head", "sub")),
                P("ctx", ("head", "sub")),
                P(("head", "sub"), "ctx"),
            ),
            out_specs=(
                P(("groups", "ctx"), None, ("head", "sub"), None),
                P(("groups", "ctx"), None, ("head", "sub"), None),
                P(("groups", "head", "sub"), "ctx"),
                P(("groups", "head", "sub"), "ctx"),
            ),
            check_vma=False,
        )(*arrays)

    return whole
```

```python
import functools

import jax
import jax.numpy as jnp
from jax import lax
from jax.experimental import pallas as pl
from jax.experimental.pallas import tpu as pltpu
from jax.sharding import PartitionSpec as P

theta_base = 500000.0
eps_norm = 1e-05
masked_score = -1e30
LANES = 128
VMEM_BYTES = 48 * 1024 * 1024


def rotate(vectors, positions):
    half_dim = vectors.shape[-1] // 2
    exponents = jnp.arange(half_dim, dtype=jnp.float32) * (2.0 / vectors.shape[-1])
    frequency = theta_base ** (-exponents)
    angles = positions[..., None, None] * frequency
    cosines = jnp.cos(angles)
    sines = jnp.sin(angles)
    lower_part = vectors[..., :half_dim]
    upper_part = vectors[..., half_dim:]
    return jnp.concatenate(
        [lower_part * cosines - upper_part * sines, upper_part * cosines + lower_part * sines],
        axis=-1,
    )


def arrange(cache, request, core, core_count, after):
    _, shard_length, heads, head_dim = cache.shape
    heads_decode = heads // core_count
    steps = 4
    places = shard_length // steps
    block = jax.ShapeDtypeStruct((shard_length, heads_decode, head_dim), cache.dtype)

    def kernel(request_ref, core_ref, in_ref, *rest):
        out_refs = rest[len(after) :]
        for own in range(core_count):

            @pl.when(core_ref[0] == own)
            def _():
                for f, out_ref in enumerate(out_refs):
                    low = (own + f) % core_count * heads_decode
                    out_ref[...] = in_ref[0, :, low : low + heads_decode, :]

    blocks = pl.pallas_call(
        kernel,
        out_shape=(block,) * core_count,
        grid_spec=pltpu.PrefetchScalarGridSpec(
            num_scalar_prefetch=2,
            grid=(steps,),
            in_specs=[
                pl.BlockSpec((1, places, heads, head_dim), lambda i, r, c: (r[0], i, 0, 0))
            ]
            + [pl.BlockSpec(memory_space=pl.ANY)] * len(after),
            out_specs=(pl.BlockSpec((places, heads_decode, head_dim), lambda i, r, c: (i, 0, 0)),)
            * core_count,
        ),
        compiler_params=pltpu.CompilerParams(vmem_limit_bytes=VMEM_BYTES),
        cost_estimate=pl.CostEstimate(
            flops=0,
            transcendentals=0,
            bytes_accessed=4 * shard_length * heads * head_dim,
        ),
        name="arrange",
    )(request, core, cache, *after)
    return [x.reshape(shard_length * heads_decode, head_dim) for x in blocks]


def assemble(blocks, places, rows, filled=None):
    block_rows, head_dim = blocks[0].shape
    count = len(blocks)
    extra = [] if filled is None else [filled]

    def kernel(places_ref, *refs):
        in_refs = refs[:count]
        out_ref, held, in_sems, out_sems = refs[count + len(extra) :]
        into = [
            pltpu.make_async_copy(in_refs[i], held.at[i], in_sems.at[i]) for i in range(count)
        ]
        out_of = [
            pltpu.make_async_copy(
                held.at[i],
                out_ref.at[pl.ds(pl.multiple_of(places_ref[i], block_rows), block_rows)],
                out_sems.at[i],
            )
            for i in range(count)
        ]
        for copy in into:
            copy.start()
        for i in range(count):
            into[i].wait()
            out_of[i].start()
        for copy in out_of:
            copy.wait()

    return pl.pallas_call(
        kernel,
        out_shape=jax.ShapeDtypeStruct((rows, head_dim), blocks[0].dtype),
        in_specs=[pl.BlockSpec(memory_space=pltpu.SMEM)]
        + [pl.BlockSpec(memory_space=pl.ANY)] * count
        + [pl.BlockSpec(memory_space=pltpu.HBM)] * len(extra),
        out_specs=pl.BlockSpec(memory_space=pltpu.HBM),
        scratch_shapes=[
            pltpu.VMEM((count, block_rows, head_dim), blocks[0].dtype),
            pltpu.SemaphoreType.DMA((count,)),
            pltpu.SemaphoreType.DMA((count,)),
        ],
        input_output_aliases={1 + count: 0} if extra else {},
        compiler_params=pltpu.CompilerParams(vmem_limit_bytes=VMEM_BYTES),
        cost_estimate=pl.CostEstimate(
            flops=0, transcendentals=0, bytes_accessed=4 * count * block_rows * head_dim
        ),
        name="assemble",
    )(places, *blocks, *extra)


def attend_shard(queries, keys, values, lengths, first_place, score_factor):
    requests, shard_length, heads, head_dim = keys.shape
    rows = queries.shape[1]
    per_head = rows // heads
    columns = shard_length * heads
    flat_keys = keys.reshape(requests, columns, head_dim)
    flat_values = values.reshape(requests, columns, head_dim)

    def kernel(lengths_ref, place_ref, q_ref, k_ref, v_ref, acc_ref, max_ref, sum_ref):
        request = pl.program_id(0)
        scores = (
            lax.dot_general(
                q_ref[0], k_ref[0], (((1,), (1,)), ((), ())), preferred_element_type=jnp.float32
            )
            * score_factor
        )
        row = lax.broadcasted_iota(jnp.int32, (rows, columns), 0)
        column = lax.broadcasted_iota(jnp.int32, (rows, columns), 1)
        live_columns = (lengths_ref[request] - place_ref[0]) * heads
        live = (lax.rem(column, heads) == lax.div(row, per_head)) & (column < live_columns)
        scores = jnp.where(live, scores, masked_score)
        row_max = jnp.max(scores, axis=1, keepdims=True)
        weights = jnp.where(live, jnp.exp(scores - row_max), 0.0)
        acc_ref[0] = jnp.dot(
            weights.astype(jnp.bfloat16), v_ref[0], preferred_element_type=jnp.float32
        )
        max_ref[0] = jnp.broadcast_to(row_max, (rows, head_dim))
        sum_ref[0] = jnp.broadcast_to(
            jnp.sum(weights, axis=1, keepdims=True), (rows, head_dim)
        )

    small = pl.BlockSpec((1, rows, head_dim), lambda r, *_: (r, 0, 0))
    large = pl.BlockSpec((1, columns, head_dim), lambda r, *_: (r, 0, 0))
    result = jax.ShapeDtypeStruct((requests, rows, head_dim), jnp.float32)
    return pl.pallas_call(
        kernel,
        out_shape=(result, result, result),
        grid_spec=pltpu.PrefetchScalarGridSpec(
            num_scalar_prefetch=2,
            grid=(requests,),
            in_specs=[small, large, large],
            out_specs=(small, small, small),
        ),
        compiler_params=pltpu.CompilerParams(vmem_limit_bytes=VMEM_BYTES),
        cost_estimate=pl.CostEstimate(
            flops=4 * requests * rows * columns * head_dim,
            transcendentals=requests * rows * columns,
            bytes_accessed=4 * keys.size,
        ),
        name="attend_shard",
    )(lengths, first_place, queries, flat_keys, flat_values)


def local(
    width,
    key_cache,
    value_cache,
    lengths,
    owner_order,
    first_tokens,
    second_tokens,
    norm_gain,
    w_query,
    w_key,
    w_value,
    w_out,
):
    ctx_count = lax.axis_size("ctx")
    sub_count = lax.axis_size("sub")
    requests, shard_length, heads, head_dim = key_cache.shape
    assert requests == ctx_count
    heads_decode = heads // sub_count
    ctx_index = lax.axis_index("ctx")
    sub_index = lax.axis_index("sub")
    take = functools.partial(jnp.take, mode="clip")

    device_rows = shard_length * heads_decode
    core = jnp.reshape(sub_index, (1,)).astype(jnp.int32)
    received = ({}, {})

    def place_of(shift, flip):
        source = lax.rem(ctx_index - shift + ctx_count, ctx_count) * sub_count + lax.rem(
            sub_index - flip + sub_count, sub_count
        )
        return source * device_rows

    def hand_off(which, shift, after=()):
        owner = lax.rem(ctx_index + shift, ctx_count)
        request = lax.dynamic_slice_in_dim(owner_order, owner, 1)
        blocks = arrange(
            (key_cache, value_cache)[which], request, core, sub_count, after
        )
        for flip, block in enumerate(blocks):
            if shift or flip:
                pairs = [
                    (
                        c * sub_count + s,
                        (c + shift) % ctx_count * sub_count + (s + flip) % sub_count,
                    )
                    for c in range(ctx_count)
                    for s in range(sub_count)
                ]
                block = lax.ppermute(block, ("ctx", "sub"), pairs)
            received[which][shift, flip] = block

    def sum_shifted(values, combine):
        return combine(
            [values]
            + [
                lax.ppermute(
                    values, "ctx", [(c, (c + shift) % ctx_count) for c in range(ctx_count)]
                )
                for shift in range(1, ctx_count)
            ]
        )

    middle = ctx_count // 2
    hand_off(0, middle)

    query_width = w_query.shape[1]
    key_width = w_key.shape[1]
    group_size = query_width // head_dim // heads_decode
    score_factor = head_dim ** (-0.5)
    rows_local = first_tokens.shape[0]
    tokens = lax.all_gather(
        jnp.stack([first_tokens, second_tokens]), ("head", "sub"), axis=1, tiled=True
    )
    wide = tokens.astype(jnp.float32).reshape(2 * requests, -1)
    gained = wide * norm_gain.astype(jnp.float32)
    upper = lax.reduce_precision(gained, 8, 7)
    lower = gained - upper
    halves = jnp.concatenate([upper, lower]).astype(jnp.bfloat16)
    products = jnp.concatenate(
        [
            jnp.dot(halves, weight, preferred_element_type=jnp.float32)
            for weight in (w_query, w_key, w_value)
        ],
        axis=1,
    )
    squares = jnp.sum(wide * wide, axis=1, keepdims=True)
    partial = jnp.concatenate(
        [
            products[: 2 * requests] + products[2 * requests :],
            jnp.broadcast_to(squares, (2 * requests, LANES)),
        ],
        axis=1,
    )
    summed = sum_shifted(partial, lambda parts: functools.reduce(jnp.add, parts))
    for which in (0, 1):
        for shift in range(1, middle):
            hand_off(which, shift, (partial,))
        hand_off(which, 0, (partial,))
    raw = summed[:, :-LANES] * lax.rsqrt(summed[:, -LANES:][:, :1] / width + eps_norm)
    raw = raw.reshape(2, requests, -1, head_dim)
    positions = lengths.astype(jnp.float32)[None, :] + jnp.arange(2, dtype=jnp.float32)[:, None]
    query_heads = query_width // head_dim
    key_heads = key_width // head_dim
    rotated = rotate(raw[:, :, : query_heads + key_heads], positions).astype(jnp.bfloat16)
    queries = rotated[:, :, :query_heads].reshape(2, requests, heads_decode, group_size, head_dim)
    fresh_keys = rotated[:, :, query_heads:]
    fresh_values = raw[:, :, query_heads + key_heads :].astype(jnp.bfloat16)

    per_head = 2 * group_size
    own_queries = jnp.transpose(queries, (1, 2, 0, 3, 4)).reshape(
        requests, heads_decode * per_head, head_dim
    )
    all_queries = lax.all_gather(own_queries, "sub", axis=1, tiled=True)
    shard_index = ctx_index * sub_count + sub_index
    first_place = jnp.reshape(shard_index * shard_length, (1,)).astype(jnp.int32)
    sums, maxima, totals = attend_shard(
        all_queries, key_cache, value_cache, lengths, first_place, score_factor
    )

    own_rows = heads_decode * per_head

    def pack(core):
        part = lambda x: lax.dynamic_slice_in_dim(x, core * own_rows, own_rows, 1)
        return (part(sums), part(maxima)[:, :, 0], part(totals)[:, :, 0])

    def send_form(sums, maxima, totals):
        return jnp.concatenate(
            [x.reshape(-1, head_dim) for x in (sums, maxima, totals)], axis=0
        )

    count = requests * own_rows
    extra = count // head_dim

    def unpack(packed):
        lead = packed.shape[:-2]
        shape = lead + (requests, own_rows)
        return (
            packed[..., :count, :].reshape(shape + (head_dim,)),
            packed[..., count : count + extra, :].reshape(shape),
            packed[..., count + extra :, :].reshape(shape),
        )

    def merge(sums, maxima, totals):
        largest = jnp.max(maxima, axis=0)
        scale = jnp.exp(maxima - largest)
        return (
            jnp.sum(sums * scale[..., None], axis=0),
            largest,
            jnp.sum(totals * scale, axis=0),
        )

    kept = pack(sub_index)
    for shift in range(1, sub_count):
        pairs = [(i, (i + shift) % sub_count) for i in range(sub_count)]
        sent = send_form(*pack(lax.rem(sub_index + shift, sub_count)))
        other = unpack(lax.ppermute(sent, "sub", pairs))
        kept = merge(*(jnp.stack([a, b]) for a, b in zip(kept, other)))
    stats = send_form(*kept)
    gathered = unpack(sum_shifted(stats, jnp.stack))
    sums, maxima, totals = merge(*gathered)
    for which in (0, 1):
        for shift in range(middle + 1, ctx_count):
            hand_off(which, shift, (stats,))
    hand_off(1, middle, (stats,))

    grouped = own_queries.reshape(requests, heads_decode, 2, group_size, head_dim).astype(
        jnp.float32
    )
    keys_wide = jnp.transpose(fresh_keys, (1, 2, 0, 3)).astype(jnp.float32)
    values_wide = jnp.transpose(fresh_values, (1, 2, 0, 3)).astype(jnp.float32)
    fresh_scores = (
        jnp.sum(grouped[:, :, :, :, None, :] * keys_wide[:, :, None, None, :, :], axis=-1)
        * score_factor
    )
    step = jnp.arange(2)
    seen = (step[None, :] <= step[:, None])[None, None, :, None, :]
    fresh_scores = jnp.where(seen, fresh_scores, masked_score)
    shape = (requests, heads_decode, 2, group_size)
    maxima = maxima.reshape(shape)
    largest = jnp.maximum(maxima, jnp.max(fresh_scores, axis=-1))
    old_scale = jnp.exp(maxima - largest)
    fresh_weights = jnp.where(seen, jnp.exp(fresh_scores - largest[..., None]), 0.0)
    denominator = totals.reshape(shape) * old_scale + jnp.sum(fresh_weights, axis=-1)
    numerator = sums.reshape(shape + (head_dim,)) * old_scale[..., None] + jnp.sum(
        lax.reduce_precision(fresh_weights, 8, 7)[..., None]
        * values_wide[:, :, None, None, :, :],
        axis=-2,
    )
    attended = (numerator / denominator[..., None]).astype(jnp.bfloat16)

    attended = take(attended, owner_order, axis=0)
    attended = jnp.transpose(attended, (2, 0, 1, 3, 4)).reshape(2 * requests, query_width)
    branch = jnp.dot(attended, w_out, preferred_element_type=jnp.float32)
    branch = branch.reshape(2, requests, -1)
    row_start = lax.axis_index(("head", "sub")) * rows_local
    parts = lax.all_gather(branch, ("head", "sub"), axis=0)
    parts = lax.dynamic_slice_in_dim(parts, row_start, rows_local, 2)
    own_ids = lax.dynamic_slice_in_dim(owner_order, row_start, rows_local)
    residual = take(tokens, own_ids, axis=1).astype(jnp.float32)
    result = (residual + jnp.sum(parts, axis=0)).astype(jnp.bfloat16)

    def outcome(which, last):
        early = [key for key in received[which] if key not in last]
        whole = None
        for keys in (early, last):
            if keys:
                whole = assemble(
                    [received[which][key] for key in keys],
                    jnp.stack([place_of(*key) for key in keys]).astype(jnp.int32),
                    ctx_count * sub_count * device_rows,
                    whole,
                )
        return whole.reshape(1, -1, heads_decode, head_dim)

    moved_keys = outcome(0, [])
    moved_values = outcome(1, [(middle, flip) for flip in range(sub_count)])
    return (moved_keys, moved_values, result[0], result[1])


def solution(mesh):
    def whole(*arrays):
        return jax.shard_map(
            functools.partial(local, arrays[6].shape[0]),
            mesh=mesh,
            in_specs=(
                P("groups", ("ctx", "sub"), "head", None),
                P("groups", ("ctx", "sub"), "head", None),
                P("groups"),
                P("groups"),
                P(("groups", "head", "sub"), "ctx"),
                P(("groups", "head", "sub"), "ctx"),
                P("ctx"),
                P("ctx", ("head", "sub")),
                P("ctx", ("head", "sub")),
                P("ctx", ("head", "sub")),
                P(("head", "sub"), "ctx"),
            ),
            out_specs=(
                P(("groups", "ctx"), None, ("head", "sub"), None),
                P(("groups", "ctx"), None, ("head", "sub"), None),
                P(("groups", "head", "sub"), "ctx"),
                P(("groups", "head", "sub"), "ctx"),
            ),
            check_vma=False,
        )(*arrays)

    return whole
```

```python
import functools

import jax
import jax.numpy as jnp
from jax import lax
from jax.experimental import pallas as pl
from jax.experimental.pallas import tpu as pltpu
from jax.sharding import PartitionSpec as P

theta_base = 500000.0
eps_norm = 1e-05
masked_score = -1e30
LANES = 128
VMEM_BYTES = 48 * 1024 * 1024


def rotate(vectors, positions):
    half_dim = vectors.shape[-1] // 2
    exponents = jnp.arange(half_dim, dtype=jnp.float32) * (2.0 / vectors.shape[-1])
    frequency = theta_base ** (-exponents)
    angles = positions[..., None, None] * frequency
    cosines = jnp.cos(angles)
    sines = jnp.sin(angles)
    lower_part = vectors[..., :half_dim]
    upper_part = vectors[..., half_dim:]
    return jnp.concatenate(
        [lower_part * cosines - upper_part * sines, upper_part * cosines + lower_part * sines],
        axis=-1,
    )


def arrange(caches, request, core, after):
    _, shard_length, heads, head_dim = caches[0].shape
    core_count = 2
    heads_decode = heads // core_count
    steps = 4
    places = shard_length // steps
    count = len(caches)
    pieces = [(w, i) for i in range(steps) for w in range(count)]

    def kernel(where_ref, *refs):
        in_refs = refs[:count]
        out_ref, taken, made, in_sems, out_sems = refs[count + len(after) :]
        rows = lambda i: pl.ds(i * places, places)
        into = [
            pltpu.make_async_copy(
                in_refs[w].at[where_ref[0], rows(i)], taken.at[w, rows(i)], in_sems.at[w, i]
            )
            for w, i in pieces
        ]
        out_of = [
            pltpu.make_async_copy(
                made.at[w, rows(i)], out_ref.at[w, rows(i)], out_sems.at[w, i]
            )
            for w, i in pieces
        ]
        for copy in into:
            copy.start()
        for p, (w, i) in enumerate(pieces):
            into[p].wait()
            for own in range(core_count):

                @pl.when(where_ref[1] == own)
                def _():
                    low = own * heads_decode
                    made[w, rows(i)] = taken[w, rows(i), low : low + heads_decode, :]

            out_of[p].start()
        for copy in out_of:
            copy.wait()

    blocks = pl.pallas_call(
        kernel,
        out_shape=jax.ShapeDtypeStruct(
            (count, shard_length, heads_decode, head_dim), caches[0].dtype
        ),
        in_specs=[pl.BlockSpec(memory_space=pltpu.SMEM)]
        + [pl.BlockSpec(memory_space=pltpu.HBM)] * count
        + [pl.BlockSpec(memory_space=pl.ANY)] * len(after),
        out_specs=pl.BlockSpec(memory_space=pltpu.HBM),
        scratch_shapes=[
            pltpu.VMEM((count, shard_length, heads, head_dim), caches[0].dtype),
            pltpu.VMEM((count, shard_length, heads_decode, head_dim), caches[0].dtype),
            pltpu.SemaphoreType.DMA((count, steps)),
            pltpu.SemaphoreType.DMA((count, steps)),
        ],
        compiler_params=pltpu.CompilerParams(vmem_limit_bytes=VMEM_BYTES),
        cost_estimate=pl.CostEstimate(
            flops=0,
            transcendentals=0,
            bytes_accessed=3 * count * shard_length * heads * head_dim,
        ),
        name="arrange",
    )(jnp.concatenate([request, core]), *caches, *after)
    return blocks.reshape(count, shard_length * heads_decode, head_dim)


def assemble(blocks, places, rows, filled=()):
    arrays, block_rows, head_dim = blocks[0].shape
    count = len(blocks)
    pieces = [(i, w) for i in range(count) for w in range(arrays)]

    def kernel(places_ref, *refs):
        in_refs = refs[:count]
        out_refs = refs[count + len(filled) :][:arrays]
        held, in_sems, out_sems = refs[count + len(filled) + arrays :]
        into = [
            pltpu.make_async_copy(in_refs[i].at[w], held.at[i, w], in_sems.at[i, w])
            for i, w in pieces
        ]
        out_of = [
            pltpu.make_async_copy(
                held.at[i, w],
                out_refs[w].at[pl.ds(pl.multiple_of(places_ref[i], block_rows), block_rows)],
                out_sems.at[i, w],
            )
            for i, w in pieces
        ]
        for copy in into:
            copy.start()
        for p in range(len(pieces)):
            into[p].wait()
            out_of[p].start()
        for copy in out_of:
            copy.wait()

    return pl.pallas_call(
        kernel,
        out_shape=(jax.ShapeDtypeStruct((rows, head_dim), blocks[0].dtype),) * arrays,
        in_specs=[pl.BlockSpec(memory_space=pltpu.SMEM)]
        + [pl.BlockSpec(memory_space=pl.ANY)] * count
        + [pl.BlockSpec(memory_space=pltpu.HBM)] * len(filled),
        out_specs=(pl.BlockSpec(memory_space=pltpu.HBM),) * arrays,
        scratch_shapes=[
            pltpu.VMEM((count, arrays, block_rows, head_dim), blocks[0].dtype),
            pltpu.SemaphoreType.DMA((count, arrays)),
            pltpu.SemaphoreType.DMA((count, arrays)),
        ],
        input_output_aliases={1 + count + w: w for w in range(len(filled))},
        compiler_params=pltpu.CompilerParams(vmem_limit_bytes=VMEM_BYTES),
        cost_estimate=pl.CostEstimate(
            flops=0,
            transcendentals=0,
            bytes_accessed=4 * count * arrays * block_rows * head_dim,
        ),
        name="assemble",
    )(places, *blocks, *filled)


def pair_tokens(first, second, after):
    def kernel(first_ref, second_ref, after_ref, out_ref):
        out_ref[0] = first_ref[...]
        out_ref[1] = second_ref[...]

    whole = pl.BlockSpec(memory_space=pltpu.VMEM)
    return pl.pallas_call(
        kernel,
        out_shape=jax.ShapeDtypeStruct((2,) + first.shape, first.dtype),
        in_specs=[whole, whole, pl.BlockSpec(memory_space=pl.ANY)],
        out_specs=whole,
        name="pair_tokens",
    )(first, second, after)


def attend_shard(queries, keys, values, lengths, first_place, score_factor):
    requests, shard_length, heads, head_dim = keys.shape
    rows = queries.shape[1]
    per_head = rows // heads
    columns = shard_length * heads
    flat_keys = keys.reshape(requests, columns, head_dim)
    flat_values = values.reshape(requests, columns, head_dim)

    def kernel(lengths_ref, place_ref, q_ref, k_ref, v_ref, acc_ref, max_ref, sum_ref):
        request = pl.program_id(0)
        scores = (
            lax.dot_general(
                q_ref[0], k_ref[0], (((1,), (1,)), ((), ())), preferred_element_type=jnp.float32
            )
            * score_factor
        )
        row = lax.broadcasted_iota(jnp.int32, (rows, columns), 0)
        column = lax.broadcasted_iota(jnp.int32, (rows, columns), 1)
        live_columns = (lengths_ref[request] - place_ref[0]) * heads
        live = (lax.rem(column, heads) == lax.div(row, per_head)) & (column < live_columns)
        scores = jnp.where(live, scores, masked_score)
        row_max = jnp.max(scores, axis=1, keepdims=True)
        weights = jnp.where(live, jnp.exp(scores - row_max), 0.0)
        acc_ref[0] = jnp.dot(
            weights.astype(jnp.bfloat16), v_ref[0], preferred_element_type=jnp.float32
        )
        max_ref[0] = jnp.broadcast_to(row_max, (rows, head_dim))
        sum_ref[0] = jnp.broadcast_to(
            jnp.sum(weights, axis=1, keepdims=True), (rows, head_dim)
        )

    small = pl.BlockSpec((1, rows, head_dim), lambda r, *_: (r, 0, 0))
    large = pl.BlockSpec((1, columns, head_dim), lambda r, *_: (r, 0, 0))
    result = jax.ShapeDtypeStruct((requests, rows, head_dim), jnp.float32)
    return pl.pallas_call(
        kernel,
        out_shape=(result, result, result),
        grid_spec=pltpu.PrefetchScalarGridSpec(
            num_scalar_prefetch=2,
            grid=(requests,),
            in_specs=[small, large, large],
            out_specs=(small, small, small),
        ),
        compiler_params=pltpu.CompilerParams(vmem_limit_bytes=VMEM_BYTES),
        cost_estimate=pl.CostEstimate(
            flops=4 * requests * rows * columns * head_dim,
            transcendentals=requests * rows * columns,
            bytes_accessed=4 * keys.size,
        ),
        name="attend_shard",
    )(lengths, first_place, queries, flat_keys, flat_values)


def local(
    width,
    key_cache,
    value_cache,
    lengths,
    owner_order,
    first_tokens,
    second_tokens,
    norm_gain,
    w_query,
    w_key,
    w_value,
    w_out,
):
    ctx_count = lax.axis_size("ctx")
    sub_count = lax.axis_size("sub")
    requests, shard_length, heads, head_dim = key_cache.shape
    assert requests == ctx_count and sub_count == 2
    heads_decode = heads // sub_count
    ctx_index = lax.axis_index("ctx")
    sub_index = lax.axis_index("sub")
    take = functools.partial(jnp.take, mode="clip")

    device_rows = shard_length * heads_decode
    received = {}

    def place_of(shift, flip):
        source = lax.rem(ctx_index - shift + ctx_count, ctx_count) * sub_count + lax.rem(
            sub_index - flip + sub_count, sub_count
        )
        return source * device_rows

    def hand_off(shift, flip, after=()):
        owner = lax.rem(ctx_index + shift, ctx_count)
        request = lax.dynamic_slice_in_dim(owner_order, owner, 1)
        core = jnp.reshape(lax.rem(sub_index + flip, sub_count), (1,)).astype(jnp.int32)
        block = made = arrange((key_cache, value_cache), request, core, after)
        if shift or flip:
            pairs = [
                (
                    c * sub_count + s,
                    (c + shift) % ctx_count * sub_count + (s + flip) % sub_count,
                )
                for c in range(ctx_count)
                for s in range(sub_count)
            ]
            block = lax.ppermute(made, ("ctx", "sub"), pairs)
        received[shift, flip] = block
        return made

    def sum_shifted(values, combine):
        return combine(
            [values]
            + [
                lax.ppermute(
                    values, "ctx", [(c, (c + shift) % ctx_count) for c in range(ctx_count)]
                )
                for shift in range(1, ctx_count)
            ]
        )

    middle = ctx_count // 2
    leading = hand_off(middle, 0)

    query_width = w_query.shape[1]
    key_width = w_key.shape[1]
    group_size = query_width // head_dim // heads_decode
    score_factor = head_dim ** (-0.5)
    rows_local = first_tokens.shape[0]
    tokens = lax.all_gather(
        pair_tokens(first_tokens, second_tokens, leading), ("head", "sub"), axis=1, tiled=True
    )
    wide = tokens.astype(jnp.float32).reshape(2 * requests, -1)
    gained = wide * norm_gain.astype(jnp.float32)
    upper = lax.reduce_precision(gained, 8, 7)
    lower = gained - upper
    halves = jnp.concatenate([upper, lower]).astype(jnp.bfloat16)
    products = jnp.concatenate(
        [
            jnp.dot(halves, weight, preferred_element_type=jnp.float32)
            for weight in (w_query, w_key, w_value)
        ],
        axis=1,
    )
    squares = jnp.sum(wide * wide, axis=1, keepdims=True)
    partial = jnp.concatenate(
        [
            products[: 2 * requests] + products[2 * requests :],
            jnp.broadcast_to(squares, (2 * requests, LANES)),
        ],
        axis=1,
    )
    summed = sum_shifted(partial, lambda parts: functools.reduce(jnp.add, parts))
    hand_off(middle, 1, (partial,))
    hand_off(0, 1, (summed,))
    hand_off(0, 0, (summed,))
    raw = summed[:, :-LANES] * lax.rsqrt(summed[:, -LANES:][:, :1] / width + eps_norm)
    raw = raw.reshape(2, requests, -1, head_dim)
    positions = lengths.astype(jnp.float32)[None, :] + jnp.arange(2, dtype=jnp.float32)[:, None]
    query_heads = query_width // head_dim
    key_heads = key_width // head_dim
    rotated = rotate(raw[:, :, : query_heads + key_heads], positions).astype(jnp.bfloat16)
    queries = rotated[:, :, :query_heads].reshape(2, requests, heads_decode, group_size, head_dim)
    fresh_keys = rotated[:, :, query_heads:]
    fresh_values = raw[:, :, query_heads + key_heads :].astype(jnp.bfloat16)

    per_head = 2 * group_size
    own_queries = jnp.transpose(queries, (1, 2, 0, 3, 4)).reshape(
        requests, heads_decode * per_head, head_dim
    )
    all_queries = lax.all_gather(own_queries, "sub", axis=1, tiled=True)
    shard_index = ctx_index * sub_count + sub_index
    first_place = jnp.reshape(shard_index * shard_length, (1,)).astype(jnp.int32)
    sums, maxima, totals = attend_shard(
        all_queries, key_cache, value_cache, lengths, first_place, score_factor
    )

    own_rows = heads_decode * per_head

    def pack(core):
        part = lambda x: lax.dynamic_slice_in_dim(x, core * own_rows, own_rows, 1)
        return (part(sums), part(maxima)[:, :, 0], part(totals)[:, :, 0])

    def send_form(sums, maxima, totals):
        return jnp.concatenate(
            [x.reshape(-1, head_dim) for x in (sums, maxima, totals)], axis=0
        )

    count = requests * own_rows
    extra = count // head_dim

    def unpack(packed):
        lead = packed.shape[:-2]
        shape = lead + (requests, own_rows)
        return (
            packed[..., :count, :].reshape(shape + (head_dim,)),
            packed[..., count : count + extra, :].reshape(shape),
            packed[..., count + extra :, :].reshape(shape),
        )

    def merge(sums, maxima, totals):
        largest = jnp.max(maxima, axis=0)
        scale = jnp.exp(maxima - largest)
        return (
            jnp.sum(sums * scale[..., None], axis=0),
            largest,
            jnp.sum(totals * scale, axis=0),
        )

    kept = pack(sub_index)
    for shift in range(1, sub_count):
        pairs = [(i, (i + shift) % sub_count) for i in range(sub_count)]
        sent = send_form(*pack(lax.rem(sub_index + shift, sub_count)))
        other = unpack(lax.ppermute(sent, "sub", pairs))
        kept = merge(*(jnp.stack([a, b]) for a, b in zip(kept, other)))
    stats = send_form(*kept)
    gathered = unpack(sum_shifted(stats, jnp.stack))
    sums, maxima, totals = merge(*gathered)
    queue = [
        (shift, flip)
        for shift in range(1, ctx_count)
        for flip in range(sub_count)
        if shift != middle
    ]
    ahead = [(middle, 0), (middle, 1)]
    hand_off(*queue[0], (stats,))
    for key, earlier in zip(queue[1:], ahead + queue):
        hand_off(*key, (stats, received[earlier]))

    grouped = own_queries.reshape(requests, heads_decode, 2, group_size, head_dim).astype(
        jnp.float32
    )
    keys_wide = jnp.transpose(fresh_keys, (1, 2, 0, 3)).astype(jnp.float32)
    values_wide = jnp.transpose(fresh_values, (1, 2, 0, 3)).astype(jnp.float32)
    fresh_scores = (
        jnp.sum(grouped[:, :, :, :, None, :] * keys_wide[:, :, None, None, :, :], axis=-1)
        * score_factor
    )
    step = jnp.arange(2)
    seen = (step[None, :] <= step[:, None])[None, None, :, None, :]
    fresh_scores = jnp.where(seen, fresh_scores, masked_score)
    shape = (requests, heads_decode, 2, group_size)
    maxima = maxima.reshape(shape)
    largest = jnp.maximum(maxima, jnp.max(fresh_scores, axis=-1))
    old_scale = jnp.exp(maxima - largest)
    fresh_weights = jnp.where(seen, jnp.exp(fresh_scores - largest[..., None]), 0.0)
    denominator = totals.reshape(shape) * old_scale + jnp.sum(fresh_weights, axis=-1)
    numerator = sums.reshape(shape + (head_dim,)) * old_scale[..., None] + jnp.sum(
        lax.reduce_precision(fresh_weights, 8, 7)[..., None]
        * values_wide[:, :, None, None, :, :],
        axis=-2,
    )
    attended = (numerator / denominator[..., None]).astype(jnp.bfloat16)

    attended = take(attended, owner_order, axis=0)
    attended = jnp.transpose(attended, (2, 0, 1, 3, 4)).reshape(2 * requests, query_width)
    branch = jnp.dot(attended, w_out, preferred_element_type=jnp.float32)
    branch = branch.reshape(2, requests, -1)
    row_start = lax.axis_index(("head", "sub")) * rows_local
    parts = lax.all_gather(branch, ("head", "sub"), axis=0)
    parts = lax.dynamic_slice_in_dim(parts, row_start, rows_local, 2)
    own_ids = lax.dynamic_slice_in_dim(owner_order, row_start, rows_local)
    residual = take(tokens, own_ids, axis=1).astype(jnp.float32)
    result = (residual + jnp.sum(parts, axis=0)).astype(jnp.bfloat16)

    moved = ()
    for keys in (
        [(0, 0), (0, 1)] + ahead,
        queue[:-2],
        queue[-2:],
    ):
        moved = assemble(
            [received[key] for key in keys],
            jnp.stack([place_of(*key) for key in keys]).astype(jnp.int32),
            ctx_count * sub_count * device_rows,
            moved,
        )
    moved_keys, moved_values = (x.reshape(1, -1, heads_decode, head_dim) for x in moved)
    return (moved_keys, moved_values, result[0], result[1])


def solution(mesh):
    def whole(*arrays):
        return jax.shard_map(
            functools.partial(local, arrays[6].shape[0]),
            mesh=mesh,
            in_specs=(
                P("groups", ("ctx", "sub"), "head", None),
                P("groups", ("ctx", "sub"), "head", None),
                P("groups"),
                P("groups"),
                P(("groups", "head", "sub"), "ctx"),
                P(("groups", "head", "sub"), "ctx"),
                P("ctx"),
                P("ctx", ("head", "sub")),
                P("ctx", ("head", "sub")),
                P("ctx", ("head", "sub")),
                P(("head", "sub"), "ctx"),
            ),
            out_specs=(
                P(("groups", "ctx"), None, ("head", "sub"), None),
                P(("groups", "ctx"), None, ("head", "sub"), None),
                P(("groups", "head", "sub"), "ctx"),
                P(("groups", "head", "sub"), "ctx"),
            ),
            check_vma=False,
        )(*arrays)

    return whole
```

```python
import functools

import jax
import jax.numpy as jnp
from jax import lax
from jax.experimental import pallas as pl
from jax.experimental.pallas import tpu as pltpu
from jax.sharding import PartitionSpec as P

theta_base = 500000.0
eps_norm = 1e-05
masked_score = -1e30
LANES = 128
VMEM_BYTES = 48 * 1024 * 1024


def rotate(vectors, positions):
    half_dim = vectors.shape[-1] // 2
    exponents = jnp.arange(half_dim, dtype=jnp.float32) * (2.0 / vectors.shape[-1])
    frequency = theta_base ** (-exponents)
    angles = positions[..., None, None] * frequency
    cosines = jnp.cos(angles)
    sines = jnp.sin(angles)
    lower_part = vectors[..., :half_dim]
    upper_part = vectors[..., half_dim:]
    return jnp.concatenate(
        [lower_part * cosines - upper_part * sines, upper_part * cosines + lower_part * sines],
        axis=-1,
    )


def in_hbm(x):
    return pltpu.with_memory_space_constraint(x, pltpu.HBM)


def arrange(caches, owner_order, shift, flip, after):
    _, shard_length, heads, head_dim = caches[0].shape
    ctx_count = lax.axis_size("ctx")
    core_count = lax.axis_size("sub")
    heads_decode = heads // core_count
    steps = 4
    places = shard_length // steps
    count = len(caches)
    pieces = [(w, i) for i in range(steps) for w in range(count)]

    def kernel(order_ref, *refs):
        request = order_ref[lax.rem(lax.axis_index("ctx") + shift, ctx_count)]
        core = lax.rem(lax.axis_index("sub") + flip, core_count)
        in_refs = refs[:count]
        out_ref, taken, made, in_sems, out_sems = refs[count + len(after) :]
        rows = lambda i: pl.ds(i * places, places)
        into = [
            pltpu.make_async_copy(
                in_refs[w].at[request, rows(i)], taken.at[w, rows(i)], in_sems.at[w, i]
            )
            for w, i in pieces
        ]
        out_of = [
            pltpu.make_async_copy(
                made.at[w, rows(i)], out_ref.at[w, rows(i)], out_sems.at[w, i]
            )
            for w, i in pieces
        ]
        for copy in into:
            copy.start()
        for p, (w, i) in enumerate(pieces):
            into[p].wait()
            for own in range(core_count):

                @pl.when(core == own)
                def _():
                    low = own * heads_decode
                    made[w, rows(i)] = taken[w, rows(i), low : low + heads_decode, :]

            out_of[p].start()
        for copy in out_of:
            copy.wait()

    blocks = pl.pallas_call(
        kernel,
        out_shape=pltpu.HBM((count, shard_length, heads_decode, head_dim), caches[0].dtype),
        in_specs=[pl.BlockSpec(memory_space=pltpu.SMEM)]
        + [pl.BlockSpec(memory_space=pltpu.HBM)] * count
        + [pl.BlockSpec(memory_space=pl.ANY)] * len(after),
        out_specs=pl.BlockSpec(memory_space=pltpu.HBM),
        scratch_shapes=[
            pltpu.VMEM((count, shard_length, heads, head_dim), caches[0].dtype),
            pltpu.VMEM((count, shard_length, heads_decode, head_dim), caches[0].dtype),
            pltpu.SemaphoreType.DMA((count, steps)),
            pltpu.SemaphoreType.DMA((count, steps)),
        ],
        compiler_params=pltpu.CompilerParams(vmem_limit_bytes=VMEM_BYTES),
        cost_estimate=pl.CostEstimate(
            flops=0,
            transcendentals=0,
            bytes_accessed=3 * count * shard_length * heads * head_dim,
        ),
        name="arrange",
    )(owner_order, *(in_hbm(x) for x in caches), *after)
    return blocks.reshape(count, shard_length * heads_decode, head_dim)


def assemble(blocks, keys, filled=()):
    ctx_count = lax.axis_size("ctx")
    core_count = lax.axis_size("sub")
    arrays, block_rows, head_dim = blocks[0].shape
    count = len(blocks)
    rows = ctx_count * core_count * block_rows
    pieces = [(i, w) for i in range(count) for w in range(arrays)]

    def kernel(*refs):
        ctx = lax.axis_index("ctx")
        core = lax.axis_index("sub")
        places = [
            (
                lax.rem(ctx + (ctx_count - shift), ctx_count) * core_count
                + lax.rem(core + (core_count - flip), core_count)
            )
            * block_rows
            for shift, flip in keys
        ]
        in_refs = refs[:count]
        out_refs = refs[count + len(filled) :][:arrays]
        held, in_sems, out_sems = refs[count + len(filled) + arrays :]
        into = [
            pltpu.make_async_copy(in_refs[i].at[w], held.at[i, w], in_sems.at[i, w])
            for i, w in pieces
        ]
        out_of = [
            pltpu.make_async_copy(
                held.at[i, w],
                out_refs[w].at[pl.ds(pl.multiple_of(places[i], block_rows), block_rows)],
                out_sems.at[i, w],
            )
            for i, w in pieces
        ]
        for copy in into:
            copy.start()
        for p in range(len(pieces)):
            into[p].wait()
            out_of[p].start()
        for copy in out_of:
            copy.wait()

    return pl.pallas_call(
        kernel,
        out_shape=(pltpu.HBM((rows, head_dim), blocks[0].dtype),) * arrays,
        in_specs=[pl.BlockSpec(memory_space=pl.ANY)] * count
        + [pl.BlockSpec(memory_space=pltpu.HBM)] * len(filled),
        out_specs=(pl.BlockSpec(memory_space=pltpu.HBM),) * arrays,
        scratch_shapes=[
            pltpu.VMEM((count, arrays, block_rows, head_dim), blocks[0].dtype),
            pltpu.SemaphoreType.DMA((count, arrays)),
            pltpu.SemaphoreType.DMA((count, arrays)),
        ],
        input_output_aliases={count + w: w for w in range(len(filled))},
        compiler_params=pltpu.CompilerParams(vmem_limit_bytes=VMEM_BYTES),
        cost_estimate=pl.CostEstimate(
            flops=0,
            transcendentals=0,
            bytes_accessed=4 * count * arrays * block_rows * head_dim,
        ),
        name="assemble",
    )(*blocks, *filled)


def pair_tokens(first, second, after):
    def kernel(first_ref, second_ref, after_ref, out_ref):
        out_ref[:, 0] = first_ref[...]
        out_ref[:, 1] = second_ref[...]

    whole = pl.BlockSpec(memory_space=pltpu.VMEM)
    return pl.pallas_call(
        kernel,
        out_shape=jax.ShapeDtypeStruct((first.shape[0], 2, first.shape[1]), first.dtype),
        in_specs=[whole, whole, pl.BlockSpec(memory_space=pl.ANY)],
        out_specs=whole,
        name="pair_tokens",
    )(first, second, in_hbm(after))


def attend_shard(queries, keys, values, lengths, score_factor, after):
    requests, shard_length, heads, head_dim = keys.shape
    rows = queries.shape[1]
    per_head = rows // heads
    columns = shard_length * heads
    flat_keys = keys.reshape(requests, columns, head_dim)
    flat_values = values.reshape(requests, columns, head_dim)

    core_count = lax.axis_size("sub")

    def kernel(lengths_ref, q_ref, k_ref, v_ref, *refs):
        acc_ref, max_ref, sum_ref = refs[len(after) :]
        request = pl.program_id(0)
        shard = lax.axis_index("ctx") * core_count + lax.axis_index("sub")
        scores = (
            lax.dot_general(
                q_ref[0], k_ref[0], (((1,), (1,)), ((), ())), preferred_element_type=jnp.float32
            )
            * score_factor
        )
        row = lax.broadcasted_iota(jnp.int32, (rows, columns), 0)
        column = lax.broadcasted_iota(jnp.int32, (rows, columns), 1)
        live_columns = (lengths_ref[request] - shard * shard_length) * heads
        live = (lax.rem(column, heads) == lax.div(row, per_head)) & (column < live_columns)
        scores = jnp.where(live, scores, masked_score)
        row_max = jnp.max(scores, axis=1, keepdims=True)
        weights = jnp.where(live, jnp.exp(scores - row_max), 0.0)
        acc_ref[0] = jnp.dot(
            weights.astype(jnp.bfloat16), v_ref[0], preferred_element_type=jnp.float32
        )
        max_ref[0] = jnp.broadcast_to(row_max, (rows, head_dim))
        sum_ref[0] = jnp.broadcast_to(
            jnp.sum(weights, axis=1, keepdims=True), (rows, head_dim)
        )

    small = pl.BlockSpec((1, rows, head_dim), lambda r, *_: (r, 0, 0))
    large = pl.BlockSpec((1, columns, head_dim), lambda r, *_: (r, 0, 0))
    result = jax.ShapeDtypeStruct((requests, rows, head_dim), jnp.float32)
    return pl.pallas_call(
        kernel,
        out_shape=(result, result, result),
        grid_spec=pltpu.PrefetchScalarGridSpec(
            num_scalar_prefetch=1,
            grid=(requests,),
            in_specs=[small, large, large]
            + [pl.BlockSpec(memory_space=pl.ANY)] * len(after),
            out_specs=(small, small, small),
        ),
        compiler_params=pltpu.CompilerParams(vmem_limit_bytes=VMEM_BYTES),
        cost_estimate=pl.CostEstimate(
            flops=4 * requests * rows * columns * head_dim,
            transcendentals=requests * rows * columns,
            bytes_accessed=4 * keys.size,
        ),
        name="attend_shard",
    )(lengths, queries, in_hbm(flat_keys), in_hbm(flat_values), *after)


def local(
    width,
    key_cache,
    value_cache,
    lengths,
    owner_order,
    first_tokens,
    second_tokens,
    norm_gain,
    w_query,
    w_key,
    w_value,
    w_out,
):
    ctx_count = lax.axis_size("ctx")
    sub_count = lax.axis_size("sub")
    requests, shard_length, heads, head_dim = key_cache.shape
    assert requests == ctx_count and sub_count == 2
    heads_decode = heads // sub_count
    sub_index = lax.axis_index("sub")
    take = functools.partial(jnp.take, mode="clip")

    received = {}

    def hand_off(shift, flip, after=()):
        block = made = arrange((key_cache, value_cache), owner_order, shift, flip, after)
        if shift or flip:
            pairs = [
                (
                    c * sub_count + s,
                    (c + shift) % ctx_count * sub_count + (s + flip) % sub_count,
                )
                for c in range(ctx_count)
                for s in range(sub_count)
            ]
            block = lax.ppermute(made, ("ctx", "sub"), pairs)
        received[shift, flip] = block
        return made

    def sum_shifted(values, combine):
        return combine(
            [values]
            + [
                lax.ppermute(
                    values, "ctx", [(c, (c + shift) % ctx_count) for c in range(ctx_count)]
                )
                for shift in range(1, ctx_count)
            ]
        )

    middle = ctx_count // 2
    leading = hand_off(middle, 0)

    query_width = w_query.shape[1]
    key_width = w_key.shape[1]
    group_size = query_width // head_dim // heads_decode
    score_factor = head_dim ** (-0.5)
    rows_local = first_tokens.shape[0]
    tokens = lax.all_gather(
        pair_tokens(first_tokens, second_tokens, leading), ("head", "sub"), axis=0, tiled=True
    )
    wide = tokens.astype(jnp.float32).reshape(2 * requests, -1)
    gained = wide * norm_gain.astype(jnp.float32)
    upper = lax.reduce_precision(gained, 8, 7)
    lower = gained - upper
    halves = jnp.concatenate([upper, lower]).astype(jnp.bfloat16)
    products = jnp.concatenate(
        [
            jnp.dot(halves, weight, preferred_element_type=jnp.float32)
            for weight in (w_query, w_key, w_value)
        ],
        axis=1,
    )
    squares = jnp.sum(wide * wide, axis=1, keepdims=True)
    partial = jnp.concatenate(
        [
            products[: 2 * requests] + products[2 * requests :],
            jnp.broadcast_to(squares, (2 * requests, LANES)),
        ],
        axis=1,
    )
    summed = sum_shifted(partial, lambda parts: functools.reduce(jnp.add, parts))
    hand_off(middle, 1, (partial,))
    hand_off(0, 0, (summed,))
    raw = summed[:, :-LANES] * lax.rsqrt(summed[:, -LANES:][:, :1] / width + eps_norm)
    raw = raw.reshape(requests, 2, -1, head_dim)
    positions = lengths.astype(jnp.float32)[:, None] + jnp.arange(2, dtype=jnp.float32)
    query_heads = query_width // head_dim
    key_heads = key_width // head_dim
    rotated = rotate(raw[:, :, : query_heads + key_heads], positions).astype(jnp.bfloat16)
    queries = rotated[:, :, :query_heads].reshape(requests, 2, heads_decode, group_size, head_dim)
    fresh_keys = rotated[:, :, query_heads:]
    fresh_values = raw[:, :, query_heads + key_heads :].astype(jnp.bfloat16)

    per_head = 2 * group_size
    own_queries = jnp.transpose(queries, (0, 2, 1, 3, 4)).reshape(
        requests, heads_decode * per_head, head_dim
    )
    all_queries = lax.all_gather(own_queries, "sub", axis=1, tiled=True)
    sums, maxima, totals = attend_shard(
        all_queries,
        key_cache,
        value_cache,
        lengths,
        score_factor,
        (received[middle, 0],),
    )

    own_rows = heads_decode * per_head

    def pack(core):
        part = lambda x: lax.dynamic_slice_in_dim(x, core * own_rows, own_rows, 1)
        return (part(sums), part(maxima)[:, :, 0], part(totals)[:, :, 0])

    def send_form(sums, maxima, totals):
        return jnp.concatenate(
            [x.reshape(-1, head_dim) for x in (sums, maxima, totals)], axis=0
        )

    count = requests * own_rows
    extra = count // head_dim

    def unpack(packed):
        lead = packed.shape[:-2]
        shape = lead + (requests, own_rows)
        return (
            packed[..., :count, :].reshape(shape + (head_dim,)),
            packed[..., count : count + extra, :].reshape(shape),
            packed[..., count + extra :, :].reshape(shape),
        )

    def merge(sums, maxima, totals):
        largest = jnp.max(maxima, axis=0)
        scale = jnp.exp(maxima - largest)
        return (
            jnp.sum(sums * scale[..., None], axis=0),
            largest,
            jnp.sum(totals * scale, axis=0),
        )

    kept = pack(sub_index)
    for shift in range(1, sub_count):
        pairs = [(i, (i + shift) % sub_count) for i in range(sub_count)]
        sent = send_form(*pack(lax.rem(sub_index + shift, sub_count)))
        other = unpack(lax.ppermute(sent, "sub", pairs))
        kept = merge(*(jnp.stack([a, b]) for a, b in zip(kept, other)))
    stats = send_form(*kept)
    gathered = unpack(sum_shifted(stats, jnp.stack))
    sums, maxima, totals = merge(*gathered)
    queue = [
        (shift, flip)
        for shift in range(1, ctx_count)
        for flip in range(sub_count)
        if shift != middle
    ]
    ahead = [(middle, 0), (middle, 1)]
    hand_off(*queue[0], (stats,))
    for key, earlier in zip(queue[1:], ahead + queue):
        hand_off(*key, (stats, received[earlier]))
    hand_off(0, 1, (stats, received[middle, 1]))

    grouped = own_queries.reshape(requests, heads_decode, 2, group_size, head_dim).astype(
        jnp.float32
    )
    keys_wide = jnp.transpose(fresh_keys, (0, 2, 1, 3)).astype(jnp.float32)
    values_wide = jnp.transpose(fresh_values, (0, 2, 1, 3)).astype(jnp.float32)
    fresh_scores = (
        jnp.sum(grouped[:, :, :, :, None, :] * keys_wide[:, :, None, None, :, :], axis=-1)
        * score_factor
    )
    step = jnp.arange(2)
    seen = (step[None, :] <= step[:, None])[None, None, :, None, :]
    fresh_scores = jnp.where(seen, fresh_scores, masked_score)
    shape = (requests, heads_decode, 2, group_size)
    maxima = maxima.reshape(shape)
    largest = jnp.maximum(maxima, jnp.max(fresh_scores, axis=-1))
    old_scale = jnp.exp(maxima - largest)
    fresh_weights = jnp.where(seen, jnp.exp(fresh_scores - largest[..., None]), 0.0)
    denominator = totals.reshape(shape) * old_scale + jnp.sum(fresh_weights, axis=-1)
    numerator = sums.reshape(shape + (head_dim,)) * old_scale[..., None] + jnp.sum(
        lax.reduce_precision(fresh_weights, 8, 7)[..., None]
        * values_wide[:, :, None, None, :, :],
        axis=-2,
    )
    attended = (numerator / denominator[..., None]).astype(jnp.bfloat16)

    attended = take(attended, owner_order, axis=0)
    attended = jnp.transpose(attended, (0, 2, 1, 3, 4)).reshape(2 * requests, query_width)
    branch = jnp.dot(attended, w_out, preferred_element_type=jnp.float32)
    branch = branch.reshape(requests, 2, -1)
    row_start = lax.axis_index(("head", "sub")) * rows_local
    parts = lax.all_gather(branch, ("head", "sub"), axis=0)
    parts = lax.dynamic_slice_in_dim(parts, row_start, rows_local, 1)
    own_ids = lax.dynamic_slice_in_dim(owner_order, row_start, rows_local)
    residual = take(tokens, own_ids, axis=0).astype(jnp.float32)
    result = (residual + jnp.sum(parts, axis=0)).astype(jnp.bfloat16)

    moved = ()
    for keys in (
        [(0, 0), (0, 1)] + ahead,
        queue[:-2],
        queue[-2:],
    ):
        moved = assemble(
            [received[key] for key in keys],
            keys,
            moved,
        )
    moved_keys, moved_values = (x.reshape(1, -1, heads_decode, head_dim) for x in moved)
    return (moved_keys, moved_values, result[:, 0], result[:, 1])


def solution(mesh):
    def whole(*arrays):
        return jax.shard_map(
            functools.partial(local, arrays[6].shape[0]),
            mesh=mesh,
            in_specs=(
                P("groups", ("ctx", "sub"), "head", None),
                P("groups", ("ctx", "sub"), "head", None),
                P("groups"),
                P("groups"),
                P(("groups", "head", "sub"), "ctx"),
                P(("groups", "head", "sub"), "ctx"),
                P("ctx"),
                P("ctx", ("head", "sub")),
                P("ctx", ("head", "sub")),
                P("ctx", ("head", "sub")),
                P(("head", "sub"), "ctx"),
            ),
            out_specs=(
                P(("groups", "ctx"), None, ("head", "sub"), None),
                P(("groups", "ctx"), None, ("head", "sub"), None),
                P(("groups", "head", "sub"), "ctx"),
                P(("groups", "head", "sub"), "ctx"),
            ),
            check_vma=False,
        )(*arrays)

    return whole
```

```python
import functools

import jax
import jax.numpy as jnp
from jax import lax
from jax.experimental import pallas as pl
from jax.experimental.pallas import tpu as pltpu
from jax.sharding import PartitionSpec as P

theta_base = 500000.0
eps_norm = 1e-05
masked_score = -1e30
LANES = 128
VMEM_BYTES = 48 * 1024 * 1024


def rotate(vectors, positions):
    half_dim = vectors.shape[-1] // 2
    exponents = jnp.arange(half_dim, dtype=jnp.float32) * (2.0 / vectors.shape[-1])
    frequency = theta_base ** (-exponents)
    angles = positions[..., None, None] * frequency
    cosines = jnp.cos(angles)
    sines = jnp.sin(angles)
    lower_part = vectors[..., :half_dim]
    upper_part = vectors[..., half_dim:]
    return jnp.concatenate(
        [lower_part * cosines - upper_part * sines, upper_part * cosines + lower_part * sines],
        axis=-1,
    )


def in_hbm(x):
    return pltpu.with_memory_space_constraint(x, pltpu.HBM)


def arrange(caches, owner_order, shift, flip, after):
    _, shard_length, heads, head_dim = caches[0].shape
    ctx_count = lax.axis_size("ctx")
    core_count = lax.axis_size("sub")
    heads_decode = heads // core_count
    steps = 4
    places = shard_length // steps
    count = len(caches)
    pieces = [(w, i) for i in range(steps) for w in range(count)]

    def kernel(order_ref, *refs):
        request = order_ref[lax.rem(lax.axis_index("ctx") + shift, ctx_count)]
        core = lax.rem(lax.axis_index("sub") + flip, core_count)
        in_refs = refs[:count]
        out_ref, taken, made, in_sems, out_sems = refs[count + len(after) :]
        rows = lambda i: pl.ds(i * places, places)
        into = [
            pltpu.make_async_copy(
                in_refs[w].at[request, rows(i)], taken.at[w, rows(i)], in_sems.at[w, i]
            )
            for w, i in pieces
        ]
        out_of = [
            pltpu.make_async_copy(
                made.at[w, rows(i)], out_ref.at[w, rows(i)], out_sems.at[w, i]
            )
            for w, i in pieces
        ]
        for copy in into:
            copy.start()
        for p, (w, i) in enumerate(pieces):
            into[p].wait()
            for own in range(core_count):

                @pl.when(core == own)
                def _():
                    low = own * heads_decode
                    made[w, rows(i)] = taken[w, rows(i), low : low + heads_decode, :]

            out_of[p].start()
        for copy in out_of:
            copy.wait()

    blocks = pl.pallas_call(
        kernel,
        out_shape=pltpu.HBM((count, shard_length, heads_decode, head_dim), caches[0].dtype),
        in_specs=[pl.BlockSpec(memory_space=pltpu.SMEM)]
        + [pl.BlockSpec(memory_space=pltpu.HBM)] * count
        + [pl.BlockSpec(memory_space=pl.ANY)] * len(after),
        out_specs=pl.BlockSpec(memory_space=pltpu.HBM),
        scratch_shapes=[
            pltpu.VMEM((count, shard_length, heads, head_dim), caches[0].dtype),
            pltpu.VMEM((count, shard_length, heads_decode, head_dim), caches[0].dtype),
            pltpu.SemaphoreType.DMA((count, steps)),
            pltpu.SemaphoreType.DMA((count, steps)),
        ],
        compiler_params=pltpu.CompilerParams(vmem_limit_bytes=VMEM_BYTES),
        cost_estimate=pl.CostEstimate(
            flops=0,
            transcendentals=0,
            bytes_accessed=3 * count * shard_length * heads * head_dim,
        ),
        name="arrange",
    )(owner_order, *(in_hbm(x) for x in caches), *after)
    return blocks.reshape(count, shard_length * heads_decode, head_dim)


def assemble(blocks, pieces, filled=()):
    ctx_count = lax.axis_size("ctx")
    core_count = lax.axis_size("sub")
    _, block_rows, head_dim = blocks[0].shape
    rows = ctx_count * core_count * block_rows
    arrays = 2
    count = len(blocks)
    total = len(pieces)

    def kernel(*refs):
        ctx = lax.axis_index("ctx")
        core = lax.axis_index("sub")
        in_refs = refs[:count]
        out_refs = refs[count + len(filled) :][:arrays]
        held, in_sems, out_sems = refs[count + len(filled) + arrays :]
        into, out_of = [], []
        for p, (block, entry, output, shift, flip) in enumerate(pieces):
            source = lax.rem(ctx + (ctx_count - shift), ctx_count) * core_count + lax.rem(
                core + (core_count - flip), core_count
            )
            place = pl.ds(pl.multiple_of(source * block_rows, block_rows), block_rows)
            into.append(
                pltpu.make_async_copy(in_refs[block].at[entry], held.at[p], in_sems.at[p])
            )
            out_of.append(
                pltpu.make_async_copy(held.at[p], out_refs[output].at[place], out_sems.at[p])
            )
        for copy in into:
            copy.start()
        for p in range(total):
            into[p].wait()
            out_of[p].start()
        for copy in out_of:
            copy.wait()

    return pl.pallas_call(
        kernel,
        out_shape=(pltpu.HBM((rows, head_dim), blocks[0].dtype),) * arrays,
        in_specs=[pl.BlockSpec(memory_space=pl.ANY)] * count
        + [pl.BlockSpec(memory_space=pltpu.HBM)] * len(filled),
        out_specs=(pl.BlockSpec(memory_space=pltpu.HBM),) * arrays,
        scratch_shapes=[
            pltpu.VMEM((total, block_rows, head_dim), blocks[0].dtype),
            pltpu.SemaphoreType.DMA((total,)),
            pltpu.SemaphoreType.DMA((total,)),
        ],
        input_output_aliases={count + w: w for w in range(len(filled))},
        compiler_params=pltpu.CompilerParams(vmem_limit_bytes=VMEM_BYTES),
        cost_estimate=pl.CostEstimate(
            flops=0, transcendentals=0, bytes_accessed=4 * total * block_rows * head_dim
        ),
        name="assemble",
    )(*blocks, *filled)


def pair_tokens(first, second, after):
    def kernel(first_ref, second_ref, after_ref, out_ref):
        out_ref[:, 0] = first_ref[...]
        out_ref[:, 1] = second_ref[...]

    whole = pl.BlockSpec(memory_space=pltpu.VMEM)
    return pl.pallas_call(
        kernel,
        out_shape=jax.ShapeDtypeStruct((first.shape[0], 2, first.shape[1]), first.dtype),
        in_specs=[whole, whole, pl.BlockSpec(memory_space=pl.ANY)],
        out_specs=whole,
        name="pair_tokens",
    )(first, second, in_hbm(after))


def pack_products(products, wide, after):
    rows = wide.shape[0]
    widths = [x.shape[1] for x in products]

    def kernel(*refs):
        wide_ref, out_ref = refs[len(products)], refs[-1]
        low = 0
        for ref, columns in zip(refs, widths):
            out_ref[:, low : low + columns] = ref[:rows] + ref[rows:]
            low += columns
        squares = jnp.sum(wide_ref[...] * wide_ref[...], axis=1, keepdims=True)
        out_ref[:, low:] = jnp.broadcast_to(squares, (rows, LANES))

    whole = pl.BlockSpec(memory_space=pltpu.VMEM)
    return pl.pallas_call(
        kernel,
        out_shape=jax.ShapeDtypeStruct((rows, sum(widths) + LANES), jnp.float32),
        in_specs=[whole] * (len(products) + 1) + [pl.BlockSpec(memory_space=pl.ANY)] * len(after),
        out_specs=whole,
        name="pack_products",
    )(*products, wide, *after)


def attend_shard(queries, keys, values, lengths, score_factor, after):
    requests, shard_length, heads, head_dim = keys.shape
    rows = queries.shape[1]
    per_head = rows // heads
    columns = shard_length * heads
    flat_keys = keys.reshape(requests, columns, head_dim)
    flat_values = values.reshape(requests, columns, head_dim)

    core_count = lax.axis_size("sub")

    def kernel(lengths_ref, q_ref, k_ref, v_ref, *refs):
        acc_ref, max_ref, sum_ref = refs[len(after) :]
        request = pl.program_id(0)
        shard = lax.axis_index("ctx") * core_count + lax.axis_index("sub")
        scores = (
            lax.dot_general(
                q_ref[0], k_ref[0], (((1,), (1,)), ((), ())), preferred_element_type=jnp.float32
            )
            * score_factor
        )
        row = lax.broadcasted_iota(jnp.int32, (rows, columns), 0)
        column = lax.broadcasted_iota(jnp.int32, (rows, columns), 1)
        live_columns = (lengths_ref[request] - shard * shard_length) * heads
        live = (lax.rem(column, heads) == lax.div(row, per_head)) & (column < live_columns)
        scores = jnp.where(live, scores, masked_score)
        row_max = jnp.max(scores, axis=1, keepdims=True)
        weights = jnp.where(live, jnp.exp(scores - row_max), 0.0)
        acc_ref[0] = jnp.dot(
            weights.astype(jnp.bfloat16), v_ref[0], preferred_element_type=jnp.float32
        )
        max_ref[0] = jnp.broadcast_to(row_max, (rows, head_dim))
        sum_ref[0] = jnp.broadcast_to(
            jnp.sum(weights, axis=1, keepdims=True), (rows, head_dim)
        )

    small = pl.BlockSpec((1, rows, head_dim), lambda r, *_: (r, 0, 0))
    large = pl.BlockSpec((1, columns, head_dim), lambda r, *_: (r, 0, 0))
    result = jax.ShapeDtypeStruct((requests, rows, head_dim), jnp.float32)
    return pl.pallas_call(
        kernel,
        out_shape=(result, result, result),
        grid_spec=pltpu.PrefetchScalarGridSpec(
            num_scalar_prefetch=1,
            grid=(requests,),
            in_specs=[small, large, large]
            + [pl.BlockSpec(memory_space=pl.ANY)] * len(after),
            out_specs=(small, small, small),
        ),
        compiler_params=pltpu.CompilerParams(vmem_limit_bytes=VMEM_BYTES),
        cost_estimate=pl.CostEstimate(
            flops=4 * requests * rows * columns * head_dim,
            transcendentals=requests * rows * columns,
            bytes_accessed=4 * keys.size,
        ),
        name="attend_shard",
    )(lengths, queries, in_hbm(flat_keys), in_hbm(flat_values), *after)


def local(
    width,
    key_cache,
    value_cache,
    lengths,
    owner_order,
    first_tokens,
    second_tokens,
    norm_gain,
    w_query,
    w_key,
    w_value,
    w_out,
):
    ctx_count = lax.axis_size("ctx")
    sub_count = lax.axis_size("sub")
    requests, shard_length, heads, head_dim = key_cache.shape
    assert requests == ctx_count and sub_count == 2
    heads_decode = heads // sub_count
    sub_index = lax.axis_index("sub")
    take = functools.partial(jnp.take, mode="clip")

    both = (0, 1)
    received = {}

    def hand_off(which, shift, flip, after=()):
        caches = [(key_cache, value_cache)[w] for w in which]
        block = made = arrange(caches, owner_order, shift, flip, after)
        if shift or flip:
            pairs = [
                (
                    c * sub_count + s,
                    (c + shift) % ctx_count * sub_count + (s + flip) % sub_count,
                )
                for c in range(ctx_count)
                for s in range(sub_count)
            ]
            block = lax.ppermute(made, ("ctx", "sub"), pairs)
        received[which, shift, flip] = block
        return made

    def sum_shifted(values, combine):
        return combine(
            [values]
            + [
                lax.ppermute(
                    values, "ctx", [(c, (c + shift) % ctx_count) for c in range(ctx_count)]
                )
                for shift in range(1, ctx_count)
            ]
        )

    middle = ctx_count // 2
    ahead = ((0,), 1, 0)
    leading = hand_off(*ahead)

    query_width = w_query.shape[1]
    key_width = w_key.shape[1]
    group_size = query_width // head_dim // heads_decode
    score_factor = head_dim ** (-0.5)
    rows_local = first_tokens.shape[0]
    tokens = lax.all_gather(
        pair_tokens(first_tokens, second_tokens, leading), ("head", "sub"), axis=0, tiled=True
    )
    wide = tokens.astype(jnp.float32).reshape(2 * requests, -1)
    gained = wide * norm_gain.astype(jnp.float32)
    upper = lax.reduce_precision(gained, 8, 7)
    lower = gained - upper
    halves = jnp.concatenate([upper, lower]).astype(jnp.bfloat16)
    partial = pack_products(
        [
            jnp.dot(halves, weight, preferred_element_type=jnp.float32)
            for weight in (w_query, w_key, w_value)
        ],
        wide,
        (received[ahead],),
    )
    summed = sum_shifted(partial, lambda parts: functools.reduce(jnp.add, parts))
    first = (both, middle, 0)
    second = (both, 1, 1)
    hand_off(*first, (summed,))
    hand_off(*second, (summed,))
    hand_off(both, 0, 0, (summed,))
    raw = summed[:, :-LANES] * lax.rsqrt(summed[:, -LANES:][:, :1] / width + eps_norm)
    raw = raw.reshape(requests, 2, -1, head_dim)
    positions = lengths.astype(jnp.float32)[:, None] + jnp.arange(2, dtype=jnp.float32)
    query_heads = query_width // head_dim
    key_heads = key_width // head_dim
    rotated = rotate(raw[:, :, : query_heads + key_heads], positions).astype(jnp.bfloat16)
    queries = rotated[:, :, :query_heads].reshape(requests, 2, heads_decode, group_size, head_dim)
    fresh_keys = rotated[:, :, query_heads:]
    fresh_values = raw[:, :, query_heads + key_heads :].astype(jnp.bfloat16)

    per_head = 2 * group_size
    own_queries = jnp.transpose(queries, (0, 2, 1, 3, 4)).reshape(
        requests, heads_decode * per_head, head_dim
    )
    all_queries = lax.all_gather(own_queries, "sub", axis=1, tiled=True)
    sums, maxima, totals = attend_shard(
        all_queries,
        key_cache,
        value_cache,
        lengths,
        score_factor,
        (),
    )

    own_rows = heads_decode * per_head

    def pack(core):
        part = lambda x: lax.dynamic_slice_in_dim(x, core * own_rows, own_rows, 1)
        return (part(sums), part(maxima)[:, :, 0], part(totals)[:, :, 0])

    def send_form(sums, maxima, totals):
        return jnp.concatenate(
            [x.reshape(-1, head_dim) for x in (sums, maxima, totals)], axis=0
        )

    count = requests * own_rows
    extra = count // head_dim

    def unpack(packed):
        lead = packed.shape[:-2]
        shape = lead + (requests, own_rows)
        return (
            packed[..., :count, :].reshape(shape + (head_dim,)),
            packed[..., count : count + extra, :].reshape(shape),
            packed[..., count + extra :, :].reshape(shape),
        )

    def merge(sums, maxima, totals):
        largest = jnp.max(maxima, axis=0)
        scale = jnp.exp(maxima - largest)
        return (
            jnp.sum(sums * scale[..., None], axis=0),
            largest,
            jnp.sum(totals * scale, axis=0),
        )

    kept = pack(sub_index)
    for shift in range(1, sub_count):
        pairs = [(i, (i + shift) % sub_count) for i in range(sub_count)]
        sent = send_form(*pack(lax.rem(sub_index + shift, sub_count)))
        other = unpack(lax.ppermute(sent, "sub", pairs))
        kept = merge(*(jnp.stack([a, b]) for a, b in zip(kept, other)))
    stats = send_form(*kept)
    gathered = unpack(sum_shifted(stats, jnp.stack))
    sums, maxima, totals = merge(*gathered)
    third = (both, middle, 1)
    hand_off(*third, (stats, received[second]))
    rest = [
        (both, shift, flip)
        for shift in range(2, ctx_count)
        for flip in range(sub_count)
        if shift != middle
    ] + [((1,), 1, 0)]
    for key in rest:
        hand_off(*key, (stats, received[first]))
    hand_off(both, 0, 1, (stats, received[first]))

    grouped = own_queries.reshape(requests, heads_decode, 2, group_size, head_dim).astype(
        jnp.float32
    )
    keys_wide = jnp.transpose(fresh_keys, (0, 2, 1, 3)).astype(jnp.float32)
    values_wide = jnp.transpose(fresh_values, (0, 2, 1, 3)).astype(jnp.float32)
    fresh_scores = (
        jnp.sum(grouped[:, :, :, :, None, :] * keys_wide[:, :, None, None, :, :], axis=-1)
        * score_factor
    )
    step = jnp.arange(2)
    seen = (step[None, :] <= step[:, None])[None, None, :, None, :]
    fresh_scores = jnp.where(seen, fresh_scores, masked_score)
    shape = (requests, heads_decode, 2, group_size)
    maxima = maxima.reshape(shape)
    largest = jnp.maximum(maxima, jnp.max(fresh_scores, axis=-1))
    old_scale = jnp.exp(maxima - largest)
    fresh_weights = jnp.where(seen, jnp.exp(fresh_scores - largest[..., None]), 0.0)
    denominator = totals.reshape(shape) * old_scale + jnp.sum(fresh_weights, axis=-1)
    numerator = sums.reshape(shape + (head_dim,)) * old_scale[..., None] + jnp.sum(
        lax.reduce_precision(fresh_weights, 8, 7)[..., None]
        * values_wide[:, :, None, None, :, :],
        axis=-2,
    )
    attended = (numerator / denominator[..., None]).astype(jnp.bfloat16)

    attended = take(attended, owner_order, axis=0)
    attended = jnp.transpose(attended, (0, 2, 1, 3, 4)).reshape(2 * requests, query_width)
    branch = jnp.dot(attended, w_out, preferred_element_type=jnp.float32)
    branch = branch.reshape(requests, 2, -1)
    row_start = lax.axis_index(("head", "sub")) * rows_local
    parts = lax.all_gather(branch, ("head", "sub"), axis=0)
    parts = lax.dynamic_slice_in_dim(parts, row_start, rows_local, 1)
    own_ids = lax.dynamic_slice_in_dim(owner_order, row_start, rows_local)
    residual = take(tokens, own_ids, axis=0).astype(jnp.float32)
    result = (residual + jnp.sum(parts, axis=0)).astype(jnp.bfloat16)

    moved = ()
    groups = [[ahead, (both, 0, 0), (both, 0, 1), first, second], [third] + rest]
    for keys in groups:
        pieces = [
            (block, entry, output, shift, flip)
            for block, (which, shift, flip) in enumerate(keys)
            for entry, output in enumerate(which)
        ]
        moved = assemble([received[key] for key in keys], pieces, moved)
    moved_keys, moved_values = (x.reshape(1, -1, heads_decode, head_dim) for x in moved)
    return (moved_keys, moved_values, result[:, 0], result[:, 1])


def solution(mesh):
    def whole(*arrays):
        return jax.shard_map(
            functools.partial(local, arrays[6].shape[0]),
            mesh=mesh,
            in_specs=(
                P("groups", ("ctx", "sub"), "head", None),
                P("groups", ("ctx", "sub"), "head", None),
                P("groups"),
                P("groups"),
                P(("groups", "head", "sub"), "ctx"),
                P(("groups", "head", "sub"), "ctx"),
                P("ctx"),
                P("ctx", ("head", "sub")),
                P("ctx", ("head", "sub")),
                P("ctx", ("head", "sub")),
                P(("head", "sub"), "ctx"),
            ),
            out_specs=(
                P(("groups", "ctx"), None, ("head", "sub"), None),
                P(("groups", "ctx"), None, ("head", "sub"), None),
                P(("groups", "head", "sub"), "ctx"),
                P(("groups", "head", "sub"), "ctx"),
            ),
            check_vma=False,
        )(*arrays)

    return whole
```

```python
import functools

import jax
import jax.numpy as jnp
from jax import lax
from jax.experimental import pallas as pl
from jax.experimental.pallas import tpu as pltpu
from jax.sharding import PartitionSpec as P

theta_base = 500000.0
eps_norm = 1e-05
masked_score = -1e30
LANES = 128
VMEM_BYTES = 48 * 1024 * 1024


def rotate(vectors, positions):
    half_dim = vectors.shape[-1] // 2
    exponents = jnp.arange(half_dim, dtype=jnp.float32) * (2.0 / vectors.shape[-1])
    frequency = theta_base ** (-exponents)
    angles = positions[..., None, None] * frequency
    cosines = jnp.cos(angles)
    sines = jnp.sin(angles)
    lower_part = vectors[..., :half_dim]
    upper_part = vectors[..., half_dim:]
    return jnp.concatenate(
        [lower_part * cosines - upper_part * sines, upper_part * cosines + lower_part * sines],
        axis=-1,
    )


def in_hbm(x):
    return pltpu.with_memory_space_constraint(x, pltpu.HBM)


def arrange(caches, owner_order, shift, flip, after):
    _, shard_length, heads, head_dim = caches[0].shape
    ctx_count = lax.axis_size("ctx")
    core_count = lax.axis_size("sub")
    heads_decode = heads // core_count
    steps = 4
    places = shard_length // steps
    count = len(caches)
    pieces = [(w, i) for i in range(steps) for w in range(count)]

    def kernel(order_ref, *refs):
        request = order_ref[lax.rem(lax.axis_index("ctx") + shift, ctx_count)]
        core = lax.rem(lax.axis_index("sub") + flip, core_count)
        in_refs = refs[:count]
        out_ref, taken, made, in_sems, out_sems = refs[count + len(after) :]
        rows = lambda i: pl.ds(i * places, places)
        into = [
            pltpu.make_async_copy(
                in_refs[w].at[request, rows(i)], taken.at[w, rows(i)], in_sems.at[w, i]
            )
            for w, i in pieces
        ]
        out_of = [
            pltpu.make_async_copy(
                made.at[w, rows(i)], out_ref.at[w, rows(i)], out_sems.at[w, i]
            )
            for w, i in pieces
        ]
        for copy in into:
            copy.start()
        for p, (w, i) in enumerate(pieces):
            into[p].wait()
            for own in range(core_count):

                @pl.when(core == own)
                def _():
                    low = own * heads_decode
                    made[w, rows(i)] = taken[w, rows(i), low : low + heads_decode, :]

            out_of[p].start()
        for copy in out_of:
            copy.wait()

    blocks = pl.pallas_call(
        kernel,
        out_shape=pltpu.HBM((count, shard_length, heads_decode, head_dim), caches[0].dtype),
        in_specs=[pl.BlockSpec(memory_space=pltpu.SMEM)]
        + [pl.BlockSpec(memory_space=pltpu.HBM)] * count
        + [pl.BlockSpec(memory_space=pl.ANY)] * len(after),
        out_specs=pl.BlockSpec(memory_space=pltpu.HBM),
        scratch_shapes=[
            pltpu.VMEM((count, shard_length, heads, head_dim), caches[0].dtype),
            pltpu.VMEM((count, shard_length, heads_decode, head_dim), caches[0].dtype),
            pltpu.SemaphoreType.DMA((count, steps)),
            pltpu.SemaphoreType.DMA((count, steps)),
        ],
        compiler_params=pltpu.CompilerParams(vmem_limit_bytes=VMEM_BYTES),
        name="arrange",
    )(owner_order, *(in_hbm(x) for x in caches), *after)
    return blocks.reshape(count, shard_length * heads_decode, head_dim)


def assemble(blocks, pieces, filled=()):
    ctx_count = lax.axis_size("ctx")
    core_count = lax.axis_size("sub")
    _, block_rows, head_dim = blocks[0].shape
    rows = ctx_count * core_count * block_rows
    arrays = 2
    count = len(blocks)
    total = len(pieces)

    def kernel(*refs):
        ctx = lax.axis_index("ctx")
        core = lax.axis_index("sub")
        in_refs = refs[:count]
        out_refs = refs[count + len(filled) :][:arrays]
        held, in_sems, out_sems = refs[count + len(filled) + arrays :]
        into, out_of = [], []
        for p, (block, entry, output, shift, flip) in enumerate(pieces):
            source = lax.rem(ctx + (ctx_count - shift), ctx_count) * core_count + lax.rem(
                core + (core_count - flip), core_count
            )
            place = pl.ds(pl.multiple_of(source * block_rows, block_rows), block_rows)
            into.append(
                pltpu.make_async_copy(in_refs[block].at[entry], held.at[p], in_sems.at[p])
            )
            out_of.append(
                pltpu.make_async_copy(held.at[p], out_refs[output].at[place], out_sems.at[p])
            )
        for copy in into:
            copy.start()
        for p in range(total):
            into[p].wait()
            out_of[p].start()
        for copy in out_of:
            copy.wait()

    return pl.pallas_call(
        kernel,
        out_shape=(pltpu.HBM((rows, head_dim), blocks[0].dtype),) * arrays,
        in_specs=[pl.BlockSpec(memory_space=pl.ANY)] * count
        + [pl.BlockSpec(memory_space=pltpu.HBM)] * len(filled),
        out_specs=(pl.BlockSpec(memory_space=pltpu.HBM),) * arrays,
        scratch_shapes=[
            pltpu.VMEM((total, block_rows, head_dim), blocks[0].dtype),
            pltpu.SemaphoreType.DMA((total,)),
            pltpu.SemaphoreType.DMA((total,)),
        ],
        input_output_aliases={count + w: w for w in range(len(filled))},
        compiler_params=pltpu.CompilerParams(vmem_limit_bytes=VMEM_BYTES),
        cost_estimate=pl.CostEstimate(
            flops=0, transcendentals=0, bytes_accessed=4 * total * block_rows * head_dim
        ),
        name="assemble",
    )(*blocks, *filled)


def pair_tokens(first, second, after):
    def kernel(first_ref, second_ref, after_ref, out_ref):
        out_ref[:, 0] = first_ref[...]
        out_ref[:, 1] = second_ref[...]

    whole = pl.BlockSpec(memory_space=pltpu.VMEM)
    return pl.pallas_call(
        kernel,
        out_shape=jax.ShapeDtypeStruct((first.shape[0], 2, first.shape[1]), first.dtype),
        in_specs=[whole, whole, pl.BlockSpec(memory_space=pl.ANY)],
        out_specs=whole,
        name="pair_tokens",
    )(first, second, in_hbm(after))


def pack_products(products, wide, after):
    rows = wide.shape[0]
    widths = [x.shape[1] for x in products]

    def kernel(*refs):
        wide_ref, out_ref = refs[len(products)], refs[-1]
        low = 0
        for ref, columns in zip(refs, widths):
            out_ref[:, low : low + columns] = ref[:rows] + ref[rows:]
            low += columns
        squares = jnp.sum(wide_ref[...] * wide_ref[...], axis=1, keepdims=True)
        out_ref[:, low:] = jnp.broadcast_to(squares, (rows, LANES))

    whole = pl.BlockSpec(memory_space=pltpu.VMEM)
    return pl.pallas_call(
        kernel,
        out_shape=jax.ShapeDtypeStruct((rows, sum(widths) + LANES), jnp.float32),
        in_specs=[whole] * (len(products) + 1) + [pl.BlockSpec(memory_space=pl.ANY)] * len(after),
        out_specs=whole,
        name="pack_products",
    )(*products, wide, *after)


def to_rows(column_form):
    count = column_form.shape[0] // LANES
    return jnp.concatenate(
        [
            jnp.sum(
                jnp.where(diagonal(), column_form[i * LANES : (i + 1) * LANES], 0.0),
                axis=0,
                keepdims=True,
            )
            for i in range(count)
        ]
    )


def to_columns(row_form):
    return jnp.concatenate(
        [
            jnp.sum(
                jnp.where(diagonal(), row_form[i : i + 1], 0.0), axis=1, keepdims=True
            )
            for i in range(row_form.shape[0])
        ]
    )


def diagonal():
    row = lax.broadcasted_iota(jnp.int32, (LANES, LANES), 0)
    return row == lax.broadcasted_iota(jnp.int32, (LANES, LANES), 1)


def attend_shard(queries, keys, values, lengths, score_factor):
    requests, shard_length, heads, head_dim = keys.shape
    rows = queries.shape[1]
    own_rows = rows // 2
    per_head = rows // heads
    columns = shard_length * heads
    count = requests * own_rows
    extra = count // LANES
    flat_keys = keys.reshape(requests, columns, head_dim)
    flat_values = values.reshape(requests, columns, head_dim)
    core_count = lax.axis_size("sub")

    def kernel(lengths_ref, q_ref, k_ref, v_ref, kept_ref, sent_ref, max_scr, sum_scr):
        request = pl.program_id(0)
        core = lax.axis_index("sub")
        shard = lax.axis_index("ctx") * core_count + core
        scores = (
            lax.dot_general(
                q_ref[0], k_ref[0], (((1,), (1,)), ((), ())), preferred_element_type=jnp.float32
            )
            * score_factor
        )
        row = lax.broadcasted_iota(jnp.int32, (rows, columns), 0)
        column = lax.broadcasted_iota(jnp.int32, (rows, columns), 1)
        live_columns = (lengths_ref[request] - shard * shard_length) * heads
        live = (lax.rem(column, heads) == lax.div(row, per_head)) & (column < live_columns)
        scores = jnp.where(live, scores, masked_score)
        row_max = jnp.max(scores, axis=1, keepdims=True)
        weights = jnp.where(live, jnp.exp(scores - row_max), 0.0)
        sums = jnp.dot(
            weights.astype(jnp.bfloat16), v_ref[0], preferred_element_type=jnp.float32
        )
        row_max = jnp.broadcast_to(row_max, (rows, head_dim))
        row_sum = jnp.broadcast_to(jnp.sum(weights, axis=1, keepdims=True), (rows, head_dim))
        place = pl.ds(pl.multiple_of(request * own_rows, own_rows), own_rows)
        first = core == 0
        for f, out_ref in enumerate((kept_ref, sent_ref)):
            low = first if f == 0 else jnp.logical_not(first)
            pick = lambda x: jnp.where(low, x[:own_rows], x[own_rows:])
            out_ref[place, :] = pick(sums)
            max_scr[f, place, :] = pick(row_max)
            sum_scr[f, place, :] = pick(row_sum)

        @pl.when(request == requests - 1)
        def _():
            for f, out_ref in enumerate((kept_ref, sent_ref)):
                out_ref[count : count + extra, :] = to_rows(max_scr[f])
                out_ref[count + extra :, :] = to_rows(sum_scr[f])

    large = pl.BlockSpec((1, columns, head_dim), lambda r, *_: (r, 0, 0))
    packed = (count + 2 * extra, head_dim)
    return pl.pallas_call(
        kernel,
        out_shape=(jax.ShapeDtypeStruct(packed, jnp.float32),) * 2,
        grid_spec=pltpu.PrefetchScalarGridSpec(
            num_scalar_prefetch=1,
            grid=(requests,),
            in_specs=[
                pl.BlockSpec((1, rows, head_dim), lambda r, *_: (r, 0, 0)),
                large,
                large,
            ],
            out_specs=(pl.BlockSpec(packed, lambda r, *_: (0, 0)),) * 2,
            scratch_shapes=[pltpu.VMEM((2, count, head_dim), jnp.float32)] * 2,
        ),
        compiler_params=pltpu.CompilerParams(vmem_limit_bytes=VMEM_BYTES),
        name="attend_shard",
    )(lengths, queries, in_hbm(flat_keys), in_hbm(flat_values))


def packed_sizes(packed_rows):
    extra = packed_rows // (LANES + 2)
    return extra * LANES, extra


def merge_packed(kept, other, after):
    count, extra = packed_sizes(kept.shape[0])

    def kernel(kept_ref, other_ref, *refs):
        out_ref = refs[-1]
        both = (kept_ref, other_ref)
        maxima = [ref[count : count + extra, :] for ref in both]
        largest = jnp.maximum(*maxima)
        scales = [jnp.exp(x - largest) for x in maxima]
        out_ref[:count, :] = sum(
            ref[:count, :] * to_columns(scale) for ref, scale in zip(both, scales)
        )
        out_ref[count : count + extra, :] = largest
        out_ref[count + extra :, :] = sum(
            ref[count + extra :, :] * scale for ref, scale in zip(both, scales)
        )

    whole = pl.BlockSpec(memory_space=pltpu.VMEM)
    return pl.pallas_call(
        kernel,
        out_shape=jax.ShapeDtypeStruct(kept.shape, kept.dtype),
        in_specs=[whole] * 2 + [pl.BlockSpec(memory_space=pl.ANY)] * len(after),
        out_specs=whole,
        name="merge_packed",
    )(kept, other, *after)


def finish(packed, queries, fresh_keys, fresh_values, group_size, score_factor, after):
    count, extra = packed_sizes(packed[0].shape[0])
    shares = len(packed)
    head_dim = queries.shape[1]

    def kernel(*refs):
        out_ref = refs[-1]
        packed_refs = refs[:shares]
        q_ref, key_ref, value_ref = refs[shares : shares + 3]
        wide = q_ref[...].astype(jnp.float32)
        row = lax.broadcasted_iota(jnp.int32, (count, 1), 0)
        second = lax.rem(lax.div(row, group_size), 2) == 1
        scores = [
            jnp.sum(wide * key_ref[u].astype(jnp.float32), axis=1, keepdims=True) * score_factor
            for u in range(2)
        ]
        scores[1] = jnp.where(second, scores[1], masked_score)
        maxima = [to_columns(ref[count : count + extra, :]) for ref in packed_refs]
        totals = [to_columns(ref[count + extra :, :]) for ref in packed_refs]
        largest = functools.reduce(jnp.maximum, maxima + scores)
        scales = [jnp.exp(x - largest) for x in maxima]
        weights = [jnp.exp(x - largest) for x in scores]
        weights[1] = jnp.where(second, weights[1], 0.0)
        denominator = sum(t * scale for t, scale in zip(totals, scales)) + weights[0] + weights[1]
        numerator = sum(ref[:count, :] * scale for ref, scale in zip(packed_refs, scales))
        for u in range(2):
            rounded = weights[u].astype(jnp.bfloat16).astype(jnp.float32)
            numerator = numerator + rounded * value_ref[u].astype(jnp.float32)
        out_ref[...] = (numerator / denominator).astype(jnp.bfloat16)

    whole = pl.BlockSpec(memory_space=pltpu.VMEM)
    return pl.pallas_call(
        kernel,
        out_shape=jax.ShapeDtypeStruct((count, head_dim), jnp.bfloat16),
        in_specs=[whole] * (shares + 3) + [pl.BlockSpec(memory_space=pl.ANY)] * len(after),
        out_specs=whole,
        name="finish",
    )(*packed, queries, fresh_keys, fresh_values, *after)


def local(
    width,
    key_cache,
    value_cache,
    lengths,
    owner_order,
    first_tokens,
    second_tokens,
    norm_gain,
    w_query,
    w_key,
    w_value,
    w_out,
):
    ctx_count = lax.axis_size("ctx")
    sub_count = lax.axis_size("sub")
    requests, shard_length, heads, head_dim = key_cache.shape
    assert requests == ctx_count and sub_count == 2
    heads_decode = heads // sub_count
    sub_index = lax.axis_index("sub")
    take = functools.partial(jnp.take, mode="clip")

    both = (0, 1)
    received = {}

    def hand_off(which, shift, flip, after=()):
        caches = [(key_cache, value_cache)[w] for w in which]
        block = made = arrange(caches, owner_order, shift, flip, after)
        if shift or flip:
            pairs = [
                (
                    c * sub_count + s,
                    (c + shift) % ctx_count * sub_count + (s + flip) % sub_count,
                )
                for c in range(ctx_count)
                for s in range(sub_count)
            ]
            block = lax.ppermute(made, ("ctx", "sub"), pairs)
        received[which, shift, flip] = block
        return made

    def from_all(values):
        return [values] + [
            lax.ppermute(values, "ctx", [(c, (c + shift) % ctx_count) for c in range(ctx_count)])
            for shift in range(1, ctx_count)
        ]

    middle = ctx_count // 2
    ahead = (both, 1, 0)
    leading = hand_off(*ahead)

    query_width = w_query.shape[1]
    key_width = w_key.shape[1]
    group_size = query_width // head_dim // heads_decode
    score_factor = head_dim ** (-0.5)
    rows_local = first_tokens.shape[0]
    tokens = lax.all_gather(
        pair_tokens(first_tokens, second_tokens, leading), ("head", "sub"), axis=0, tiled=True
    )
    wide = tokens.astype(jnp.float32).reshape(2 * requests, -1)
    gained = wide * norm_gain.astype(jnp.float32)
    upper = lax.reduce_precision(gained, 8, 7)
    lower = gained - upper
    halves = jnp.concatenate([upper, lower]).astype(jnp.bfloat16)
    partial = pack_products(
        [
            jnp.dot(halves, weight, preferred_element_type=jnp.float32)
            for weight in (w_query, w_key, w_value)
        ],
        wide,
        (received[ahead],),
    )
    summed = functools.reduce(jnp.add, from_all(partial))
    behind = (both, 1, 1)
    hand_off(*behind, (summed,))
    raw = summed[:, :-LANES] * lax.rsqrt(summed[:, -LANES:][:, :1] / width + eps_norm)
    raw = raw.reshape(requests, 2, -1, head_dim)
    positions = lengths.astype(jnp.float32)[:, None] + jnp.arange(2, dtype=jnp.float32)
    query_heads = query_width // head_dim
    key_heads = key_width // head_dim
    rotated = rotate(raw[:, :, : query_heads + key_heads], positions).astype(jnp.bfloat16)
    queries = rotated[:, :, :query_heads].reshape(requests, 2, heads_decode, group_size, head_dim)
    fresh_keys = rotated[:, :, query_heads:]
    fresh_values = raw[:, :, query_heads + key_heads :].astype(jnp.bfloat16)

    per_head = 2 * group_size
    own_queries = jnp.transpose(queries, (0, 2, 1, 3, 4)).reshape(
        requests, heads_decode * per_head, head_dim
    )
    all_queries = lax.all_gather(own_queries, "sub", axis=1, tiled=True)
    kept, sent = attend_shard(all_queries, key_cache, value_cache, lengths, score_factor)

    swap = [(i, (i + 1) % sub_count) for i in range(sub_count)]
    stats = merge_packed(kept, lax.ppermute(sent, "sub", swap), (received[behind],))
    hand_off(both, 0, 0, (stats,))
    hand_off(both, 0, 1, (stats,))
    packed = from_all(stats)

    rest = [
        (both, shift, flip)
        for shift in sorted(range(2, ctx_count), key=lambda d: -d)
        for flip in range(sub_count)
    ]
    blocks = [hand_off(*key, tuple(packed[1:])) for key in rest]

    def for_rows(fresh):
        spread = jnp.broadcast_to(
            fresh[:, :, :, None], (requests, 2, heads_decode, per_head, head_dim)
        )
        return jnp.swapaxes(spread, 0, 1).reshape(2, -1, head_dim)

    attended = finish(
        packed,
        own_queries.reshape(-1, head_dim),
        for_rows(fresh_keys),
        for_rows(fresh_values),
        group_size,
        score_factor,
        (received[rest[0]],) + tuple(in_hbm(x) for x in blocks[1:]),
    ).reshape(requests, heads_decode, 2, group_size, head_dim)

    attended = take(attended, owner_order, axis=0)
    attended = jnp.transpose(attended, (0, 2, 1, 3, 4)).reshape(2 * requests, query_width)
    branch = jnp.dot(attended, w_out, preferred_element_type=jnp.float32)
    branch = branch.reshape(requests, 2, -1)
    row_start = lax.axis_index(("head", "sub")) * rows_local
    parts = lax.all_gather(branch, ("head", "sub"), axis=0)
    parts = lax.dynamic_slice_in_dim(parts, row_start, rows_local, 1)
    own_ids = lax.dynamic_slice_in_dim(owner_order, row_start, rows_local)
    residual = take(tokens, own_ids, axis=0).astype(jnp.float32)
    result = (residual + jnp.sum(parts, axis=0)).astype(jnp.bfloat16)

    moved = ()
    groups = [[ahead, (both, 0, 0), (both, 0, 1), behind], rest]
    for keys in groups:
        pieces = [
            (block, entry, output, shift, flip)
            for block, (which, shift, flip) in enumerate(keys)
            for entry, output in enumerate(which)
        ]
        moved = assemble([received[key] for key in keys], pieces, moved)
    moved_keys, moved_values = (x.reshape(1, -1, heads_decode, head_dim) for x in moved)
    return (moved_keys, moved_values, result[:, 0], result[:, 1])


def solution(mesh):
    def whole(*arrays):
        return jax.shard_map(
            functools.partial(local, arrays[6].shape[0]),
            mesh=mesh,
            in_specs=(
                P("groups", ("ctx", "sub"), "head", None),
                P("groups", ("ctx", "sub"), "head", None),
                P("groups"),
                P("groups"),
                P(("groups", "head", "sub"), "ctx"),
                P(("groups", "head", "sub"), "ctx"),
                P("ctx"),
                P("ctx", ("head", "sub")),
                P("ctx", ("head", "sub")),
                P("ctx", ("head", "sub")),
                P(("head", "sub"), "ctx"),
            ),
            out_specs=(
                P(("groups", "ctx"), None, ("head", "sub"), None),
                P(("groups", "ctx"), None, ("head", "sub"), None),
                P(("groups", "head", "sub"), "ctx"),
                P(("groups", "head", "sub"), "ctx"),
            ),
            check_vma=False,
        )(*arrays)

    return whole
```

```python
import functools

import jax
import jax.numpy as jnp
from jax import lax
from jax.experimental import pallas as pl
from jax.experimental.pallas import tpu as pltpu
from jax.sharding import PartitionSpec as P

theta_base = 500000.0
eps_norm = 1e-05
masked_score = -1e30
LANES = 128
VMEM_BYTES = 48 * 1024 * 1024


def rotate(vectors, positions):
    half_dim = vectors.shape[-1] // 2
    exponents = jnp.arange(half_dim, dtype=jnp.float32) * (2.0 / vectors.shape[-1])
    frequency = theta_base ** (-exponents)
    angles = positions[..., None, None] * frequency
    cosines = jnp.cos(angles)
    sines = jnp.sin(angles)
    lower_part = vectors[..., :half_dim]
    upper_part = vectors[..., half_dim:]
    return jnp.concatenate(
        [lower_part * cosines - upper_part * sines, upper_part * cosines + lower_part * sines],
        axis=-1,
    )


def in_hbm(x):
    return pltpu.with_memory_space_constraint(x, pltpu.HBM)


def arrange(caches, owner_order, shift, flip, after, apart):
    _, shard_length, heads, head_dim = caches[0].shape
    ctx_count = lax.axis_size("ctx")
    core_count = lax.axis_size("sub")
    heads_decode = heads // core_count
    steps = 4
    places = shard_length // steps
    count = len(caches)
    pieces = [(w, i) for i in range(steps) for w in range(count)]
    outputs = count if apart else 1
    shape = (count // outputs, shard_length, heads_decode, head_dim)

    def kernel(order_ref, *refs):
        request = order_ref[lax.rem(lax.axis_index("ctx") + shift, ctx_count)]
        core = lax.rem(lax.axis_index("sub") + flip, core_count)
        in_refs = refs[:count]
        out_refs = refs[count + len(after) : -4]
        taken, made, in_sems, out_sems = refs[-4:]
        rows = lambda i: pl.ds(i * places, places)
        into = [
            pltpu.make_async_copy(
                in_refs[w].at[request, rows(i)], taken.at[w, rows(i)], in_sems.at[w, i]
            )
            for w, i in pieces
        ]
        out_of = [
            pltpu.make_async_copy(
                made.at[w, rows(i)],
                out_refs[w].at[0, rows(i)] if apart else out_refs[0].at[w, rows(i)],
                out_sems.at[w, i],
            )
            for w, i in pieces
        ]
        for copy in into:
            copy.start()
        for p, (w, i) in enumerate(pieces):
            into[p].wait()
            for own in range(core_count):

                @pl.when(core == own)
                def _():
                    low = own * heads_decode
                    made[w, rows(i)] = taken[w, rows(i), low : low + heads_decode, :]

            out_of[p].start()
        for copy in out_of:
            copy.wait()

    blocks = pl.pallas_call(
        kernel,
        out_shape=(pltpu.HBM(shape, caches[0].dtype),) * outputs,
        in_specs=[pl.BlockSpec(memory_space=pltpu.SMEM)]
        + [pl.BlockSpec(memory_space=pltpu.HBM)] * count
        + [pl.BlockSpec(memory_space=pl.ANY)] * len(after),
        out_specs=(pl.BlockSpec(memory_space=pltpu.HBM),) * outputs,
        scratch_shapes=[
            pltpu.VMEM((count, shard_length, heads, head_dim), caches[0].dtype),
            pltpu.VMEM((count, shard_length, heads_decode, head_dim), caches[0].dtype),
            pltpu.SemaphoreType.DMA((count, steps)),
            pltpu.SemaphoreType.DMA((count, steps)),
        ],
        compiler_params=pltpu.CompilerParams(vmem_limit_bytes=VMEM_BYTES),
        name="arrange",
    )(owner_order, *(in_hbm(x) for x in caches), *after)
    blocks = [x.reshape(shape[0], shard_length * heads_decode, head_dim) for x in blocks]
    return blocks if apart else blocks[0]


def hold(blocks, after):
    def kernel(*refs):
        pass

    in_place = pl.BlockSpec(memory_space=pltpu.HBM)
    return pl.pallas_call(
        kernel,
        out_shape=tuple(pltpu.HBM(x.shape, x.dtype) for x in blocks),
        in_specs=[in_place] * len(blocks) + [pl.BlockSpec(memory_space=pl.ANY)] * len(after),
        out_specs=(in_place,) * len(blocks),
        input_output_aliases={i: i for i in range(len(blocks))},
        name="hold",
    )(*(in_hbm(x) for x in blocks), *after)


def assemble(blocks, pieces, filled=()):
    ctx_count = lax.axis_size("ctx")
    core_count = lax.axis_size("sub")
    _, block_rows, head_dim = blocks[0].shape
    rows = ctx_count * core_count * block_rows
    arrays = 2
    count = len(blocks)
    total = len(pieces)

    def kernel(*refs):
        ctx = lax.axis_index("ctx")
        core = lax.axis_index("sub")
        in_refs = refs[:count]
        out_refs = refs[count + len(filled) :][:arrays]
        held, in_sems, out_sems = refs[count + len(filled) + arrays :]
        into, out_of = [], []
        for p, (block, entry, output, shift, flip) in enumerate(pieces):
            source = lax.rem(ctx + (ctx_count - shift), ctx_count) * core_count + lax.rem(
                core + (core_count - flip), core_count
            )
            place = pl.ds(pl.multiple_of(source * block_rows, block_rows), block_rows)
            into.append(
                pltpu.make_async_copy(in_refs[block].at[entry], held.at[p], in_sems.at[p])
            )
            out_of.append(
                pltpu.make_async_copy(held.at[p], out_refs[output].at[place], out_sems.at[p])
            )
        for copy in into:
            copy.start()
        for p in range(total):
            into[p].wait()
            out_of[p].start()
        for copy in out_of:
            copy.wait()

    return pl.pallas_call(
        kernel,
        out_shape=(pltpu.HBM((rows, head_dim), blocks[0].dtype),) * arrays,
        in_specs=[pl.BlockSpec(memory_space=pl.ANY)] * count
        + [pl.BlockSpec(memory_space=pltpu.HBM)] * len(filled),
        out_specs=(pl.BlockSpec(memory_space=pltpu.HBM),) * arrays,
        scratch_shapes=[
            pltpu.VMEM((total, block_rows, head_dim), blocks[0].dtype),
            pltpu.SemaphoreType.DMA((total,)),
            pltpu.SemaphoreType.DMA((total,)),
        ],
        input_output_aliases={count + w: w for w in range(len(filled))},
        compiler_params=pltpu.CompilerParams(vmem_limit_bytes=VMEM_BYTES),
        cost_estimate=pl.CostEstimate(
            flops=0, transcendentals=0, bytes_accessed=4 * total * block_rows * head_dim
        ),
        name="assemble",
    )(*blocks, *filled)


def pair_tokens(first, second, after):
    def kernel(first_ref, second_ref, after_ref, out_ref):
        out_ref[:, 0] = first_ref[...]
        out_ref[:, 1] = second_ref[...]

    whole = pl.BlockSpec(memory_space=pltpu.VMEM)
    return pl.pallas_call(
        kernel,
        out_shape=jax.ShapeDtypeStruct((first.shape[0], 2, first.shape[1]), first.dtype),
        in_specs=[whole, whole, pl.BlockSpec(memory_space=pl.ANY)],
        out_specs=whole,
        name="pair_tokens",
    )(first, second, in_hbm(after))


def pack_products(products, wide, after):
    rows = wide.shape[0]
    widths = [x.shape[1] for x in products]

    def kernel(*refs):
        wide_ref, out_ref = refs[len(products)], refs[-1]
        low = 0
        for ref, columns in zip(refs, widths):
            out_ref[:, low : low + columns] = ref[:rows] + ref[rows:]
            low += columns
        squares = jnp.sum(wide_ref[...] * wide_ref[...], axis=1, keepdims=True)
        out_ref[:, low:] = jnp.broadcast_to(squares, (rows, LANES))

    whole = pl.BlockSpec(memory_space=pltpu.VMEM)
    return pl.pallas_call(
        kernel,
        out_shape=jax.ShapeDtypeStruct((rows, sum(widths) + LANES), jnp.float32),
        in_specs=[whole] * (len(products) + 1) + [pl.BlockSpec(memory_space=pl.ANY)] * len(after),
        out_specs=whole,
        name="pack_products",
    )(*products, wide, *after)


def add_all(parts, after):
    def kernel(*refs):
        refs[-1][...] = functools.reduce(jnp.add, [ref[...] for ref in refs[: len(parts)]])

    whole = pl.BlockSpec(memory_space=pltpu.VMEM)
    return pl.pallas_call(
        kernel,
        out_shape=jax.ShapeDtypeStruct(parts[0].shape, parts[0].dtype),
        in_specs=[whole] * len(parts) + [pl.BlockSpec(memory_space=pl.ANY)] * len(after),
        out_specs=whole,
        name="add_all",
    )(*parts, *after)


def to_rows(column_form):
    count = column_form.shape[0] // LANES
    return jnp.concatenate(
        [
            jnp.sum(
                jnp.where(diagonal(), column_form[i * LANES : (i + 1) * LANES], 0.0),
                axis=0,
                keepdims=True,
            )
            for i in range(count)
        ]
    )


def to_columns(row_form):
    return jnp.concatenate(
        [
            jnp.sum(
                jnp.where(diagonal(), row_form[i : i + 1], 0.0), axis=1, keepdims=True
            )
            for i in range(row_form.shape[0])
        ]
    )


def diagonal():
    row = lax.broadcasted_iota(jnp.int32, (LANES, LANES), 0)
    return row == lax.broadcasted_iota(jnp.int32, (LANES, LANES), 1)


def attend_shard(queries, keys, values, lengths, score_factor):
    requests, shard_length, heads, head_dim = keys.shape
    rows = queries.shape[1]
    own_rows = rows // 2
    per_head = rows // heads
    columns = shard_length * heads
    count = requests * own_rows
    extra = count // LANES
    flat_keys = keys.reshape(requests, columns, head_dim)
    flat_values = values.reshape(requests, columns, head_dim)
    core_count = lax.axis_size("sub")

    def kernel(lengths_ref, q_ref, k_ref, v_ref, kept_ref, sent_ref, max_scr, sum_scr):
        request = pl.program_id(0)
        core = lax.axis_index("sub")
        shard = lax.axis_index("ctx") * core_count + core
        scores = (
            lax.dot_general(
                q_ref[0], k_ref[0], (((1,), (1,)), ((), ())), preferred_element_type=jnp.float32
            )
            * score_factor
        )
        row = lax.broadcasted_iota(jnp.int32, (rows, columns), 0)
        column = lax.broadcasted_iota(jnp.int32, (rows, columns), 1)
        live_columns = (lengths_ref[request] - shard * shard_length) * heads
        live = (lax.rem(column, heads) == lax.div(row, per_head)) & (column < live_columns)
        scores = jnp.where(live, scores, masked_score)
        row_max = jnp.max(scores, axis=1, keepdims=True)
        weights = jnp.where(live, jnp.exp(scores - row_max), 0.0)
        sums = jnp.dot(
            weights.astype(jnp.bfloat16), v_ref[0], preferred_element_type=jnp.float32
        )
        row_max = jnp.broadcast_to(row_max, (rows, head_dim))
        row_sum = jnp.broadcast_to(jnp.sum(weights, axis=1, keepdims=True), (rows, head_dim))
        place = pl.ds(pl.multiple_of(request * own_rows, own_rows), own_rows)
        first = core == 0
        for f, out_ref in enumerate((kept_ref, sent_ref)):
            low = first if f == 0 else jnp.logical_not(first)
            pick = lambda x: jnp.where(low, x[:own_rows], x[own_rows:])
            out_ref[place, :] = pick(sums)
            max_scr[f, place, :] = pick(row_max)
            sum_scr[f, place, :] = pick(row_sum)

        @pl.when(request == requests - 1)
        def _():
            for f, out_ref in enumerate((kept_ref, sent_ref)):
                out_ref[count : count + extra, :] = to_rows(max_scr[f])
                out_ref[count + extra :, :] = to_rows(sum_scr[f])

    large = pl.BlockSpec((1, columns, head_dim), lambda r, *_: (r, 0, 0))
    packed = (count + 2 * extra, head_dim)
    return pl.pallas_call(
        kernel,
        out_shape=(jax.ShapeDtypeStruct(packed, jnp.float32),) * 2,
        grid_spec=pltpu.PrefetchScalarGridSpec(
            num_scalar_prefetch=1,
            grid=(requests,),
            in_specs=[
                pl.BlockSpec((1, rows, head_dim), lambda r, *_: (r, 0, 0)),
                large,
                large,
            ],
            out_specs=(pl.BlockSpec(packed, lambda r, *_: (0, 0)),) * 2,
            scratch_shapes=[pltpu.VMEM((2, count, head_dim), jnp.float32)] * 2,
        ),
        compiler_params=pltpu.CompilerParams(vmem_limit_bytes=VMEM_BYTES),
        name="attend_shard",
    )(lengths, queries, in_hbm(flat_keys), in_hbm(flat_values))


def packed_sizes(packed_rows):
    extra = packed_rows // (LANES + 2)
    return extra * LANES, extra


def merge_packed(kept, other, after):
    count, extra = packed_sizes(kept.shape[0])

    def kernel(kept_ref, other_ref, *refs):
        out_ref = refs[-1]
        both = (kept_ref, other_ref)
        maxima = [ref[count : count + extra, :] for ref in both]
        largest = jnp.maximum(*maxima)
        scales = [jnp.exp(x - largest) for x in maxima]
        out_ref[:count, :] = sum(
            ref[:count, :] * to_columns(scale) for ref, scale in zip(both, scales)
        )
        out_ref[count : count + extra, :] = largest
        out_ref[count + extra :, :] = sum(
            ref[count + extra :, :] * scale for ref, scale in zip(both, scales)
        )

    whole = pl.BlockSpec(memory_space=pltpu.VMEM)
    return pl.pallas_call(
        kernel,
        out_shape=jax.ShapeDtypeStruct(kept.shape, kept.dtype),
        in_specs=[whole] * 2 + [pl.BlockSpec(memory_space=pl.ANY)] * len(after),
        out_specs=whole,
        name="merge_packed",
    )(kept, other, *after)


def finish(packed, queries, fresh_keys, fresh_values, group_size, score_factor, after):
    count, extra = packed_sizes(packed[0].shape[0])
    shares = len(packed)
    head_dim = queries.shape[1]

    def kernel(*refs):
        out_ref = refs[-1]
        packed_refs = refs[:shares]
        q_ref, key_ref, value_ref = refs[shares : shares + 3]
        wide = q_ref[...].astype(jnp.float32)
        row = lax.broadcasted_iota(jnp.int32, (count, 1), 0)
        second = lax.rem(lax.div(row, group_size), 2) == 1
        scores = [
            jnp.sum(wide * key_ref[u].astype(jnp.float32), axis=1, keepdims=True) * score_factor
            for u in range(2)
        ]
        scores[1] = jnp.where(second, scores[1], masked_score)
        maxima = [to_columns(ref[count : count + extra, :]) for ref in packed_refs]
        totals = [to_columns(ref[count + extra :, :]) for ref in packed_refs]
        largest = functools.reduce(jnp.maximum, maxima + scores)
        scales = [jnp.exp(x - largest) for x in maxima]
        weights = [jnp.exp(x - largest) for x in scores]
        weights[1] = jnp.where(second, weights[1], 0.0)
        denominator = sum(t * scale for t, scale in zip(totals, scales)) + weights[0] + weights[1]
        numerator = sum(ref[:count, :] * scale for ref, scale in zip(packed_refs, scales))
        for u in range(2):
            rounded = weights[u].astype(jnp.bfloat16).astype(jnp.float32)
            numerator = numerator + rounded * value_ref[u].astype(jnp.float32)
        out_ref[...] = (numerator / denominator).astype(jnp.bfloat16)

    whole = pl.BlockSpec(memory_space=pltpu.VMEM)
    return pl.pallas_call(
        kernel,
        out_shape=jax.ShapeDtypeStruct((count, head_dim), jnp.bfloat16),
        in_specs=[whole] * (shares + 3) + [pl.BlockSpec(memory_space=pl.ANY)] * len(after),
        out_specs=whole,
        name="finish",
    )(*packed, queries, fresh_keys, fresh_values, *after)


def local(
    width,
    key_cache,
    value_cache,
    lengths,
    owner_order,
    first_tokens,
    second_tokens,
    norm_gain,
    w_query,
    w_key,
    w_value,
    w_out,
):
    ctx_count = lax.axis_size("ctx")
    sub_count = lax.axis_size("sub")
    requests, shard_length, heads, head_dim = key_cache.shape
    assert requests == ctx_count and sub_count == 2
    heads_decode = heads // sub_count
    sub_index = lax.axis_index("sub")
    take = functools.partial(jnp.take, mode="clip")

    both = (0, 1)
    received = {}

    def make(shift, flip, after=(), apart=False):
        return arrange((key_cache, value_cache), owner_order, shift, flip, after, apart)

    def send(block, which, shift, flip):
        pairs = [
            (
                c * sub_count + s,
                (c + shift) % ctx_count * sub_count + (s + flip) % sub_count,
            )
            for c in range(ctx_count)
            for s in range(sub_count)
        ]
        moved = lax.ppermute(block, ("ctx", "sub"), pairs)
        received[which, shift, flip] = moved
        return moved

    def from_all(values):
        return [values] + [
            lax.ppermute(values, "ctx", [(c, (c + shift) % ctx_count) for c in range(ctx_count)])
            for shift in range(1, ctx_count)
        ]

    middle = ctx_count // 2
    leading = make(1, 0, apart=True)
    ahead = [send(leading[w], (w,), 1, 0) for w in both]

    query_width = w_query.shape[1]
    key_width = w_key.shape[1]
    group_size = query_width // head_dim // heads_decode
    score_factor = head_dim ** (-0.5)
    rows_local = first_tokens.shape[0]
    tokens = lax.all_gather(
        pair_tokens(first_tokens, second_tokens, leading[0]), ("head", "sub"), axis=0, tiled=True
    )
    wide = tokens.astype(jnp.float32).reshape(2 * requests, -1)
    gained = wide * norm_gain.astype(jnp.float32)
    upper = lax.reduce_precision(gained, 8, 7)
    lower = gained - upper
    halves = jnp.concatenate([upper, lower]).astype(jnp.bfloat16)
    partial = pack_products(
        [
            jnp.dot(halves, weight, preferred_element_type=jnp.float32)
            for weight in (w_query, w_key, w_value)
        ],
        wide,
        (ahead[0],),
    )
    summed = add_all(from_all(partial), (ahead[1],))
    waiting = hold(make(1, 1, (partial,), apart=True), (summed,))
    behind = [send(waiting[w], (w,), 1, 1) for w in both]
    raw = summed[:, :-LANES] * lax.rsqrt(summed[:, -LANES:][:, :1] / width + eps_norm)
    raw = raw.reshape(requests, 2, -1, head_dim)
    positions = lengths.astype(jnp.float32)[:, None] + jnp.arange(2, dtype=jnp.float32)
    query_heads = query_width // head_dim
    key_heads = key_width // head_dim
    rotated = rotate(raw[:, :, : query_heads + key_heads], positions).astype(jnp.bfloat16)
    queries = rotated[:, :, :query_heads].reshape(requests, 2, heads_decode, group_size, head_dim)
    fresh_keys = rotated[:, :, query_heads:]
    fresh_values = raw[:, :, query_heads + key_heads :].astype(jnp.bfloat16)

    per_head = 2 * group_size
    own_queries = jnp.transpose(queries, (0, 2, 1, 3, 4)).reshape(
        requests, heads_decode * per_head, head_dim
    )
    all_queries = lax.all_gather(own_queries, "sub", axis=1, tiled=True)
    kept, sent = attend_shard(all_queries, key_cache, value_cache, lengths, score_factor)

    swap = [(i, (i + 1) % sub_count) for i in range(sub_count)]
    stats = merge_packed(kept, lax.ppermute(sent, "sub", swap), (behind[0],))
    packed = from_all(stats)

    rest = [
        (shift, flip)
        for shift in sorted(range(2, ctx_count), key=lambda d: -d)
        for flip in range(sub_count)
    ]
    blocks = hold(
        [make(*key, (stats,)) for key in rest], tuple(packed[1:]) + (behind[1],)
    )
    for block, key in zip(blocks, rest):
        send(block, both, *key)
    received[both, 0, 0] = make(0, 0, tuple(packed[1:]))
    send(make(0, 1, tuple(packed[1:])), both, 0, 1)

    def for_rows(fresh):
        spread = jnp.broadcast_to(
            fresh[:, :, :, None], (requests, 2, heads_decode, per_head, head_dim)
        )
        return jnp.swapaxes(spread, 0, 1).reshape(2, -1, head_dim)

    attended = finish(
        packed,
        own_queries.reshape(-1, head_dim),
        for_rows(fresh_keys),
        for_rows(fresh_values),
        group_size,
        score_factor,
        (received[both, *rest[0]],) + tuple(in_hbm(x) for x in blocks[1:]),
    ).reshape(requests, heads_decode, 2, group_size, head_dim)

    attended = take(attended, owner_order, axis=0)
    attended = jnp.transpose(attended, (0, 2, 1, 3, 4)).reshape(2 * requests, query_width)
    branch = jnp.dot(attended, w_out, preferred_element_type=jnp.float32)
    branch = branch.reshape(requests, 2, -1)
    row_start = lax.axis_index(("head", "sub")) * rows_local
    parts = lax.all_gather(branch, ("head", "sub"), axis=0)
    parts = lax.dynamic_slice_in_dim(parts, row_start, rows_local, 1)
    own_ids = lax.dynamic_slice_in_dim(owner_order, row_start, rows_local)
    residual = take(tokens, own_ids, axis=0).astype(jnp.float32)
    result = (residual + jnp.sum(parts, axis=0)).astype(jnp.bfloat16)

    moved = ()
    early = [((w,), 1, flip) for flip in range(sub_count) for w in both]
    groups = [
        early + [(both, 0, 0), (both, 0, 1)],
        [(both, *key) for key in rest],
    ]
    for keys in groups:
        pieces = [
            (block, entry, output, shift, flip)
            for block, (which, shift, flip) in enumerate(keys)
            for entry, output in enumerate(which)
        ]
        moved = assemble([received[key] for key in keys], pieces, moved)
    moved_keys, moved_values = (x.reshape(1, -1, heads_decode, head_dim) for x in moved)
    return (moved_keys, moved_values, result[:, 0], result[:, 1])


def solution(mesh):
    def whole(*arrays):
        return jax.shard_map(
            functools.partial(local, arrays[6].shape[0]),
            mesh=mesh,
            in_specs=(
                P("groups", ("ctx", "sub"), "head", None),
                P("groups", ("ctx", "sub"), "head", None),
                P("groups"),
                P("groups"),
                P(("groups", "head", "sub"), "ctx"),
                P(("groups", "head", "sub"), "ctx"),
                P("ctx"),
                P("ctx", ("head", "sub")),
                P("ctx", ("head", "sub")),
                P("ctx", ("head", "sub")),
                P(("head", "sub"), "ctx"),
            ),
            out_specs=(
                P(("groups", "ctx"), None, ("head", "sub"), None),
                P(("groups", "ctx"), None, ("head", "sub"), None),
                P(("groups", "head", "sub"), "ctx"),
                P(("groups", "head", "sub"), "ctx"),
            ),
            check_vma=False,
        )(*arrays)

    return whole
```

```python
import functools

import jax
import jax.numpy as jnp
from jax import lax
from jax.experimental import pallas as pl
from jax.experimental.pallas import tpu as pltpu
from jax.sharding import PartitionSpec as P

theta_base = 500000.0
eps_norm = 1e-05
masked_score = -1e30
LANES = 128
VMEM_BYTES = 48 * 1024 * 1024


def rotate(vectors, positions):
    half_dim = vectors.shape[-1] // 2
    exponents = jnp.arange(half_dim, dtype=jnp.float32) * (2.0 / vectors.shape[-1])
    frequency = theta_base ** (-exponents)
    angles = positions[..., None, None] * frequency
    cosines = jnp.cos(angles)
    sines = jnp.sin(angles)
    lower_part = vectors[..., :half_dim]
    upper_part = vectors[..., half_dim:]
    return jnp.concatenate(
        [lower_part * cosines - upper_part * sines, upper_part * cosines + lower_part * sines],
        axis=-1,
    )


def in_hbm(x):
    return pltpu.with_memory_space_constraint(x, pltpu.HBM)


def in_vmem(x):
    return pltpu.with_memory_space_constraint(x, pltpu.VMEM)


def vmem_specs(count):
    return [pl.BlockSpec(memory_space=pltpu.VMEM)] * count


def arrange(caches, owner_order, shift, flip, after, apart):
    _, shard_length, heads, head_dim = caches[0].shape
    ctx_count = lax.axis_size("ctx")
    core_count = lax.axis_size("sub")
    heads_decode = heads // core_count
    steps = 4
    places = shard_length // steps
    count = len(caches)
    pieces = [(w, i) for i in range(steps) for w in range(count)]
    outputs = count if apart else 1
    shape = (count // outputs, shard_length, heads_decode, head_dim)

    def kernel(order_ref, *refs):
        request = order_ref[lax.rem(lax.axis_index("ctx") + shift, ctx_count)]
        core = lax.rem(lax.axis_index("sub") + flip, core_count)
        in_refs = refs[:count]
        out_refs = refs[count + len(after) : -4]
        taken, made, in_sems, out_sems = refs[-4:]
        rows = lambda i: pl.ds(i * places, places)
        into = [
            pltpu.make_async_copy(
                in_refs[w].at[request, rows(i)], taken.at[w, rows(i)], in_sems.at[w, i]
            )
            for w, i in pieces
        ]
        out_of = [
            pltpu.make_async_copy(
                made.at[w, rows(i)],
                out_refs[w].at[0, rows(i)] if apart else out_refs[0].at[w, rows(i)],
                out_sems.at[w, i],
            )
            for w, i in pieces
        ]
        for copy in into:
            copy.start()
        for p, (w, i) in enumerate(pieces):
            into[p].wait()
            for own in range(core_count):

                @pl.when(core == own)
                def _():
                    low = own * heads_decode
                    made[w, rows(i)] = taken[w, rows(i), low : low + heads_decode, :]

            out_of[p].start()
        for copy in out_of:
            copy.wait()

    blocks = pl.pallas_call(
        kernel,
        out_shape=(pltpu.HBM(shape, caches[0].dtype),) * outputs,
        in_specs=[pl.BlockSpec(memory_space=pltpu.SMEM)]
        + [pl.BlockSpec(memory_space=pltpu.HBM)] * count
        + vmem_specs(len(after)),
        out_specs=(pl.BlockSpec(memory_space=pltpu.HBM),) * outputs,
        scratch_shapes=[
            pltpu.VMEM((count, shard_length, heads, head_dim), caches[0].dtype),
            pltpu.VMEM((count, shard_length, heads_decode, head_dim), caches[0].dtype),
            pltpu.SemaphoreType.DMA((count, steps)),
            pltpu.SemaphoreType.DMA((count, steps)),
        ],
        compiler_params=pltpu.CompilerParams(vmem_limit_bytes=VMEM_BYTES),
        name="arrange",
    )(owner_order, *(in_hbm(x) for x in caches), *(in_vmem(x) for x in after))
    blocks = [x.reshape(shape[0], shard_length * heads_decode, head_dim) for x in blocks]
    return blocks if apart else blocks[0]


def hold(blocks, after):
    def kernel(*refs):
        pass

    in_place = pl.BlockSpec(memory_space=pltpu.HBM)
    return pl.pallas_call(
        kernel,
        out_shape=tuple(pltpu.HBM(x.shape, x.dtype) for x in blocks),
        in_specs=[in_place] * len(blocks) + vmem_specs(len(after)),
        out_specs=(in_place,) * len(blocks),
        input_output_aliases={i: i for i in range(len(blocks))},
        name="hold",
    )(*(in_hbm(x) for x in blocks), *(in_vmem(x) for x in after))


def assemble(blocks, pieces, filled=()):
    ctx_count = lax.axis_size("ctx")
    core_count = lax.axis_size("sub")
    _, block_rows, head_dim = blocks[0].shape
    rows = ctx_count * core_count * block_rows
    arrays = 2
    count = len(blocks)
    total = len(pieces)

    def kernel(*refs):
        ctx = lax.axis_index("ctx")
        core = lax.axis_index("sub")
        in_refs = refs[:count]
        out_refs = refs[count + len(filled) :][:arrays]
        held, in_sems, out_sems = refs[count + len(filled) + arrays :]
        into, out_of = [], []
        for p, (block, entry, output, shift, flip) in enumerate(pieces):
            source = lax.rem(ctx + (ctx_count - shift), ctx_count) * core_count + lax.rem(
                core + (core_count - flip), core_count
            )
            place = pl.ds(pl.multiple_of(source * block_rows, block_rows), block_rows)
            into.append(
                pltpu.make_async_copy(in_refs[block].at[entry], held.at[p], in_sems.at[p])
            )
            out_of.append(
                pltpu.make_async_copy(held.at[p], out_refs[output].at[place], out_sems.at[p])
            )
        for copy in into:
            copy.start()
        for p in range(total):
            into[p].wait()
            out_of[p].start()
        for copy in out_of:
            copy.wait()

    return pl.pallas_call(
        kernel,
        out_shape=(pltpu.HBM((rows, head_dim), blocks[0].dtype),) * arrays,
        in_specs=[pl.BlockSpec(memory_space=pl.ANY)] * count
        + [pl.BlockSpec(memory_space=pltpu.HBM)] * len(filled),
        out_specs=(pl.BlockSpec(memory_space=pltpu.HBM),) * arrays,
        scratch_shapes=[
            pltpu.VMEM((total, block_rows, head_dim), blocks[0].dtype),
            pltpu.SemaphoreType.DMA((total,)),
            pltpu.SemaphoreType.DMA((total,)),
        ],
        input_output_aliases={count + w: w for w in range(len(filled))},
        compiler_params=pltpu.CompilerParams(vmem_limit_bytes=VMEM_BYTES),
        cost_estimate=pl.CostEstimate(
            flops=0, transcendentals=0, bytes_accessed=4 * total * block_rows * head_dim
        ),
        name="assemble",
    )(*blocks, *filled)


def pair_tokens(first, second, after):
    def kernel(first_ref, second_ref, after_ref, out_ref):
        out_ref[:, 0] = first_ref[...]
        out_ref[:, 1] = second_ref[...]

    whole = pl.BlockSpec(memory_space=pltpu.VMEM)
    return pl.pallas_call(
        kernel,
        out_shape=jax.ShapeDtypeStruct((first.shape[0], 2, first.shape[1]), first.dtype),
        in_specs=[whole, whole, pl.BlockSpec(memory_space=pl.ANY)],
        out_specs=whole,
        name="pair_tokens",
    )(first, second, in_hbm(after))


def pack_products(products, wide, after):
    rows = wide.shape[0]
    widths = [x.shape[1] for x in products]

    def kernel(*refs):
        wide_ref, out_ref = refs[len(products)], refs[-1]
        low = 0
        for ref, columns in zip(refs, widths):
            out_ref[:, low : low + columns] = ref[:rows] + ref[rows:]
            low += columns
        squares = jnp.sum(wide_ref[...] * wide_ref[...], axis=1, keepdims=True)
        out_ref[:, low:] = jnp.broadcast_to(squares, (rows, LANES))

    whole = pl.BlockSpec(memory_space=pltpu.VMEM)
    return pl.pallas_call(
        kernel,
        out_shape=pltpu.VMEM((rows, sum(widths) + LANES), jnp.float32),
        in_specs=[whole] * (len(products) + 1 + len(after)),
        out_specs=whole,
        name="pack_products",
    )(*(in_vmem(x) for x in (*products, wide, *after)))


def to_rows(column_form):
    count = column_form.shape[0] // LANES
    return jnp.concatenate(
        [
            jnp.sum(
                jnp.where(diagonal(), column_form[i * LANES : (i + 1) * LANES], 0.0),
                axis=0,
                keepdims=True,
            )
            for i in range(count)
        ]
    )


def to_columns(row_form):
    return jnp.concatenate(
        [
            jnp.sum(
                jnp.where(diagonal(), row_form[i : i + 1], 0.0), axis=1, keepdims=True
            )
            for i in range(row_form.shape[0])
        ]
    )


def diagonal():
    row = lax.broadcasted_iota(jnp.int32, (LANES, LANES), 0)
    return row == lax.broadcasted_iota(jnp.int32, (LANES, LANES), 1)


def attend_shard(queries, keys, values, lengths, score_factor):
    requests, shard_length, heads, head_dim = keys.shape
    rows = queries.shape[1]
    own_rows = rows // 2
    per_head = rows // heads
    columns = shard_length * heads
    count = requests * own_rows
    extra = count // LANES
    flat_keys = keys.reshape(requests, columns, head_dim)
    flat_values = values.reshape(requests, columns, head_dim)
    core_count = lax.axis_size("sub")

    def kernel(lengths_ref, q_ref, k_ref, v_ref, kept_ref, sent_ref, max_scr, sum_scr):
        request = pl.program_id(0)
        core = lax.axis_index("sub")
        shard = lax.axis_index("ctx") * core_count + core
        scores = (
            lax.dot_general(
                q_ref[0], k_ref[0], (((1,), (1,)), ((), ())), preferred_element_type=jnp.float32
            )
            * score_factor
        )
        row = lax.broadcasted_iota(jnp.int32, (rows, columns), 0)
        column = lax.broadcasted_iota(jnp.int32, (rows, columns), 1)
        live_columns = (lengths_ref[request] - shard * shard_length) * heads
        live = (lax.rem(column, heads) == lax.div(row, per_head)) & (column < live_columns)
        scores = jnp.where(live, scores, masked_score)
        row_max = jnp.max(scores, axis=1, keepdims=True)
        weights = jnp.where(live, jnp.exp(scores - row_max), 0.0)
        sums = jnp.dot(
            weights.astype(jnp.bfloat16), v_ref[0], preferred_element_type=jnp.float32
        )
        row_max = jnp.broadcast_to(row_max, (rows, head_dim))
        row_sum = jnp.broadcast_to(jnp.sum(weights, axis=1, keepdims=True), (rows, head_dim))
        place = pl.ds(pl.multiple_of(request * own_rows, own_rows), own_rows)
        first = core == 0
        for f, out_ref in enumerate((kept_ref, sent_ref)):
            low = first if f == 0 else jnp.logical_not(first)
            pick = lambda x: jnp.where(low, x[:own_rows], x[own_rows:])
            out_ref[place, :] = pick(sums)
            max_scr[f, place, :] = pick(row_max)
            sum_scr[f, place, :] = pick(row_sum)

        @pl.when(request == requests - 1)
        def _():
            for f, out_ref in enumerate((kept_ref, sent_ref)):
                out_ref[count : count + extra, :] = to_rows(max_scr[f])
                out_ref[count + extra :, :] = to_rows(sum_scr[f])

    large = pl.BlockSpec((1, columns, head_dim), lambda r, *_: (r, 0, 0))
    packed = (count + 2 * extra, head_dim)
    return pl.pallas_call(
        kernel,
        out_shape=(pltpu.VMEM(packed, jnp.float32),) * 2,
        grid_spec=pltpu.PrefetchScalarGridSpec(
            num_scalar_prefetch=1,
            grid=(requests,),
            in_specs=[
                pl.BlockSpec((1, rows, head_dim), lambda r, *_: (r, 0, 0)),
                large,
                large,
            ],
            out_specs=tuple(vmem_specs(2)),
            scratch_shapes=[pltpu.VMEM((2, count, head_dim), jnp.float32)] * 2,
        ),
        compiler_params=pltpu.CompilerParams(vmem_limit_bytes=VMEM_BYTES),
        name="attend_shard",
    )(lengths, queries, in_hbm(flat_keys), in_hbm(flat_values))


def packed_sizes(packed_rows):
    extra = packed_rows // (LANES + 2)
    return extra * LANES, extra


def merge_packed(kept, other, after):
    count, extra = packed_sizes(kept.shape[0])

    def kernel(kept_ref, other_ref, *refs):
        out_ref = refs[-1]
        both = (kept_ref, other_ref)
        maxima = [ref[count : count + extra, :] for ref in both]
        largest = jnp.maximum(*maxima)
        scales = [jnp.exp(x - largest) for x in maxima]
        out_ref[:count, :] = sum(
            ref[:count, :] * to_columns(scale) for ref, scale in zip(both, scales)
        )
        out_ref[count : count + extra, :] = largest
        out_ref[count + extra :, :] = sum(
            ref[count + extra :, :] * scale for ref, scale in zip(both, scales)
        )

    whole = pl.BlockSpec(memory_space=pltpu.VMEM)
    return pl.pallas_call(
        kernel,
        out_shape=pltpu.VMEM(kept.shape, kept.dtype),
        in_specs=[whole] * (2 + len(after)),
        out_specs=whole,
        name="merge_packed",
    )(*(in_vmem(x) for x in (kept, other, *after)))


def finish(packed, queries, fresh_keys, fresh_values, group_size, score_factor, after, made):
    count, extra = packed_sizes(packed[0].shape[0])
    shares = len(packed)
    head_dim = queries.shape[1]

    def kernel(*refs):
        out_ref = refs[-1]
        packed_refs = refs[:shares]
        q_ref, key_ref, value_ref = refs[shares : shares + 3]
        wide = q_ref[...].astype(jnp.float32)
        row = lax.broadcasted_iota(jnp.int32, (count, 1), 0)
        second = lax.rem(lax.div(row, group_size), 2) == 1
        scores = [
            jnp.sum(wide * key_ref[u].astype(jnp.float32), axis=1, keepdims=True) * score_factor
            for u in range(2)
        ]
        scores[1] = jnp.where(second, scores[1], masked_score)
        maxima = [to_columns(ref[count : count + extra, :]) for ref in packed_refs]
        totals = [to_columns(ref[count + extra :, :]) for ref in packed_refs]
        largest = functools.reduce(jnp.maximum, maxima + scores)
        scales = [jnp.exp(x - largest) for x in maxima]
        weights = [jnp.exp(x - largest) for x in scores]
        weights[1] = jnp.where(second, weights[1], 0.0)
        denominator = sum(t * scale for t, scale in zip(totals, scales)) + weights[0] + weights[1]
        numerator = sum(ref[:count, :] * scale for ref, scale in zip(packed_refs, scales))
        for u in range(2):
            rounded = weights[u].astype(jnp.bfloat16).astype(jnp.float32)
            numerator = numerator + rounded * value_ref[u].astype(jnp.float32)
        out_ref[...] = (numerator / denominator).astype(jnp.bfloat16)

    whole = pl.BlockSpec(memory_space=pltpu.VMEM)
    return pl.pallas_call(
        kernel,
        out_shape=pltpu.VMEM((count, head_dim), jnp.bfloat16),
        in_specs=[whole] * (shares + 3 + len(after))
        + [pl.BlockSpec(memory_space=pltpu.HBM)] * len(made),
        out_specs=whole,
        name="finish",
    )(
        *(in_vmem(x) for x in (*packed, queries, fresh_keys, fresh_values, *after)),
        *(in_hbm(x) for x in made),
    )


def local(
    width,
    key_cache,
    value_cache,
    lengths,
    owner_order,
    first_tokens,
    second_tokens,
    norm_gain,
    w_query,
    w_key,
    w_value,
    w_out,
):
    ctx_count = lax.axis_size("ctx")
    sub_count = lax.axis_size("sub")
    requests, shard_length, heads, head_dim = key_cache.shape
    assert requests == ctx_count and sub_count == 2
    heads_decode = heads // sub_count
    sub_index = lax.axis_index("sub")
    take = functools.partial(jnp.take, mode="clip")

    both = (0, 1)
    received = {}

    def make(shift, flip, after=(), apart=False):
        return arrange((key_cache, value_cache), owner_order, shift, flip, after, apart)

    def send(block, which, shift, flip):
        pairs = [
            (
                c * sub_count + s,
                (c + shift) % ctx_count * sub_count + (s + flip) % sub_count,
            )
            for c in range(ctx_count)
            for s in range(sub_count)
        ]
        moved = lax.ppermute(block, ("ctx", "sub"), pairs)
        received[which, shift, flip] = moved
        return moved

    def from_all(values):
        return [values] + [
            lax.ppermute(values, "ctx", [(c, (c + shift) % ctx_count) for c in range(ctx_count)])
            for shift in range(1, ctx_count)
        ]

    middle = ctx_count // 2
    leading = make(1, 0, apart=True)
    paired = pair_tokens(first_tokens, second_tokens, leading[0])
    later = hold(leading[1:], (paired,))
    ahead = [send(block, (w,), 1, 0) for w, block in enumerate([leading[0], *later])]

    query_width = w_query.shape[1]
    key_width = w_key.shape[1]
    group_size = query_width // head_dim // heads_decode
    score_factor = head_dim ** (-0.5)
    rows_local = first_tokens.shape[0]
    tokens = lax.all_gather(
        paired, ("head", "sub"), axis=0, tiled=True
    )
    wide = tokens.astype(jnp.float32).reshape(2 * requests, -1)
    gained = wide * norm_gain.astype(jnp.float32)
    upper = lax.reduce_precision(gained, 8, 7)
    lower = gained - upper
    halves = jnp.concatenate([upper, lower]).astype(jnp.bfloat16)
    partial = pack_products(
        [
            jnp.dot(halves, weight, preferred_element_type=jnp.float32)
            for weight in (w_query, w_key, w_value)
        ],
        wide,
        (ahead[0],),
    )
    summed = functools.reduce(jnp.add, from_all(partial))
    waiting = hold(make(1, 1, (partial,), apart=True), (summed, ahead[1]))
    behind = [send(waiting[w], (w,), 1, 1) for w in both]
    raw = summed[:, :-LANES] * lax.rsqrt(summed[:, -LANES:][:, :1] / width + eps_norm)
    raw = raw.reshape(requests, 2, -1, head_dim)
    positions = lengths.astype(jnp.float32)[:, None] + jnp.arange(2, dtype=jnp.float32)
    query_heads = query_width // head_dim
    key_heads = key_width // head_dim
    rotated = rotate(raw[:, :, : query_heads + key_heads], positions).astype(jnp.bfloat16)
    queries = rotated[:, :, :query_heads].reshape(requests, 2, heads_decode, group_size, head_dim)
    fresh_keys = rotated[:, :, query_heads:]
    fresh_values = raw[:, :, query_heads + key_heads :].astype(jnp.bfloat16)

    per_head = 2 * group_size
    own_queries = jnp.transpose(queries, (0, 2, 1, 3, 4)).reshape(
        requests, heads_decode * per_head, head_dim
    )
    all_queries = lax.all_gather(own_queries, "sub", axis=1, tiled=True)
    kept, sent = attend_shard(all_queries, key_cache, value_cache, lengths, score_factor)

    swap = [(i, (i + 1) % sub_count) for i in range(sub_count)]
    stats = merge_packed(kept, lax.ppermute(sent, "sub", swap), (behind[0],))
    packed = from_all(stats)

    rest = [
        (shift, flip)
        for shift in sorted(range(2, ctx_count), key=lambda d: -d)
        for flip in range(sub_count)
    ]
    blocks = hold([make(*rest[0], (partial,))], (*packed[1:], behind[1]))
    blocks = [*blocks, *(make(*key, tuple(packed[1:])) for key in rest[1:])]
    for block, key in zip(blocks, rest):
        send(block, both, *key)
    received[both, 0, 0] = make(0, 0, tuple(packed[1:]))
    send(make(0, 1, tuple(packed[1:])), both, 0, 1)

    def for_rows(fresh):
        spread = jnp.broadcast_to(
            fresh[:, :, :, None], (requests, 2, heads_decode, per_head, head_dim)
        )
        return jnp.swapaxes(spread, 0, 1).reshape(2, -1, head_dim)

    attended = finish(
        packed,
        own_queries.reshape(-1, head_dim),
        for_rows(fresh_keys),
        for_rows(fresh_values),
        group_size,
        score_factor,
        (received[both, *rest[0]],),
        blocks[1:],
    ).reshape(requests, heads_decode, 2, group_size, head_dim)

    attended = take(attended, owner_order, axis=0)
    attended = jnp.transpose(attended, (0, 2, 1, 3, 4)).reshape(2 * requests, query_width)
    branch = jnp.dot(attended, w_out, preferred_element_type=jnp.float32)
    branch = branch.reshape(requests, 2, -1)
    row_start = lax.axis_index(("head", "sub")) * rows_local
    parts = lax.all_gather(branch, ("head", "sub"), axis=0)
    parts = lax.dynamic_slice_in_dim(parts, row_start, rows_local, 1)
    own_ids = lax.dynamic_slice_in_dim(owner_order, row_start, rows_local)
    residual = take(tokens, own_ids, axis=0).astype(jnp.float32)
    result = (residual + jnp.sum(parts, axis=0)).astype(jnp.bfloat16)

    moved = ()
    early = [((w,), 1, flip) for flip in range(sub_count) for w in both]
    groups = [
        early + [(both, 0, 0), (both, 0, 1)],
        [(both, *key) for key in rest[:-1]],
        [(both, *rest[-1])],
    ]
    for keys in groups:
        pieces = [
            (block, entry, output, shift, flip)
            for block, (which, shift, flip) in enumerate(keys)
            for entry, output in enumerate(which)
        ]
        moved = assemble([received[key] for key in keys], pieces, moved)
    moved_keys, moved_values = (x.reshape(1, -1, heads_decode, head_dim) for x in moved)
    return (moved_keys, moved_values, result[:, 0], result[:, 1])


def solution(mesh):
    def whole(*arrays):
        return jax.shard_map(
            functools.partial(local, arrays[6].shape[0]),
            mesh=mesh,
            in_specs=(
                P("groups", ("ctx", "sub"), "head", None),
                P("groups", ("ctx", "sub"), "head", None),
                P("groups"),
                P("groups"),
                P(("groups", "head", "sub"), "ctx"),
                P(("groups", "head", "sub"), "ctx"),
                P("ctx"),
                P("ctx", ("head", "sub")),
                P("ctx", ("head", "sub")),
                P("ctx", ("head", "sub")),
                P(("head", "sub"), "ctx"),
            ),
            out_specs=(
                P(("groups", "ctx"), None, ("head", "sub"), None),
                P(("groups", "ctx"), None, ("head", "sub"), None),
                P(("groups", "head", "sub"), "ctx"),
                P(("groups", "head", "sub"), "ctx"),
            ),
            check_vma=False,
        )(*arrays)

    return whole
```

```python
import functools

import jax
import jax.numpy as jnp
from jax import lax
from jax.experimental import pallas as pl
from jax.experimental.pallas import tpu as pltpu
from jax.sharding import PartitionSpec as P

theta_base = 500000.0
eps_norm = 1e-05
masked_score = -1e30
LANES = 128
VMEM_BYTES = 48 * 1024 * 1024


def rotate(vectors, positions):
    half_dim = vectors.shape[-1] // 2
    exponents = jnp.arange(half_dim, dtype=jnp.float32) * (2.0 / vectors.shape[-1])
    frequency = theta_base ** (-exponents)
    angles = positions[..., None, None] * frequency
    cosines = jnp.cos(angles)
    sines = jnp.sin(angles)
    lower_part = vectors[..., :half_dim]
    upper_part = vectors[..., half_dim:]
    return jnp.concatenate(
        [lower_part * cosines - upper_part * sines, upper_part * cosines + lower_part * sines],
        axis=-1,
    )


def in_hbm(x):
    return pltpu.with_memory_space_constraint(x, pltpu.HBM)


def in_vmem(x):
    return pltpu.with_memory_space_constraint(x, pltpu.VMEM)


def vmem_specs(count):
    return [pl.BlockSpec(memory_space=pltpu.VMEM)] * count


def arrange(caches, owner_order, shift, flip, after, apart):
    _, shard_length, heads, head_dim = caches[0].shape
    ctx_count = lax.axis_size("ctx")
    core_count = lax.axis_size("sub")
    heads_decode = heads // core_count
    steps = 4
    places = shard_length // steps
    count = len(caches)
    pieces = [(w, i) for i in range(steps) for w in range(count)]
    outputs = count if apart else 1
    shape = (count // outputs, shard_length, heads_decode, head_dim)

    def kernel(order_ref, *refs):
        request = order_ref[lax.rem(lax.axis_index("ctx") + shift, ctx_count)]
        core = lax.rem(lax.axis_index("sub") + flip, core_count)
        in_refs = refs[:count]
        out_refs = refs[count + len(after) : -4]
        taken, made, in_sems, out_sems = refs[-4:]
        rows = lambda i: pl.ds(i * places, places)
        into = [
            pltpu.make_async_copy(
                in_refs[w].at[request, rows(i)], taken.at[w, rows(i)], in_sems.at[w, i]
            )
            for w, i in pieces
        ]
        out_of = [
            pltpu.make_async_copy(
                made.at[w, rows(i)],
                out_refs[w].at[0, rows(i)] if apart else out_refs[0].at[w, rows(i)],
                out_sems.at[w, i],
            )
            for w, i in pieces
        ]
        for copy in into:
            copy.start()
        for p, (w, i) in enumerate(pieces):
            into[p].wait()
            for own in range(core_count):

                @pl.when(core == own)
                def _():
                    low = own * heads_decode
                    made[w, rows(i)] = taken[w, rows(i), low : low + heads_decode, :]

            out_of[p].start()
        for copy in out_of:
            copy.wait()

    blocks = pl.pallas_call(
        kernel,
        out_shape=(pltpu.HBM(shape, caches[0].dtype),) * outputs,
        in_specs=[pl.BlockSpec(memory_space=pltpu.SMEM)]
        + [pl.BlockSpec(memory_space=pltpu.HBM)] * count
        + vmem_specs(len(after)),
        out_specs=(pl.BlockSpec(memory_space=pltpu.HBM),) * outputs,
        scratch_shapes=[
            pltpu.VMEM((count, shard_length, heads, head_dim), caches[0].dtype),
            pltpu.VMEM((count, shard_length, heads_decode, head_dim), caches[0].dtype),
            pltpu.SemaphoreType.DMA((count, steps)),
            pltpu.SemaphoreType.DMA((count, steps)),
        ],
        compiler_params=pltpu.CompilerParams(vmem_limit_bytes=VMEM_BYTES),
        name="arrange",
    )(owner_order, *(in_hbm(x) for x in caches), *(in_vmem(x) for x in after))
    blocks = [x.reshape(shape[0], shard_length * heads_decode, head_dim) for x in blocks]
    return blocks if apart else blocks[0]


def hold(blocks, after):
    def kernel(*refs):
        pass

    in_place = pl.BlockSpec(memory_space=pltpu.HBM)
    return pl.pallas_call(
        kernel,
        out_shape=tuple(pltpu.HBM(x.shape, x.dtype) for x in blocks),
        in_specs=[in_place] * len(blocks) + vmem_specs(len(after)),
        out_specs=(in_place,) * len(blocks),
        input_output_aliases={i: i for i in range(len(blocks))},
        name="hold",
    )(*(in_hbm(x) for x in blocks), *(in_vmem(x) for x in after))


def assemble(blocks, pieces, filled=()):
    ctx_count = lax.axis_size("ctx")
    core_count = lax.axis_size("sub")
    _, block_rows, head_dim = blocks[0].shape
    rows = ctx_count * core_count * block_rows
    arrays = 2
    count = len(blocks)
    total = len(pieces)

    def kernel(*refs):
        ctx = lax.axis_index("ctx")
        core = lax.axis_index("sub")
        in_refs = refs[:count]
        out_refs = refs[count + len(filled) :][:arrays]
        held, in_sems, out_sems = refs[count + len(filled) + arrays :]
        into, out_of = [], []
        for p, (block, entry, output, shift, flip) in enumerate(pieces):
            source = lax.rem(ctx + (ctx_count - shift), ctx_count) * core_count + lax.rem(
                core + (core_count - flip), core_count
            )
            place = pl.ds(pl.multiple_of(source * block_rows, block_rows), block_rows)
            into.append(
                pltpu.make_async_copy(in_refs[block].at[entry], held.at[p], in_sems.at[p])
            )
            out_of.append(
                pltpu.make_async_copy(held.at[p], out_refs[output].at[place], out_sems.at[p])
            )
        for copy in into:
            copy.start()
        for p in range(total):
            into[p].wait()
            out_of[p].start()
        for copy in out_of:
            copy.wait()

    return pl.pallas_call(
        kernel,
        out_shape=(pltpu.HBM((rows, head_dim), blocks[0].dtype),) * arrays,
        in_specs=[pl.BlockSpec(memory_space=pl.ANY)] * count
        + [pl.BlockSpec(memory_space=pltpu.HBM)] * len(filled),
        out_specs=(pl.BlockSpec(memory_space=pltpu.HBM),) * arrays,
        scratch_shapes=[
            pltpu.VMEM((total, block_rows, head_dim), blocks[0].dtype),
            pltpu.SemaphoreType.DMA((total,)),
            pltpu.SemaphoreType.DMA((total,)),
        ],
        input_output_aliases={count + w: w for w in range(len(filled))},
        compiler_params=pltpu.CompilerParams(vmem_limit_bytes=VMEM_BYTES),
        cost_estimate=pl.CostEstimate(
            flops=0, transcendentals=0, bytes_accessed=4 * total * block_rows * head_dim
        ),
        name="assemble",
    )(*blocks, *filled)


def pair_tokens(first, second, after):
    def kernel(first_ref, second_ref, after_ref, out_ref):
        out_ref[:, 0] = first_ref[...]
        out_ref[:, 1] = second_ref[...]

    whole = pl.BlockSpec(memory_space=pltpu.VMEM)
    return pl.pallas_call(
        kernel,
        out_shape=jax.ShapeDtypeStruct((first.shape[0], 2, first.shape[1]), first.dtype),
        in_specs=[whole, whole, pl.BlockSpec(memory_space=pl.ANY)],
        out_specs=whole,
        name="pair_tokens",
    )(first, second, in_hbm(after))


def in_parts(x, count):
    parts = []
    for _ in range(count):
        part = x.astype(jnp.bfloat16).astype(jnp.float32)
        parts.append(part)
        x = x - part
    return parts


def pack_products(products, wide, after):
    rows = wide.shape[0]
    widths = [x.shape[1] for x in products]
    total = sum(widths) + LANES
    columns = 2 * total - widths[0]

    def kernel(*refs):
        wide_ref, out_ref = refs[len(products)], refs[-1]
        squares = jnp.sum(wide_ref[...] * wide_ref[...], axis=1, keepdims=True)
        values = [ref[:rows] + ref[rows:] for ref in refs[: len(products)]]
        values.append(jnp.broadcast_to(squares, (rows, LANES)))
        low = 0
        for i, value in enumerate(values):
            first, second = in_parts(value, 2)
            high = low + value.shape[1]
            out_ref[:, low:high] = first.astype(jnp.bfloat16)
            if i:
                shift = total - widths[0]
                out_ref[:, low + shift : high + shift] = second.astype(jnp.bfloat16)
            low = high

    whole = pl.BlockSpec(memory_space=pltpu.VMEM)
    return pl.pallas_call(
        kernel,
        out_shape=pltpu.VMEM((rows, columns), jnp.bfloat16),
        in_specs=[whole] * (len(products) + 1 + len(after)),
        out_specs=whole,
        name="pack_products",
    )(*(in_vmem(x) for x in (*products, wide, *after)))


def to_rows(column_form):
    count = column_form.shape[0] // LANES
    return jnp.concatenate(
        [
            jnp.sum(
                jnp.where(diagonal(), column_form[i * LANES : (i + 1) * LANES], 0.0),
                axis=0,
                keepdims=True,
            )
            for i in range(count)
        ]
    )


def to_columns(row_form):
    return jnp.concatenate(
        [
            jnp.sum(
                jnp.where(diagonal(), row_form[i : i + 1], 0.0), axis=1, keepdims=True
            )
            for i in range(row_form.shape[0])
        ]
    )


def diagonal():
    row = lax.broadcasted_iota(jnp.int32, (LANES, LANES), 0)
    return row == lax.broadcasted_iota(jnp.int32, (LANES, LANES), 1)


def attend_shard(queries, keys, values, lengths, score_factor):
    requests, shard_length, heads, head_dim = keys.shape
    rows = queries.shape[1]
    own_rows = rows // 2
    per_head = rows // heads
    columns = shard_length * heads
    count = requests * own_rows
    extra = count // LANES
    flat_keys = keys.reshape(requests, columns, head_dim)
    flat_values = values.reshape(requests, columns, head_dim)
    core_count = lax.axis_size("sub")

    def kernel(lengths_ref, q_ref, k_ref, v_ref, kept_ref, sent_ref, max_scr, sum_scr):
        request = pl.program_id(0)
        core = lax.axis_index("sub")
        shard = lax.axis_index("ctx") * core_count + core
        scores = (
            lax.dot_general(
                q_ref[0], k_ref[0], (((1,), (1,)), ((), ())), preferred_element_type=jnp.float32
            )
            * score_factor
        )
        row = lax.broadcasted_iota(jnp.int32, (rows, columns), 0)
        column = lax.broadcasted_iota(jnp.int32, (rows, columns), 1)
        live_columns = (lengths_ref[request] - shard * shard_length) * heads
        live = (lax.rem(column, heads) == lax.div(row, per_head)) & (column < live_columns)
        scores = jnp.where(live, scores, masked_score)
        row_max = jnp.max(scores, axis=1, keepdims=True)
        weights = jnp.where(live, jnp.exp(scores - row_max), 0.0)
        sums = jnp.dot(
            weights.astype(jnp.bfloat16), v_ref[0], preferred_element_type=jnp.float32
        )
        row_max = jnp.broadcast_to(row_max, (rows, head_dim))
        row_sum = jnp.broadcast_to(jnp.sum(weights, axis=1, keepdims=True), (rows, head_dim))
        place = pl.ds(pl.multiple_of(request * own_rows, own_rows), own_rows)
        first = core == 0
        for f, out_ref in enumerate((kept_ref, sent_ref)):
            low = first if f == 0 else jnp.logical_not(first)
            pick = lambda x: jnp.where(low, x[:own_rows], x[own_rows:])
            out_ref[place, :] = pick(sums)
            max_scr[f, place, :] = pick(row_max)
            sum_scr[f, place, :] = pick(row_sum)

        @pl.when(request == requests - 1)
        def _():
            for f, out_ref in enumerate((kept_ref, sent_ref)):
                out_ref[count : count + extra, :] = to_rows(max_scr[f])
                out_ref[count + extra :, :] = to_rows(sum_scr[f])

    large = pl.BlockSpec((1, columns, head_dim), lambda r, *_: (r, 0, 0))
    packed = (count + 2 * extra, head_dim)
    return pl.pallas_call(
        kernel,
        out_shape=(pltpu.VMEM(packed, jnp.float32),) * 2,
        grid_spec=pltpu.PrefetchScalarGridSpec(
            num_scalar_prefetch=1,
            grid=(requests,),
            in_specs=[
                pl.BlockSpec((1, rows, head_dim), lambda r, *_: (r, 0, 0)),
                large,
                large,
            ],
            out_specs=tuple(vmem_specs(2)),
            scratch_shapes=[pltpu.VMEM((2, count, head_dim), jnp.float32)] * 2,
        ),
        compiler_params=pltpu.CompilerParams(vmem_limit_bytes=VMEM_BYTES),
        name="attend_shard",
    )(lengths, queries, in_hbm(flat_keys), in_hbm(flat_values))


def merge_packed(kept, other, after):
    extra = kept.shape[0] // (LANES + 2)
    count = extra * LANES
    tail = -(-5 * extra // 16) * 16

    def kernel(kept_ref, other_ref, *refs):
        out_ref = refs[-1]
        both = (kept_ref, other_ref)
        maxima = [ref[count : count + extra, :] for ref in both]
        largest = jnp.maximum(*maxima)
        scales = [jnp.exp(x - largest) for x in maxima]
        out_ref[:count, :] = sum(
            ref[:count, :] * to_columns(scale) for ref, scale in zip(both, scales)
        ).astype(jnp.bfloat16)
        totals = sum(ref[count + extra :, :] * scale for ref, scale in zip(both, scales))
        rest = in_parts(largest, 3) + in_parts(totals, 2)
        rest.append(jnp.zeros((tail - 5 * extra, LANES), jnp.float32))
        out_ref[count:, :] = jnp.concatenate(rest).astype(jnp.bfloat16)

    whole = pl.BlockSpec(memory_space=pltpu.VMEM)
    return pl.pallas_call(
        kernel,
        out_shape=pltpu.VMEM((count + tail, LANES), jnp.bfloat16),
        in_specs=[whole] * (2 + len(after)),
        out_specs=whole,
        name="merge_packed",
    )(*(in_vmem(x) for x in (kept, other, *after)))


def finish(packed, queries, fresh_keys, fresh_values, group_size, score_factor, after, made):
    shares = len(packed)
    count, head_dim = queries.shape
    extra = count // LANES

    def kernel(*refs):
        out_ref = refs[-1]
        packed_refs = refs[:shares]
        q_ref, key_ref, value_ref = refs[shares : shares + 3]
        wide = q_ref[...].astype(jnp.float32)
        row = lax.broadcasted_iota(jnp.int32, (count, 1), 0)
        second = lax.rem(lax.div(row, group_size), 2) == 1
        scores = [
            jnp.sum(wide * key_ref[u].astype(jnp.float32), axis=1, keepdims=True) * score_factor
            for u in range(2)
        ]
        scores[1] = jnp.where(second, scores[1], masked_score)
        tails = [ref[count:, :].astype(jnp.float32) for ref in packed_refs]
        part = lambda tail, i: tail[i * extra : (i + 1) * extra]
        maxima = [to_columns(part(t, 0) + part(t, 1) + part(t, 2)) for t in tails]
        totals = [to_columns(part(t, 3) + part(t, 4)) for t in tails]
        largest = functools.reduce(jnp.maximum, maxima + scores)
        scales = [jnp.exp(x - largest) for x in maxima]
        weights = [jnp.exp(x - largest) for x in scores]
        weights[1] = jnp.where(second, weights[1], 0.0)
        denominator = sum(t * scale for t, scale in zip(totals, scales)) + weights[0] + weights[1]
        numerator = sum(
            ref[:count, :].astype(jnp.float32) * scale for ref, scale in zip(packed_refs, scales)
        )
        for u in range(2):
            rounded = weights[u].astype(jnp.bfloat16).astype(jnp.float32)
            numerator = numerator + rounded * value_ref[u].astype(jnp.float32)
        out_ref[...] = (numerator / denominator).astype(jnp.bfloat16)

    whole = pl.BlockSpec(memory_space=pltpu.VMEM)
    return pl.pallas_call(
        kernel,
        out_shape=pltpu.VMEM((count, head_dim), jnp.bfloat16),
        in_specs=[whole] * (shares + 3 + len(after))
        + [pl.BlockSpec(memory_space=pltpu.HBM)] * len(made),
        out_specs=whole,
        name="finish",
    )(
        *(in_vmem(x) for x in (*packed, queries, fresh_keys, fresh_values, *after)),
        *(in_hbm(x) for x in made),
    )


def local(
    width,
    key_cache,
    value_cache,
    lengths,
    owner_order,
    first_tokens,
    second_tokens,
    norm_gain,
    w_query,
    w_key,
    w_value,
    w_out,
):
    ctx_count = lax.axis_size("ctx")
    sub_count = lax.axis_size("sub")
    requests, shard_length, heads, head_dim = key_cache.shape
    assert requests == ctx_count and sub_count == 2
    heads_decode = heads // sub_count
    sub_index = lax.axis_index("sub")
    take = functools.partial(jnp.take, mode="clip")

    both = (0, 1)
    received = {}

    def make(shift, flip, after=(), apart=False):
        return arrange((key_cache, value_cache), owner_order, shift, flip, after, apart)

    def send(block, which, shift, flip):
        pairs = [
            (
                c * sub_count + s,
                (c + shift) % ctx_count * sub_count + (s + flip) % sub_count,
            )
            for c in range(ctx_count)
            for s in range(sub_count)
        ]
        moved = lax.ppermute(block, ("ctx", "sub"), pairs)
        received[which, shift, flip] = moved
        return moved

    def from_all(values):
        return [values] + [
            lax.ppermute(values, "ctx", [(c, (c + shift) % ctx_count) for c in range(ctx_count)])
            for shift in range(1, ctx_count)
        ]

    middle = ctx_count // 2
    leading = make(1, 0, apart=True)
    paired = pair_tokens(first_tokens, second_tokens, leading[0])
    later = hold(leading[1:], (paired,))
    ahead = [send(block, (w,), 1, 0) for w, block in enumerate([leading[0], *later])]

    query_width = w_query.shape[1]
    key_width = w_key.shape[1]
    group_size = query_width // head_dim // heads_decode
    score_factor = head_dim ** (-0.5)
    rows_local = first_tokens.shape[0]
    tokens = lax.all_gather(
        paired, ("head", "sub"), axis=0, tiled=True
    )
    wide = tokens.astype(jnp.float32).reshape(2 * requests, -1)
    gained = wide * norm_gain.astype(jnp.float32)
    upper = lax.reduce_precision(gained, 8, 7)
    lower = gained - upper
    halves = jnp.concatenate([upper, lower]).astype(jnp.bfloat16)
    partial = pack_products(
        [
            jnp.dot(halves, weight, preferred_element_type=jnp.float32)
            for weight in (w_query, w_key, w_value)
        ],
        wide,
        (ahead[0],),
    )
    summed = functools.reduce(jnp.add, [x.astype(jnp.float32) for x in from_all(partial)])
    waiting = hold(make(1, 1, (partial,), apart=True), (summed, ahead[1]))
    behind = [send(waiting[w], (w,), 1, 1) for w in both]
    others = 2 * key_width + LANES
    tail = summed[:, query_width : query_width + others] + summed[:, query_width + others :]
    raw = jnp.concatenate([summed[:, :query_width], tail[:, :-LANES]], axis=1)
    raw = raw * lax.rsqrt(tail[:, -LANES:][:, :1] / width + eps_norm)
    raw = raw.reshape(requests, 2, -1, head_dim)
    positions = lengths.astype(jnp.float32)[:, None] + jnp.arange(2, dtype=jnp.float32)
    query_heads = query_width // head_dim
    key_heads = key_width // head_dim
    rotated = rotate(raw[:, :, : query_heads + key_heads], positions).astype(jnp.bfloat16)
    queries = rotated[:, :, :query_heads].reshape(requests, 2, heads_decode, group_size, head_dim)
    fresh_keys = rotated[:, :, query_heads:]
    fresh_values = raw[:, :, query_heads + key_heads :].astype(jnp.bfloat16)

    per_head = 2 * group_size
    own_queries = jnp.transpose(queries, (0, 2, 1, 3, 4)).reshape(
        requests, heads_decode * per_head, head_dim
    )
    all_queries = lax.all_gather(own_queries, "sub", axis=1, tiled=True)
    kept, sent = attend_shard(all_queries, key_cache, value_cache, lengths, score_factor)

    swap = [(i, (i + 1) % sub_count) for i in range(sub_count)]
    stats = merge_packed(kept, lax.ppermute(sent, "sub", swap), (behind[0],))
    packed = from_all(stats)

    rest = [
        (shift, flip)
        for shift in sorted(range(2, ctx_count), key=lambda d: -d)
        for flip in range(sub_count)
    ]
    blocks = hold([make(*rest[0], (partial,))], (*packed[1:], behind[1]))
    blocks = [*blocks, *(make(*key, tuple(packed[1:])) for key in rest[1:])]
    for block, key in zip(blocks, rest):
        send(block, both, *key)
    received[both, 0, 0] = make(0, 0, tuple(packed[1:]))
    send(make(0, 1, tuple(packed[1:])), both, 0, 1)

    def for_rows(fresh):
        spread = jnp.broadcast_to(
            fresh[:, :, :, None], (requests, 2, heads_decode, per_head, head_dim)
        )
        return jnp.swapaxes(spread, 0, 1).reshape(2, -1, head_dim)

    attended = finish(
        packed,
        own_queries.reshape(-1, head_dim),
        for_rows(fresh_keys),
        for_rows(fresh_values),
        group_size,
        score_factor,
        (received[both, *rest[0]],),
        blocks[1:],
    ).reshape(requests, heads_decode, 2, group_size, head_dim)

    attended = take(attended, owner_order, axis=0)
    attended = jnp.transpose(attended, (0, 2, 1, 3, 4)).reshape(2 * requests, query_width)
    branch = jnp.dot(attended, w_out, preferred_element_type=jnp.float32)
    branch = branch.reshape(requests, 2, -1)
    row_start = lax.axis_index(("head", "sub")) * rows_local
    parts = lax.all_gather(branch, ("head", "sub"), axis=0)
    parts = lax.dynamic_slice_in_dim(parts, row_start, rows_local, 1)
    own_ids = lax.dynamic_slice_in_dim(owner_order, row_start, rows_local)
    residual = take(tokens, own_ids, axis=0).astype(jnp.float32)
    result = (residual + jnp.sum(parts, axis=0)).astype(jnp.bfloat16)

    moved = ()
    early = [((w,), 1, flip) for flip in range(sub_count) for w in both]
    groups = [
        early + [(both, 0, 0), (both, 0, 1)],
        [(both, *key) for key in rest[:-1]],
        [(both, *rest[-1])],
    ]
    for keys in groups:
        pieces = [
            (block, entry, output, shift, flip)
            for block, (which, shift, flip) in enumerate(keys)
            for entry, output in enumerate(which)
        ]
        moved = assemble([received[key] for key in keys], pieces, moved)
    moved_keys, moved_values = (x.reshape(1, -1, heads_decode, head_dim) for x in moved)
    return (moved_keys, moved_values, result[:, 0], result[:, 1])


def solution(mesh):
    def whole(*arrays):
        return jax.shard_map(
            functools.partial(local, arrays[6].shape[0]),
            mesh=mesh,
            in_specs=(
                P("groups", ("ctx", "sub"), "head", None),
                P("groups", ("ctx", "sub"), "head", None),
                P("groups"),
                P("groups"),
                P(("groups", "head", "sub"), "ctx"),
                P(("groups", "head", "sub"), "ctx"),
                P("ctx"),
                P("ctx", ("head", "sub")),
                P("ctx", ("head", "sub")),
                P("ctx", ("head", "sub")),
                P(("head", "sub"), "ctx"),
            ),
            out_specs=(
                P(("groups", "ctx"), None, ("head", "sub"), None),
                P(("groups", "ctx"), None, ("head", "sub"), None),
                P(("groups", "head", "sub"), "ctx"),
                P(("groups", "head", "sub"), "ctx"),
            ),
            check_vma=False,
        )(*arrays)

    return whole
```

```python
import functools

import jax
import jax.numpy as jnp
from jax import lax
from jax.experimental import pallas as pl
from jax.experimental.pallas import tpu as pltpu
from jax.sharding import PartitionSpec as P

theta_base = 500000.0
eps_norm = 1e-05
masked_score = -1e30
LANES = 128
VMEM_BYTES = 48 * 1024 * 1024


def rotate(vectors, positions):
    half_dim = vectors.shape[-1] // 2
    exponents = jnp.arange(half_dim, dtype=jnp.float32) * (2.0 / vectors.shape[-1])
    frequency = theta_base ** (-exponents)
    angles = positions[..., None, None] * frequency
    cosines = jnp.cos(angles)
    sines = jnp.sin(angles)
    lower_part = vectors[..., :half_dim]
    upper_part = vectors[..., half_dim:]
    return jnp.concatenate(
        [lower_part * cosines - upper_part * sines, upper_part * cosines + lower_part * sines],
        axis=-1,
    )


def in_hbm(x):
    return pltpu.with_memory_space_constraint(x, pltpu.HBM)


def in_vmem(x):
    return pltpu.with_memory_space_constraint(x, pltpu.VMEM)


def vmem_specs(count):
    return [pl.BlockSpec(memory_space=pltpu.VMEM)] * count


def arrange(caches, owner_order, shift, flip, after, apart):
    _, shard_length, heads, head_dim = caches[0].shape
    ctx_count = lax.axis_size("ctx")
    core_count = lax.axis_size("sub")
    heads_decode = heads // core_count
    steps = 4
    places = shard_length // steps
    count = len(caches)
    pieces = [(w, i) for i in range(steps) for w in range(count)]
    outputs = count if apart else 1
    shape = (count // outputs, shard_length, heads_decode, head_dim)

    def kernel(order_ref, *refs):
        request = order_ref[lax.rem(lax.axis_index("ctx") + shift, ctx_count)]
        core = lax.rem(lax.axis_index("sub") + flip, core_count)
        in_refs = refs[:count]
        out_refs = refs[count + len(after) : -4]
        taken, made, in_sems, out_sems = refs[-4:]
        rows = lambda i: pl.ds(i * places, places)
        into = [
            pltpu.make_async_copy(
                in_refs[w].at[request, rows(i)], taken.at[w, rows(i)], in_sems.at[w, i]
            )
            for w, i in pieces
        ]
        out_of = [
            pltpu.make_async_copy(
                made.at[w, rows(i)],
                out_refs[w].at[0, rows(i)] if apart else out_refs[0].at[w, rows(i)],
                out_sems.at[w, i],
            )
            for w, i in pieces
        ]
        for copy in into:
            copy.start()
        for p, (w, i) in enumerate(pieces):
            into[p].wait()
            for own in range(core_count):

                @pl.when(core == own)
                def _():
                    low = own * heads_decode
                    made[w, rows(i)] = taken[w, rows(i), low : low + heads_decode, :]

            out_of[p].start()
        for copy in out_of:
            copy.wait()

    blocks = pl.pallas_call(
        kernel,
        out_shape=(pltpu.HBM(shape, caches[0].dtype),) * outputs,
        in_specs=[pl.BlockSpec(memory_space=pltpu.SMEM)]
        + [pl.BlockSpec(memory_space=pltpu.HBM)] * count
        + vmem_specs(len(after)),
        out_specs=(pl.BlockSpec(memory_space=pltpu.HBM),) * outputs,
        scratch_shapes=[
            pltpu.VMEM((count, shard_length, heads, head_dim), caches[0].dtype),
            pltpu.VMEM((count, shard_length, heads_decode, head_dim), caches[0].dtype),
            pltpu.SemaphoreType.DMA((count, steps)),
            pltpu.SemaphoreType.DMA((count, steps)),
        ],
        compiler_params=pltpu.CompilerParams(vmem_limit_bytes=VMEM_BYTES),
        name="arrange",
    )(owner_order, *(in_hbm(x) for x in caches), *(in_vmem(x) for x in after))
    blocks = [x.reshape(shape[0], shard_length * heads_decode, head_dim) for x in blocks]
    return blocks if apart else blocks[0]


def hold(blocks, after, stored=()):
    def kernel(*refs):
        pass

    in_place = pl.BlockSpec(memory_space=pltpu.HBM)
    return pl.pallas_call(
        kernel,
        out_shape=tuple(pltpu.HBM(x.shape, x.dtype) for x in blocks),
        in_specs=[in_place] * len(blocks)
        + vmem_specs(len(after))
        + [in_place] * len(stored),
        out_specs=(in_place,) * len(blocks),
        input_output_aliases={i: i for i in range(len(blocks))},
        name="hold",
    )(
        *(in_hbm(x) for x in blocks),
        *(in_vmem(x) for x in after),
        *(in_hbm(x) for x in stored),
    )


def assemble(blocks, pieces, filled, straight):
    ctx_count = lax.axis_size("ctx")
    core_count = lax.axis_size("sub")
    _, block_rows, head_dim = blocks[0].shape
    rows = ctx_count * core_count * block_rows
    arrays = 2
    count = len(blocks)
    total = len(pieces)

    def kernel(*refs):
        ctx = lax.axis_index("ctx")
        core = lax.axis_index("sub")
        in_refs = refs[:count]
        out_refs = refs[count + len(filled) :][:arrays]
        held, in_sems, out_sems = refs[count + len(filled) + arrays :]
        into, out_of = [], []
        for p, (block, entry, output, shift, flip) in enumerate(pieces):
            source = lax.rem(ctx + (ctx_count - shift), ctx_count) * core_count + lax.rem(
                core + (core_count - flip), core_count
            )
            place = pl.ds(pl.multiple_of(source * block_rows, block_rows), block_rows)
            taken = in_refs[block].at[entry]
            if not straight:
                into.append(pltpu.make_async_copy(taken, held.at[p], in_sems.at[p]))
                taken = held.at[p]
            out_of.append(
                pltpu.make_async_copy(taken, out_refs[output].at[place], out_sems.at[p])
            )
        for copy in into:
            copy.start()
        for p in range(total):
            if not straight:
                into[p].wait()
            out_of[p].start()
        for copy in out_of:
            copy.wait()

    return pl.pallas_call(
        kernel,
        out_shape=(pltpu.HBM((rows, head_dim), blocks[0].dtype),) * arrays,
        in_specs=(vmem_specs(count) if straight else [pl.BlockSpec(memory_space=pl.ANY)] * count)
        + [pl.BlockSpec(memory_space=pltpu.HBM)] * len(filled),
        out_specs=(pl.BlockSpec(memory_space=pltpu.HBM),) * arrays,
        scratch_shapes=[
            pltpu.VMEM((1 if straight else total, block_rows, head_dim), blocks[0].dtype),
            pltpu.SemaphoreType.DMA((total,)),
            pltpu.SemaphoreType.DMA((total,)),
        ],
        input_output_aliases={count + w: w for w in range(len(filled))},
        compiler_params=pltpu.CompilerParams(vmem_limit_bytes=VMEM_BYTES),
        cost_estimate=pl.CostEstimate(
            flops=0, transcendentals=0, bytes_accessed=4 * total * block_rows * head_dim
        ),
        name="assemble",
    )(*(in_vmem(x) if straight else x for x in blocks), *filled)


def pair_tokens(first, second, after):
    def kernel(first_ref, second_ref, after_ref, out_ref):
        out_ref[:, 0] = first_ref[...]
        out_ref[:, 1] = second_ref[...]

    whole = pl.BlockSpec(memory_space=pltpu.VMEM)
    return pl.pallas_call(
        kernel,
        out_shape=jax.ShapeDtypeStruct((first.shape[0], 2, first.shape[1]), first.dtype),
        in_specs=[whole, whole, pl.BlockSpec(memory_space=pl.ANY)],
        out_specs=whole,
        name="pair_tokens",
    )(first, second, in_hbm(after))


def in_parts(x, count):
    parts = []
    for _ in range(count):
        part = x.astype(jnp.bfloat16).astype(jnp.float32)
        parts.append(part)
        x = x - part
    return parts


def pack_products(products, wide, after):
    rows = wide.shape[0]
    widths = [x.shape[1] for x in products]
    total = sum(widths) + LANES
    columns = 2 * total - widths[0]

    def kernel(*refs):
        wide_ref, out_ref = refs[len(products)], refs[-1]
        squares = jnp.sum(wide_ref[...] * wide_ref[...], axis=1, keepdims=True)
        values = [ref[:rows] + ref[rows:] for ref in refs[: len(products)]]
        values.append(jnp.broadcast_to(squares, (rows, LANES)))
        low = 0
        for i, value in enumerate(values):
            first, second = in_parts(value, 2)
            high = low + value.shape[1]
            out_ref[:, low:high] = first.astype(jnp.bfloat16)
            if i:
                shift = total - widths[0]
                out_ref[:, low + shift : high + shift] = second.astype(jnp.bfloat16)
            low = high

    whole = pl.BlockSpec(memory_space=pltpu.VMEM)
    return pl.pallas_call(
        kernel,
        out_shape=pltpu.VMEM((rows, columns), jnp.bfloat16),
        in_specs=[whole] * (len(products) + 1 + len(after)),
        out_specs=whole,
        name="pack_products",
    )(*(in_vmem(x) for x in (*products, wide, *after)))


def to_rows(column_form):
    count = column_form.shape[0] // LANES
    return jnp.concatenate(
        [
            jnp.sum(
                jnp.where(diagonal(), column_form[i * LANES : (i + 1) * LANES], 0.0),
                axis=0,
                keepdims=True,
            )
            for i in range(count)
        ]
    )


def to_columns(row_form):
    return jnp.concatenate(
        [
            jnp.sum(
                jnp.where(diagonal(), row_form[i : i + 1], 0.0), axis=1, keepdims=True
            )
            for i in range(row_form.shape[0])
        ]
    )


def diagonal():
    row = lax.broadcasted_iota(jnp.int32, (LANES, LANES), 0)
    return row == lax.broadcasted_iota(jnp.int32, (LANES, LANES), 1)


def attend_shard(queries, keys, values, lengths, score_factor):
    requests, shard_length, heads, head_dim = keys.shape
    rows = queries.shape[1]
    own_rows = rows // 2
    per_head = rows // heads
    columns = shard_length * heads
    count = requests * own_rows
    extra = count // LANES
    flat_keys = keys.reshape(requests, columns, head_dim)
    flat_values = values.reshape(requests, columns, head_dim)
    core_count = lax.axis_size("sub")

    def kernel(lengths_ref, q_ref, k_ref, v_ref, kept_ref, sent_ref, max_scr, sum_scr):
        request = pl.program_id(0)
        core = lax.axis_index("sub")
        shard = lax.axis_index("ctx") * core_count + core
        scores = (
            lax.dot_general(
                q_ref[0], k_ref[0], (((1,), (1,)), ((), ())), preferred_element_type=jnp.float32
            )
            * score_factor
        )
        row = lax.broadcasted_iota(jnp.int32, (rows, columns), 0)
        column = lax.broadcasted_iota(jnp.int32, (rows, columns), 1)
        live_columns = (lengths_ref[request] - shard * shard_length) * heads
        live = (lax.rem(column, heads) == lax.div(row, per_head)) & (column < live_columns)
        scores = jnp.where(live, scores, masked_score)
        row_max = jnp.max(scores, axis=1, keepdims=True)
        weights = jnp.where(live, jnp.exp(scores - row_max), 0.0)
        sums = jnp.dot(
            weights.astype(jnp.bfloat16), v_ref[0], preferred_element_type=jnp.float32
        )
        row_max = jnp.broadcast_to(row_max, (rows, head_dim))
        row_sum = jnp.broadcast_to(jnp.sum(weights, axis=1, keepdims=True), (rows, head_dim))
        place = pl.ds(pl.multiple_of(request * own_rows, own_rows), own_rows)
        first = core == 0
        for f, out_ref in enumerate((kept_ref, sent_ref)):
            low = first if f == 0 else jnp.logical_not(first)
            pick = lambda x: jnp.where(low, x[:own_rows], x[own_rows:])
            out_ref[place, :] = pick(sums)
            max_scr[f, place, :] = pick(row_max)
            sum_scr[f, place, :] = pick(row_sum)

        @pl.when(request == requests - 1)
        def _():
            for f, out_ref in enumerate((kept_ref, sent_ref)):
                out_ref[count : count + extra, :] = to_rows(max_scr[f])
                out_ref[count + extra :, :] = to_rows(sum_scr[f])

    large = pl.BlockSpec((1, columns, head_dim), lambda r, *_: (r, 0, 0))
    packed = (count + 2 * extra, head_dim)
    return pl.pallas_call(
        kernel,
        out_shape=(pltpu.VMEM(packed, jnp.float32),) * 2,
        grid_spec=pltpu.PrefetchScalarGridSpec(
            num_scalar_prefetch=1,
            grid=(requests,),
            in_specs=[
                pl.BlockSpec((1, rows, head_dim), lambda r, *_: (r, 0, 0)),
                large,
                large,
            ],
            out_specs=tuple(vmem_specs(2)),
            scratch_shapes=[pltpu.VMEM((2, count, head_dim), jnp.float32)] * 2,
        ),
        compiler_params=pltpu.CompilerParams(vmem_limit_bytes=VMEM_BYTES),
        name="attend_shard",
    )(lengths, queries, in_hbm(flat_keys), in_hbm(flat_values))


def merge_packed(kept, other, after):
    extra = kept.shape[0] // (LANES + 2)
    count = extra * LANES
    tail = -(-5 * extra // 16) * 16

    def kernel(kept_ref, other_ref, *refs):
        out_ref = refs[-1]
        both = (kept_ref, other_ref)
        maxima = [ref[count : count + extra, :] for ref in both]
        largest = jnp.maximum(*maxima)
        scales = [jnp.exp(x - largest) for x in maxima]
        out_ref[:count, :] = sum(
            ref[:count, :] * to_columns(scale) for ref, scale in zip(both, scales)
        ).astype(jnp.bfloat16)
        totals = sum(ref[count + extra :, :] * scale for ref, scale in zip(both, scales))
        rest = in_parts(largest, 3) + in_parts(totals, 2)
        rest.append(jnp.zeros((tail - 5 * extra, LANES), jnp.float32))
        out_ref[count:, :] = jnp.concatenate(rest).astype(jnp.bfloat16)

    whole = pl.BlockSpec(memory_space=pltpu.VMEM)
    return pl.pallas_call(
        kernel,
        out_shape=pltpu.VMEM((count + tail, LANES), jnp.bfloat16),
        in_specs=[whole] * (2 + len(after)),
        out_specs=whole,
        name="merge_packed",
    )(*(in_vmem(x) for x in (kept, other, *after)))


def finish(packed, queries, fresh_keys, fresh_values, group_size, score_factor, after, made):
    shares = len(packed)
    count, head_dim = queries.shape
    extra = count // LANES

    def kernel(*refs):
        out_ref = refs[-1]
        packed_refs = refs[:shares]
        q_ref, key_ref, value_ref = refs[shares : shares + 3]
        wide = q_ref[...].astype(jnp.float32)
        row = lax.broadcasted_iota(jnp.int32, (count, 1), 0)
        second = lax.rem(lax.div(row, group_size), 2) == 1
        scores = [
            jnp.sum(wide * key_ref[u].astype(jnp.float32), axis=1, keepdims=True) * score_factor
            for u in range(2)
        ]
        scores[1] = jnp.where(second, scores[1], masked_score)
        tails = [ref[count:, :].astype(jnp.float32) for ref in packed_refs]
        part = lambda tail, i: tail[i * extra : (i + 1) * extra]
        maxima = [to_columns(part(t, 0) + part(t, 1) + part(t, 2)) for t in tails]
        totals = [to_columns(part(t, 3) + part(t, 4)) for t in tails]
        largest = functools.reduce(jnp.maximum, maxima + scores)
        scales = [jnp.exp(x - largest) for x in maxima]
        weights = [jnp.exp(x - largest) for x in scores]
        weights[1] = jnp.where(second, weights[1], 0.0)
        denominator = sum(t * scale for t, scale in zip(totals, scales)) + weights[0] + weights[1]
        numerator = sum(
            ref[:count, :].astype(jnp.float32) * scale for ref, scale in zip(packed_refs, scales)
        )
        for u in range(2):
            rounded = weights[u].astype(jnp.bfloat16).astype(jnp.float32)
            numerator = numerator + rounded * value_ref[u].astype(jnp.float32)
        out_ref[...] = (numerator / denominator).astype(jnp.bfloat16)

    whole = pl.BlockSpec(memory_space=pltpu.VMEM)
    return pl.pallas_call(
        kernel,
        out_shape=pltpu.VMEM((count, head_dim), jnp.bfloat16),
        in_specs=[whole] * (shares + 3 + len(after))
        + [pl.BlockSpec(memory_space=pltpu.HBM)] * len(made),
        out_specs=whole,
        name="finish",
    )(
        *(in_vmem(x) for x in (*packed, queries, fresh_keys, fresh_values, *after)),
        *(in_hbm(x) for x in made),
    )


def local(
    width,
    key_cache,
    value_cache,
    lengths,
    owner_order,
    first_tokens,
    second_tokens,
    norm_gain,
    w_query,
    w_key,
    w_value,
    w_out,
):
    ctx_count = lax.axis_size("ctx")
    sub_count = lax.axis_size("sub")
    requests, shard_length, heads, head_dim = key_cache.shape
    assert requests == ctx_count and sub_count == 2
    heads_decode = heads // sub_count
    sub_index = lax.axis_index("sub")
    take = functools.partial(jnp.take, mode="clip")

    both = (0, 1)
    received = {}

    def make(shift, flip, after=(), apart=False):
        return arrange((key_cache, value_cache), owner_order, shift, flip, after, apart)

    def send(block, which, shift, flip):
        pairs = [
            (
                c * sub_count + s,
                (c + shift) % ctx_count * sub_count + (s + flip) % sub_count,
            )
            for c in range(ctx_count)
            for s in range(sub_count)
        ]
        moved = lax.ppermute(block, ("ctx", "sub"), pairs)
        received[which, shift, flip] = moved
        return moved

    def from_all(values):
        return [values] + [
            lax.ppermute(values, "ctx", [(c, (c + shift) % ctx_count) for c in range(ctx_count)])
            for shift in range(1, ctx_count)
        ]

    middle = ctx_count // 2
    leading = make(1, 0, apart=True)
    paired = pair_tokens(first_tokens, second_tokens, leading[0])
    later = hold(leading[1:], (paired,))
    ahead = [send(block, (w,), 1, 0) for w, block in enumerate([leading[0], *later])]

    query_width = w_query.shape[1]
    key_width = w_key.shape[1]
    group_size = query_width // head_dim // heads_decode
    score_factor = head_dim ** (-0.5)
    rows_local = first_tokens.shape[0]
    tokens = lax.all_gather(
        paired, ("head", "sub"), axis=0, tiled=True
    )
    wide = tokens.astype(jnp.float32).reshape(2 * requests, -1)
    gained = wide * norm_gain.astype(jnp.float32)
    upper = lax.reduce_precision(gained, 8, 7)
    lower = gained - upper
    halves = jnp.concatenate([upper, lower]).astype(jnp.bfloat16)
    partial = pack_products(
        [
            jnp.dot(halves, weight, preferred_element_type=jnp.float32)
            for weight in (w_query, w_key, w_value)
        ],
        wide,
        (ahead[0],),
    )
    summed = functools.reduce(jnp.add, [x.astype(jnp.float32) for x in from_all(partial)])
    waiting = hold(make(1, 1, (partial,), apart=True), (summed, ahead[1]))
    behind = [send(waiting[w], (w,), 1, 1) for w in both]
    others = 2 * key_width + LANES
    tail = summed[:, query_width : query_width + others] + summed[:, query_width + others :]
    raw = jnp.concatenate([summed[:, :query_width], tail[:, :-LANES]], axis=1)
    raw = raw * lax.rsqrt(tail[:, -LANES:][:, :1] / width + eps_norm)
    raw = raw.reshape(requests, 2, -1, head_dim)
    positions = lengths.astype(jnp.float32)[:, None] + jnp.arange(2, dtype=jnp.float32)
    query_heads = query_width // head_dim
    key_heads = key_width // head_dim
    rotated = rotate(raw[:, :, : query_heads + key_heads], positions).astype(jnp.bfloat16)
    queries = rotated[:, :, :query_heads].reshape(requests, 2, heads_decode, group_size, head_dim)
    fresh_keys = rotated[:, :, query_heads:]
    fresh_values = raw[:, :, query_heads + key_heads :].astype(jnp.bfloat16)

    per_head = 2 * group_size
    own_queries = jnp.transpose(queries, (0, 2, 1, 3, 4)).reshape(
        requests, heads_decode * per_head, head_dim
    )
    all_queries = lax.all_gather(own_queries, "sub", axis=1, tiled=True)
    kept, sent = attend_shard(all_queries, key_cache, value_cache, lengths, score_factor)

    swap = [(i, (i + 1) % sub_count) for i in range(sub_count)]
    stats = merge_packed(kept, lax.ppermute(sent, "sub", swap), (behind[0],))
    packed = from_all(stats)

    rest = [
        (shift, flip)
        for shift in sorted(range(2, ctx_count), key=lambda d: -d)
        for flip in range(sub_count)
    ]
    blocks = hold([make(*rest[0], (partial,))], tuple(packed[1:]), (behind[1],))
    blocks = [*blocks, *(make(*key, tuple(packed[1:])) for key in rest[1:])]
    for block, key in zip(blocks, rest):
        send(block, both, *key)
    received[both, 0, 0] = make(0, 0, tuple(packed[1:]))
    send(make(0, 1, tuple(packed[1:])), both, 0, 1)

    def for_rows(fresh):
        spread = jnp.broadcast_to(
            fresh[:, :, :, None], (requests, 2, heads_decode, per_head, head_dim)
        )
        return jnp.swapaxes(spread, 0, 1).reshape(2, -1, head_dim)

    attended = finish(
        packed,
        own_queries.reshape(-1, head_dim),
        for_rows(fresh_keys),
        for_rows(fresh_values),
        group_size,
        score_factor,
        (received[both, *rest[0]],),
        blocks[1:],
    ).reshape(requests, heads_decode, 2, group_size, head_dim)

    attended = take(attended, owner_order, axis=0)
    attended = jnp.transpose(attended, (0, 2, 1, 3, 4)).reshape(2 * requests, query_width)
    branch = jnp.dot(attended, w_out, preferred_element_type=jnp.float32)
    branch = branch.reshape(requests, 2, -1)
    row_start = lax.axis_index(("head", "sub")) * rows_local
    parts = lax.all_gather(branch, ("head", "sub"), axis=0)
    parts = lax.dynamic_slice_in_dim(parts, row_start, rows_local, 1)
    own_ids = lax.dynamic_slice_in_dim(owner_order, row_start, rows_local)
    residual = take(tokens, own_ids, axis=0).astype(jnp.float32)
    result = (residual + jnp.sum(parts, axis=0)).astype(jnp.bfloat16)

    moved = ()
    early = [((w,), 1, flip) for flip in range(sub_count) for w in both]
    groups = [
        early + [(both, 0, 0), (both, 0, 1)],
        [(both, *key) for key in rest[:-1]],
        [(both, *rest[-1])],
    ]
    for keys in groups:
        pieces = [
            (block, entry, output, shift, flip)
            for block, (which, shift, flip) in enumerate(keys)
            for entry, output in enumerate(which)
        ]
        moved = assemble([received[key] for key in keys], pieces, moved, len(keys) == 1)
    moved_keys, moved_values = (x.reshape(1, -1, heads_decode, head_dim) for x in moved)
    return (moved_keys, moved_values, result[:, 0], result[:, 1])


def solution(mesh):
    def whole(*arrays):
        return jax.shard_map(
            functools.partial(local, arrays[6].shape[0]),
            mesh=mesh,
            in_specs=(
                P("groups", ("ctx", "sub"), "head", None),
                P("groups", ("ctx", "sub"), "head", None),
                P("groups"),
                P("groups"),
                P(("groups", "head", "sub"), "ctx"),
                P(("groups", "head", "sub"), "ctx"),
                P("ctx"),
                P("ctx", ("head", "sub")),
                P("ctx", ("head", "sub")),
                P("ctx", ("head", "sub")),
                P(("head", "sub"), "ctx"),
            ),
            out_specs=(
                P(("groups", "ctx"), None, ("head", "sub"), None),
                P(("groups", "ctx"), None, ("head", "sub"), None),
                P(("groups", "head", "sub"), "ctx"),
                P(("groups", "head", "sub"), "ctx"),
            ),
            check_vma=False,
        )(*arrays)

    return whole
```

```python
import functools

import jax
import jax.numpy as jnp
from jax import lax
from jax.experimental import pallas as pl
from jax.experimental.pallas import tpu as pltpu
from jax.sharding import PartitionSpec as P

theta_base = 500000.0
eps_norm = 1e-05
masked_score = -1e30
LANES = 128
VMEM_BYTES = 48 * 1024 * 1024


def rotate(vectors, positions):
    half_dim = vectors.shape[-1] // 2
    exponents = jnp.arange(half_dim, dtype=jnp.float32) * (2.0 / vectors.shape[-1])
    frequency = theta_base ** (-exponents)
    angles = positions[..., None, None] * frequency
    cosines = jnp.cos(angles)
    sines = jnp.sin(angles)
    lower_part = vectors[..., :half_dim]
    upper_part = vectors[..., half_dim:]
    return jnp.concatenate(
        [lower_part * cosines - upper_part * sines, upper_part * cosines + lower_part * sines],
        axis=-1,
    )


def in_hbm(x):
    return pltpu.with_memory_space_constraint(x, pltpu.HBM)


def in_vmem(x):
    return pltpu.with_memory_space_constraint(x, pltpu.VMEM)


def vmem_specs(count):
    return [pl.BlockSpec(memory_space=pltpu.VMEM)] * count


def arrange(caches, owner_order, shift, flip, after, apart):
    _, shard_length, heads, head_dim = caches[0].shape
    ctx_count = lax.axis_size("ctx")
    core_count = lax.axis_size("sub")
    heads_decode = heads // core_count
    steps = 4
    places = shard_length // steps
    count = len(caches)
    pieces = [(w, i) for i in range(steps) for w in range(count)]
    outputs = count if apart else 1
    shape = (count // outputs, shard_length, heads_decode, head_dim)

    def kernel(order_ref, *refs):
        request = order_ref[lax.rem(lax.axis_index("ctx") + shift, ctx_count)]
        core = lax.rem(lax.axis_index("sub") + flip, core_count)
        in_refs = refs[:count]
        out_refs = refs[count + len(after) : -4]
        taken, made, in_sems, out_sems = refs[-4:]
        rows = lambda i: pl.ds(i * places, places)
        into = [
            pltpu.make_async_copy(
                in_refs[w].at[request, rows(i)], taken.at[w, rows(i)], in_sems.at[w, i]
            )
            for w, i in pieces
        ]
        out_of = [
            pltpu.make_async_copy(
                made.at[w, rows(i)],
                out_refs[w].at[0, rows(i)] if apart else out_refs[0].at[w, rows(i)],
                out_sems.at[w, i],
            )
            for w, i in pieces
        ]
        for copy in into:
            copy.start()
        for p, (w, i) in enumerate(pieces):
            into[p].wait()
            for own in range(core_count):

                @pl.when(core == own)
                def _():
                    low = own * heads_decode
                    made[w, rows(i)] = taken[w, rows(i), low : low + heads_decode, :]

            out_of[p].start()
        for copy in out_of:
            copy.wait()

    blocks = pl.pallas_call(
        kernel,
        out_shape=(pltpu.HBM(shape, caches[0].dtype),) * outputs,
        in_specs=[pl.BlockSpec(memory_space=pltpu.SMEM)]
        + [pl.BlockSpec(memory_space=pltpu.HBM)] * count
        + vmem_specs(len(after)),
        out_specs=(pl.BlockSpec(memory_space=pltpu.HBM),) * outputs,
        scratch_shapes=[
            pltpu.VMEM((count, shard_length, heads, head_dim), caches[0].dtype),
            pltpu.VMEM((count, shard_length, heads_decode, head_dim), caches[0].dtype),
            pltpu.SemaphoreType.DMA((count, steps)),
            pltpu.SemaphoreType.DMA((count, steps)),
        ],
        compiler_params=pltpu.CompilerParams(vmem_limit_bytes=VMEM_BYTES),
        name="arrange",
    )(owner_order, *(in_hbm(x) for x in caches), *(in_vmem(x) for x in after))
    blocks = [x.reshape(shape[0], shard_length * heads_decode, head_dim) for x in blocks]
    return blocks if apart else blocks[0]


def hold(blocks, after, stored=()):
    def kernel(*refs):
        pass

    in_place = pl.BlockSpec(memory_space=pltpu.HBM)
    return pl.pallas_call(
        kernel,
        out_shape=tuple(pltpu.HBM(x.shape, x.dtype) for x in blocks),
        in_specs=[in_place] * len(blocks)
        + vmem_specs(len(after))
        + [in_place] * len(stored),
        out_specs=(in_place,) * len(blocks),
        input_output_aliases={i: i for i in range(len(blocks))},
        name="hold",
    )(
        *(in_hbm(x) for x in blocks),
        *(in_vmem(x) for x in after),
        *(in_hbm(x) for x in stored),
    )


def assemble(blocks, pieces, filled, straight):
    ctx_count = lax.axis_size("ctx")
    core_count = lax.axis_size("sub")
    _, block_rows, head_dim = blocks[0].shape
    rows = ctx_count * core_count * block_rows
    arrays = 2
    count = len(blocks)
    total = len(pieces)

    def kernel(*refs):
        ctx = lax.axis_index("ctx")
        core = lax.axis_index("sub")
        in_refs = refs[:count]
        out_refs = refs[count + len(filled) :][:arrays]
        held, in_sems, out_sems = refs[count + len(filled) + arrays :]
        into, out_of = [], []
        for p, (block, entry, output, shift, flip) in enumerate(pieces):
            source = lax.rem(ctx + (ctx_count - shift), ctx_count) * core_count + lax.rem(
                core + (core_count - flip), core_count
            )
            place = pl.ds(pl.multiple_of(source * block_rows, block_rows), block_rows)
            taken = in_refs[block].at[entry]
            if not straight:
                into.append(pltpu.make_async_copy(taken, held.at[p], in_sems.at[p]))
                taken = held.at[p]
            out_of.append(
                pltpu.make_async_copy(taken, out_refs[output].at[place], out_sems.at[p])
            )
        for copy in into:
            copy.start()
        for p in range(total):
            if not straight:
                into[p].wait()
            out_of[p].start()
        for copy in out_of:
            copy.wait()

    return pl.pallas_call(
        kernel,
        out_shape=(pltpu.HBM((rows, head_dim), blocks[0].dtype),) * arrays,
        in_specs=(vmem_specs(count) if straight else [pl.BlockSpec(memory_space=pl.ANY)] * count)
        + [pl.BlockSpec(memory_space=pltpu.HBM)] * len(filled),
        out_specs=(pl.BlockSpec(memory_space=pltpu.HBM),) * arrays,
        scratch_shapes=[
            pltpu.VMEM((1 if straight else total, block_rows, head_dim), blocks[0].dtype),
            pltpu.SemaphoreType.DMA((total,)),
            pltpu.SemaphoreType.DMA((total,)),
        ],
        input_output_aliases={count + w: w for w in range(len(filled))},
        compiler_params=pltpu.CompilerParams(vmem_limit_bytes=VMEM_BYTES),
        cost_estimate=pl.CostEstimate(
            flops=0, transcendentals=0, bytes_accessed=4 * total * block_rows * head_dim
        ),
        name="assemble",
    )(*(in_vmem(x) if straight else x for x in blocks), *filled)


def pair_tokens(first, second, after):
    def kernel(first_ref, second_ref, after_ref, out_ref):
        out_ref[:, 0] = first_ref[...]
        out_ref[:, 1] = second_ref[...]

    whole = pl.BlockSpec(memory_space=pltpu.VMEM)
    return pl.pallas_call(
        kernel,
        out_shape=jax.ShapeDtypeStruct((first.shape[0], 2, first.shape[1]), first.dtype),
        in_specs=[whole, whole, pl.BlockSpec(memory_space=pl.ANY)],
        out_specs=whole,
        name="pair_tokens",
    )(first, second, in_hbm(after))


def in_parts(x, count):
    parts = []
    for _ in range(count):
        part = x.astype(jnp.bfloat16).astype(jnp.float32)
        parts.append(part)
        x = x - part
    return parts


def pack_products(products, wide, after):
    rows = wide.shape[0]
    widths = [x.shape[1] for x in products]
    total = sum(widths) + LANES
    columns = 2 * total - widths[0]

    def kernel(*refs):
        wide_ref, out_ref = refs[len(products)], refs[-1]
        squares = jnp.sum(wide_ref[...] * wide_ref[...], axis=1, keepdims=True)
        values = [ref[:rows] + ref[rows:] for ref in refs[: len(products)]]
        values.append(jnp.broadcast_to(squares, (rows, LANES)))
        low = 0
        for i, value in enumerate(values):
            first, second = in_parts(value, 2)
            high = low + value.shape[1]
            out_ref[:, low:high] = first.astype(jnp.bfloat16)
            if i:
                shift = total - widths[0]
                out_ref[:, low + shift : high + shift] = second.astype(jnp.bfloat16)
            low = high

    whole = pl.BlockSpec(memory_space=pltpu.VMEM)
    return pl.pallas_call(
        kernel,
        out_shape=pltpu.VMEM((rows, columns), jnp.bfloat16),
        in_specs=[whole] * (len(products) + 1 + len(after)),
        out_specs=whole,
        name="pack_products",
    )(*(in_vmem(x) for x in (*products, wide, *after)))


def to_rows(column_form):
    count = column_form.shape[0] // LANES
    return jnp.concatenate(
        [
            jnp.sum(
                jnp.where(diagonal(), column_form[i * LANES : (i + 1) * LANES], 0.0),
                axis=0,
                keepdims=True,
            )
            for i in range(count)
        ]
    )


def to_columns(row_form):
    return jnp.concatenate(
        [
            jnp.sum(
                jnp.where(diagonal(), row_form[i : i + 1], 0.0), axis=1, keepdims=True
            )
            for i in range(row_form.shape[0])
        ]
    )


def diagonal():
    row = lax.broadcasted_iota(jnp.int32, (LANES, LANES), 0)
    return row == lax.broadcasted_iota(jnp.int32, (LANES, LANES), 1)


def attend_shard(queries, keys, values, lengths, score_factor):
    requests, shard_length, heads, head_dim = keys.shape
    rows = queries.shape[1]
    own_rows = rows // 2
    per_head = rows // heads
    columns = shard_length * heads
    count = requests * own_rows
    extra = count // LANES
    flat_keys = keys.reshape(requests, columns, head_dim)
    flat_values = values.reshape(requests, columns, head_dim)
    core_count = lax.axis_size("sub")

    def kernel(lengths_ref, q_ref, k_ref, v_ref, kept_ref, sent_ref, max_scr, sum_scr):
        request = pl.program_id(0)
        core = lax.axis_index("sub")
        shard = lax.axis_index("ctx") * core_count + core
        scores = (
            lax.dot_general(
                q_ref[0], k_ref[0], (((1,), (1,)), ((), ())), preferred_element_type=jnp.float32
            )
            * score_factor
        )
        row = lax.broadcasted_iota(jnp.int32, (rows, columns), 0)
        column = lax.broadcasted_iota(jnp.int32, (rows, columns), 1)
        live_columns = (lengths_ref[request] - shard * shard_length) * heads
        live = (lax.rem(column, heads) == lax.div(row, per_head)) & (column < live_columns)
        scores = jnp.where(live, scores, masked_score)
        row_max = jnp.max(scores, axis=1, keepdims=True)
        weights = jnp.where(live, jnp.exp(scores - row_max), 0.0)
        sums = jnp.dot(
            weights.astype(jnp.bfloat16), v_ref[0], preferred_element_type=jnp.float32
        )
        row_max = jnp.broadcast_to(row_max, (rows, head_dim))
        row_sum = jnp.broadcast_to(jnp.sum(weights, axis=1, keepdims=True), (rows, head_dim))
        place = pl.ds(pl.multiple_of(request * own_rows, own_rows), own_rows)
        first = core == 0
        for f, out_ref in enumerate((kept_ref, sent_ref)):
            low = first if f == 0 else jnp.logical_not(first)
            pick = lambda x: jnp.where(low, x[:own_rows], x[own_rows:])
            out_ref[place, :] = pick(sums)
            max_scr[f, place, :] = pick(row_max)
            sum_scr[f, place, :] = pick(row_sum)

        @pl.when(request == requests - 1)
        def _():
            for f, out_ref in enumerate((kept_ref, sent_ref)):
                out_ref[count : count + extra, :] = to_rows(max_scr[f])
                out_ref[count + extra :, :] = to_rows(sum_scr[f])

    large = pl.BlockSpec((1, columns, head_dim), lambda r, *_: (r, 0, 0))
    packed = (count + 2 * extra, head_dim)
    return pl.pallas_call(
        kernel,
        out_shape=(pltpu.VMEM(packed, jnp.float32),) * 2,
        grid_spec=pltpu.PrefetchScalarGridSpec(
            num_scalar_prefetch=1,
            grid=(requests,),
            in_specs=[
                pl.BlockSpec((1, rows, head_dim), lambda r, *_: (r, 0, 0)),
                large,
                large,
            ],
            out_specs=tuple(vmem_specs(2)),
            scratch_shapes=[pltpu.VMEM((2, count, head_dim), jnp.float32)] * 2,
        ),
        compiler_params=pltpu.CompilerParams(vmem_limit_bytes=VMEM_BYTES),
        name="attend_shard",
    )(lengths, queries, in_hbm(flat_keys), in_hbm(flat_values))


def merge_packed(kept, other, after):
    extra = kept.shape[0] // (LANES + 2)
    count = extra * LANES
    tail = -(-5 * extra // 16) * 16

    def kernel(kept_ref, other_ref, *refs):
        out_ref = refs[-1]
        both = (kept_ref, other_ref)
        maxima = [ref[count : count + extra, :] for ref in both]
        largest = jnp.maximum(*maxima)
        scales = [jnp.exp(x - largest) for x in maxima]
        out_ref[:count, :] = sum(
            ref[:count, :] * to_columns(scale) for ref, scale in zip(both, scales)
        ).astype(jnp.bfloat16)
        totals = sum(ref[count + extra :, :] * scale for ref, scale in zip(both, scales))
        rest = in_parts(largest, 3) + in_parts(totals, 2)
        rest.append(jnp.zeros((tail - 5 * extra, LANES), jnp.float32))
        out_ref[count:, :] = jnp.concatenate(rest).astype(jnp.bfloat16)

    whole = pl.BlockSpec(memory_space=pltpu.VMEM)
    return pl.pallas_call(
        kernel,
        out_shape=pltpu.VMEM((count + tail, LANES), jnp.bfloat16),
        in_specs=[whole] * (2 + len(after)),
        out_specs=whole,
        name="merge_packed",
    )(*(in_vmem(x) for x in (kept, other, *after)))


def finish(packed, queries, fresh_keys, fresh_values, group_size, score_factor, after, made):
    shares = len(packed)
    count, head_dim = queries.shape
    extra = count // LANES

    def kernel(*refs):
        out_ref = refs[-1]
        packed_refs = refs[:shares]
        q_ref, key_ref, value_ref = refs[shares : shares + 3]
        wide = q_ref[...].astype(jnp.float32)
        row = lax.broadcasted_iota(jnp.int32, (count, 1), 0)
        second = lax.rem(lax.div(row, group_size), 2) == 1
        scores = [
            jnp.sum(wide * key_ref[u].astype(jnp.float32), axis=1, keepdims=True) * score_factor
            for u in range(2)
        ]
        scores[1] = jnp.where(second, scores[1], masked_score)
        tails = [ref[count:, :].astype(jnp.float32) for ref in packed_refs]
        part = lambda tail, i: tail[i * extra : (i + 1) * extra]
        maxima = [to_columns(part(t, 0) + part(t, 1) + part(t, 2)) for t in tails]
        totals = [to_columns(part(t, 3) + part(t, 4)) for t in tails]
        largest = functools.reduce(jnp.maximum, maxima + scores)
        scales = [jnp.exp(x - largest) for x in maxima]
        weights = [jnp.exp(x - largest) for x in scores]
        weights[1] = jnp.where(second, weights[1], 0.0)
        denominator = sum(t * scale for t, scale in zip(totals, scales)) + weights[0] + weights[1]
        numerator = sum(
            ref[:count, :].astype(jnp.float32) * scale for ref, scale in zip(packed_refs, scales)
        )
        for u in range(2):
            rounded = weights[u].astype(jnp.bfloat16).astype(jnp.float32)
            numerator = numerator + rounded * value_ref[u].astype(jnp.float32)
        out_ref[...] = (numerator / denominator).astype(jnp.bfloat16)

    whole = pl.BlockSpec(memory_space=pltpu.VMEM)
    return pl.pallas_call(
        kernel,
        out_shape=pltpu.VMEM((count, head_dim), jnp.bfloat16),
        in_specs=[whole] * (shares + 3 + len(after))
        + [pl.BlockSpec(memory_space=pltpu.HBM)] * len(made),
        out_specs=whole,
        name="finish",
    )(
        *(in_vmem(x) for x in (*packed, queries, fresh_keys, fresh_values, *after)),
        *(in_hbm(x) for x in made),
    )


def local(
    width,
    key_cache,
    value_cache,
    lengths,
    owner_order,
    first_tokens,
    second_tokens,
    norm_gain,
    w_query,
    w_key,
    w_value,
    w_out,
):
    ctx_count = lax.axis_size("ctx")
    sub_count = lax.axis_size("sub")
    requests, shard_length, heads, head_dim = key_cache.shape
    assert requests == ctx_count and sub_count == 2
    heads_decode = heads // sub_count
    sub_index = lax.axis_index("sub")
    take = functools.partial(jnp.take, mode="clip")

    both = (0, 1)
    received = {}

    def make(shift, flip, after=(), apart=False):
        return arrange((key_cache, value_cache), owner_order, shift, flip, after, apart)

    def send(block, which, shift, flip):
        pairs = [
            (
                c * sub_count + s,
                (c + shift) % ctx_count * sub_count + (s + flip) % sub_count,
            )
            for c in range(ctx_count)
            for s in range(sub_count)
        ]
        moved = lax.ppermute(block, ("ctx", "sub"), pairs)
        received[which, shift, flip] = moved
        return moved

    def from_all(values):
        return [values] + [
            lax.ppermute(values, "ctx", [(c, (c + shift) % ctx_count) for c in range(ctx_count)])
            for shift in range(1, ctx_count)
        ]

    middle = ctx_count // 2
    leading = make(1, 0, apart=True)
    paired = pair_tokens(first_tokens, second_tokens, leading[0])
    last = ctx_count - 1
    later = make(last, 0, (paired,), apart=True)
    ahead = [send(leading[0], (0,), 1, 0), send(later[0], (0,), last, 0)]

    query_width = w_query.shape[1]
    key_width = w_key.shape[1]
    group_size = query_width // head_dim // heads_decode
    score_factor = head_dim ** (-0.5)
    rows_local = first_tokens.shape[0]
    tokens = lax.all_gather(
        paired, ("head", "sub"), axis=0, tiled=True
    )
    wide = tokens.astype(jnp.float32).reshape(2 * requests, -1)
    gained = wide * norm_gain.astype(jnp.float32)
    upper = lax.reduce_precision(gained, 8, 7)
    lower = gained - upper
    halves = jnp.concatenate([upper, lower]).astype(jnp.bfloat16)
    partial = pack_products(
        [
            jnp.dot(halves, weight, preferred_element_type=jnp.float32)
            for weight in (w_query, w_key, w_value)
        ],
        wide,
        (ahead[0],),
    )
    summed = functools.reduce(jnp.add, [x.astype(jnp.float32) for x in from_all(partial)])
    waiting = hold([leading[1], later[1]], (summed, ahead[1]))
    behind = [send(block, (1,), shift, 0) for block, shift in zip(waiting, (1, last))]
    others = 2 * key_width + LANES
    tail = summed[:, query_width : query_width + others] + summed[:, query_width + others :]
    raw = jnp.concatenate([summed[:, :query_width], tail[:, :-LANES]], axis=1)
    raw = raw * lax.rsqrt(tail[:, -LANES:][:, :1] / width + eps_norm)
    raw = raw.reshape(requests, 2, -1, head_dim)
    positions = lengths.astype(jnp.float32)[:, None] + jnp.arange(2, dtype=jnp.float32)
    query_heads = query_width // head_dim
    key_heads = key_width // head_dim
    rotated = rotate(raw[:, :, : query_heads + key_heads], positions).astype(jnp.bfloat16)
    queries = rotated[:, :, :query_heads].reshape(requests, 2, heads_decode, group_size, head_dim)
    fresh_keys = rotated[:, :, query_heads:]
    fresh_values = raw[:, :, query_heads + key_heads :].astype(jnp.bfloat16)

    per_head = 2 * group_size
    own_queries = jnp.transpose(queries, (0, 2, 1, 3, 4)).reshape(
        requests, heads_decode * per_head, head_dim
    )
    all_queries = lax.all_gather(own_queries, "sub", axis=1, tiled=True)
    kept, sent = attend_shard(all_queries, key_cache, value_cache, lengths, score_factor)

    swap = [(i, (i + 1) % sub_count) for i in range(sub_count)]
    stats = merge_packed(kept, lax.ppermute(sent, "sub", swap), (behind[0],))
    packed = from_all(stats)

    rest = [
        (shift, flip)
        for shift in sorted(range(1, ctx_count), key=lambda d: -abs(d - middle))
        for flip in range(sub_count)
        if flip or shift not in (1, last)
    ]
    blocks = hold([make(*rest[0], (partial,))], tuple(packed[1:]), (behind[1],))
    blocks = [*blocks, *(make(*key, tuple(packed[1:])) for key in rest[1:])]
    for block, key in zip(blocks, rest):
        send(block, both, *key)
    received[both, 0, 0] = make(0, 0, tuple(packed[1:]))
    send(make(0, 1, tuple(packed[1:])), both, 0, 1)

    def for_rows(fresh):
        spread = jnp.broadcast_to(
            fresh[:, :, :, None], (requests, 2, heads_decode, per_head, head_dim)
        )
        return jnp.swapaxes(spread, 0, 1).reshape(2, -1, head_dim)

    attended = finish(
        packed,
        own_queries.reshape(-1, head_dim),
        for_rows(fresh_keys),
        for_rows(fresh_values),
        group_size,
        score_factor,
        (received[both, *rest[0]],),
        blocks[1:],
    ).reshape(requests, heads_decode, 2, group_size, head_dim)

    attended = take(attended, owner_order, axis=0)
    attended = jnp.transpose(attended, (0, 2, 1, 3, 4)).reshape(2 * requests, query_width)
    branch = jnp.dot(attended, w_out, preferred_element_type=jnp.float32)
    branch = branch.reshape(requests, 2, -1)
    row_start = lax.axis_index(("head", "sub")) * rows_local
    parts = lax.all_gather(branch, ("head", "sub"), axis=0)
    parts = lax.dynamic_slice_in_dim(parts, row_start, rows_local, 1)
    own_ids = lax.dynamic_slice_in_dim(owner_order, row_start, rows_local)
    residual = take(tokens, own_ids, axis=0).astype(jnp.float32)
    result = (residual + jnp.sum(parts, axis=0)).astype(jnp.bfloat16)

    moved = ()
    early = [((w,), shift, 0) for shift in (1, last) for w in both]
    groups = [
        early + [(both, 0, 0), (both, 0, 1)],
        [(both, *key) for key in rest[:-1]],
        [(both, *rest[-1])],
    ]
    for keys in groups:
        pieces = [
            (block, entry, output, shift, flip)
            for block, (which, shift, flip) in enumerate(keys)
            for entry, output in enumerate(which)
        ]
        moved = assemble([received[key] for key in keys], pieces, moved, len(keys) == 1)
    moved_keys, moved_values = (x.reshape(1, -1, heads_decode, head_dim) for x in moved)
    return (moved_keys, moved_values, result[:, 0], result[:, 1])


def solution(mesh):
    def whole(*arrays):
        return jax.shard_map(
            functools.partial(local, arrays[6].shape[0]),
            mesh=mesh,
            in_specs=(
                P("groups", ("ctx", "sub"), "head", None),
                P("groups", ("ctx", "sub"), "head", None),
                P("groups"),
                P("groups"),
                P(("groups", "head", "sub"), "ctx"),
                P(("groups", "head", "sub"), "ctx"),
                P("ctx"),
                P("ctx", ("head", "sub")),
                P("ctx", ("head", "sub")),
                P("ctx", ("head", "sub")),
                P(("head", "sub"), "ctx"),
            ),
            out_specs=(
                P(("groups", "ctx"), None, ("head", "sub"), None),
                P(("groups", "ctx"), None, ("head", "sub"), None),
                P(("groups", "head", "sub"), "ctx"),
                P(("groups", "head", "sub"), "ctx"),
            ),
            check_vma=False,
        )(*arrays)

    return whole
```
